32 devices in a mesh: grp: 8 (over z, x), loc: 4 (over y, core).
Axes of the slice: x: 2, y: 2, z: 4, core: 2. Of those that a mesh axis runs over, the one named last changes fastest.
Arguments:
- carried: float32 [2, 2048, 1000], P(None, ('grp', 'loc')), may hold values from -0.9 to 0.9
- session_plan: int32 [2048], P(('grp', 'loc')), may hold values from 0 to 511, as said below
- item_ids: int32 [4, 2048], P(None, ('grp', 'loc')), may hold values from 0 to 4703, as said below
- target_ids: int32 [4, 2048], P(None, ('grp', 'loc')), may hold values from 0 to 4703, as said below
- reset_mask: int32 [4, 2048], P(None, ('grp', 'loc')), may hold values 0 or 1
- valid_counts: int32 [2048], P(('grp', 'loc')), may hold values from 1 to 4
- negative_ids: int32 [2048], replicated, may hold values from 0 to 4703, as said below
- input_table: bfloat16 [4704, 3000], P('grp'), may hold values from -4 to 4
- output_table: bfloat16 [4704, 1000], P('grp'), may hold values from -0.69921875 to 0.69921875
- output_bias: bfloat16 [4704], P('grp'), may hold values from -3 to 3
- hidden_one: bfloat16 [1000, 3000], P(None, 'loc'), may hold values from -0.1875 to 0.1875
- input_two: bfloat16 [1000, 3000], P(None, 'loc'), may hold values from -0.1875 to 0.1875
- hidden_two: bfloat16 [1000, 3000], P(None, 'loc'), may hold values from -0.1875 to 0.1875
- gate_biases: bfloat16 [2, 3000], P(None, 'loc'), may hold values from -2 to 2
Outputs:
- grad_input_table: float32 [4704, 3000], P(('grp', 'loc'))
- grad_output_table: float32 [4704, 1000], P(('grp', 'loc'))
- grad_output_bias: float32 [4704], P(('grp', 'loc'))
- grad_hidden_one: float32 [1000, 3000], P(None, 'loc')
- grad_input_two: float32 [1000, 3000], P(None, 'loc')
- grad_hidden_two: float32 [1000, 3000], P(None, 'loc')
- grad_gate_biases: float32 [2, 3000], P(None, 'loc')
- grad_carried: float32 [2, 2048, 1000], P(None, ('grp', 'loc'))
The draws below stay inside these ranges and needn't reach their ends.
Inputs may be any that keep to these rules, and one draw needn't show every extreme that they name: `item_ids`: within each device's block of 4 x 64 events, the items of group g's range g * 588 to (g + 1) * 588 - 1 are named at most 48 times, and exactly 48 times for some group. `target_ids`: within each device's block of 4 x 64 events, the items of one group's range are named at most 48 times, and exactly 48 times for some group. `session_plan`: each value is e * 64 + j for a group e and a new slot j; over the devices of one loc index every pair (e, j) is named exactly once; at most 32 of one device's slots name the same group e, and exactly 32 for some group. `negative_ids`: entry j lies in the range of group j // 256, from (j // 256) * 588 to (j // 256 + 1) * 588 - 1.
All inputs are finite; a program needn't handle non-finite values. No bound on the sum of `reset_mask` on one device may be relied on, other than what follows from the above.
Results may differ from the reference program's by a relative error of at most 0.0075.
Values may be sent and summed in bfloat16 or wider, within the bound.
No kernel may reach another device: no remote copies, remote signals or barrier semaphores. Data moves between devices by JAX's collectives and lax.ppermute only.
A program may use at most 256 MiB of HBM per device.

```python
import jax
import jax.numpy as jnp
from jax import lax

H = 1000
ITEMS_GRP = 588
NEG = 2048
B_DEV = 64
STEPS = 4
G3 = 3000
OWNERS = 8
ITEMS = 4704
SESS = 2048
EVT_DEV = 256
CAP = 48
NPG = 256
N_LOC = 4


def owned_items(key):
    device_count = SESS // B_DEV

    def one_device(device_key):
        key_owner, key_order, key_offset = jax.random.split(device_key, 3)
        heavy = jax.random.randint(key_owner, (), 0, OWNERS)
        position = jnp.arange(EVT_DEV, dtype=jnp.int32)
        others = (heavy + 1 + (position - CAP) % (OWNERS - 1)) % OWNERS
        owner_of = jnp.where(position < CAP, heavy, others)
        owner_of = jax.random.permutation(key_order, owner_of)
        offset = jax.random.randint(key_offset, (EVT_DEV,), 0, ITEMS_GRP)
        return (owner_of * ITEMS_GRP + offset).reshape(STEPS, B_DEV)
    blocks = jax.vmap(one_device)(jax.random.split(key, device_count))
    return jnp.transpose(blocks, (1, 0, 2)).reshape(STEPS, SESS).astype(jnp.int32)


def draw_item_ids(key, part):
    key = jax.random.fold_in(key, 11)
    return owned_items(key)


def draw_target_ids(key, part):
    key = jax.random.fold_in(key, 23)
    return owned_items(key)


def draw_session_plan(key, part):
    key = jax.random.fold_in(key, 37)
    column_count = SESS // B_DEV // OWNERS
    bound = 4 * B_DEV // OWNERS
    half = B_DEV // 2
    heavy_ranks = OWNERS // 8
    order = jnp.arange(B_DEV, dtype=jnp.int32)
    rank_of = jnp.where(order < half, order // bound, heavy_ranks + (order - half) * (OWNERS - heavy_ranks) // half)
    same_rank = (rank_of[:, None] == rank_of[None, :]) & (order[None, :] < order[:, None])
    within = jnp.sum(same_rank.astype(jnp.int32), axis=1)
    count_of_rank = jnp.sum((rank_of[None, :] == jnp.arange(OWNERS, dtype=jnp.int32)[:, None]).astype(jnp.int32), axis=1)
    groups = jnp.arange(OWNERS, dtype=jnp.int32)

    def column(column_key):
        key_offset, key_perm = jax.random.split(column_key)
        offsets = jax.random.permutation(key_offset, groups)
        count_of_offset = jnp.zeros((OWNERS,), jnp.int32).at[offsets].set(count_of_rank)
        pair_counts = count_of_offset[(groups[None, :] - groups[:, None]) % OWNERS]
        prefix = jnp.cumsum(pair_counts, axis=0) - pair_counts
        dest = (groups[:, None] + offsets[rank_of][None, :]) % OWNERS
        slot = prefix[groups[:, None], dest] + within[None, :]
        value = dest * B_DEV + slot
        perms = jax.vmap(lambda one_key: jax.random.permutation(one_key, order))(jax.random.split(key_perm, OWNERS))
        return jnp.zeros((OWNERS, B_DEV), jnp.int32).at[groups[:, None], perms].set(value)
    columns = jax.vmap(column)(jax.random.split(key, column_count))
    return jnp.transpose(columns, (1, 0, 2)).reshape(SESS).astype(jnp.int32)


def draw_negative_ids(key, part):
    key = jax.random.fold_in(key, 41)
    group_of = jnp.arange(NEG, dtype=jnp.int32) // NPG
    offset = jax.random.randint(key, (NEG,), 0, ITEMS_GRP)
    return (group_of * ITEMS_GRP + offset).astype(jnp.int32)


def with_ends(entries, rng, low, high):
    spot = [jax.random.randint(jax.random.fold_in(rng, axis), (), 0, length) for axis, length in enumerate(entries.shape)]
    widest = entries.shape.index(max(entries.shape))
    beside = spot[:widest] + [(spot[widest] + 1) % entries.shape[widest]] + spot[widest + 1:]
    return entries.at[tuple(spot)].set(low).at[tuple(beside)].set(high)


def levels(key, shape, shards, low, largest):
    factor_of = 1.0
    for dim, parts in shards:
        draws = jax.random.uniform(jax.random.fold_in(jax.random.fold_in(key, 6), dim), (parts,), jnp.float32, low / len(shards), largest / len(shards))
        factor_of = factor_of * jnp.repeat(jnp.exp(draws), shape[dim] // parts).reshape((-1,) + (1,) * (len(shape) - 1 - dim))
    return factor_of


def gaussian(stream_key, dims, deviation, limit, cuts=(), kind=jnp.bfloat16):
    result = deviation * jax.random.normal(stream_key, dims, jnp.float32)
    if cuts:
        result = result * levels(stream_key, dims, cuts, -0.22, 0.18)
    return jnp.clip(result, -limit, limit).astype(kind)


def setup_inputs(seed: int = 0) -> dict:
    arg_keys = jax.random.split(jax.random.key(seed), 15)
    return {
        "carried": jnp.clip(jax.random.uniform(arg_keys[0], (2, SESS, H), jnp.float32, -0.9, 0.9) * levels(arg_keys[0], (2, SESS, H), ((1, 32),), -0.4, 0.0), -0.9, 0.9),
        "session_plan": draw_session_plan(jax.random.fold_in(arg_keys[14], 71), 0),
        "item_ids": draw_item_ids(jax.random.fold_in(arg_keys[14], 71), 0),
        "target_ids": draw_target_ids(jax.random.fold_in(arg_keys[14], 71), 0),
        "reset_mask": with_ends((jax.random.randint(arg_keys[4], (STEPS, SESS), 0, 6) < 1).astype(jnp.int32), jax.random.fold_in(arg_keys[4], 1), 0, 1),
        "valid_counts": with_ends(jax.random.randint(arg_keys[5], (SESS,), 1, STEPS + 1), jax.random.fold_in(arg_keys[5], 1), 1, STEPS).astype(jnp.int32),
        "negative_ids": draw_negative_ids(jax.random.fold_in(arg_keys[14], 71), 0),
        "input_table": gaussian(arg_keys[7], (ITEMS, G3), 0.6, 4.0, ((0, 8),)),
        "output_table": gaussian(arg_keys[8], (ITEMS, H), 0.12, 0.69921875, ((0, 8),)),
        "output_bias": gaussian(arg_keys[9], (ITEMS,), 0.5, 3.0, ((0, 8),)),
        "hidden_one": gaussian(arg_keys[10], (H, G3), H ** -0.5, 0.1875, ((1, 4),)),
        "input_two": gaussian(arg_keys[11], (H, G3), H ** -0.5, 0.1875, ((1, 4),)),
        "hidden_two": gaussian(arg_keys[12], (H, G3), H ** -0.5, 0.1875, ((1, 4),)),
        "gate_biases": gaussian(arg_keys[13], (2, G3), 0.3, 2.0, ((1, 4),)),
    }


BPREG = 1.0
HIGHEST = lax.Precision.HIGHEST

@jax.custom_vjp
def low(v):
    return lax.optimization_barrier(v.astype(jnp.bfloat16)).astype(jnp.float32)

@jax.custom_vjp
def low_back(v):
    return v

def low_keep(v):
    return (low(v), None)

def low_pass(kept, grad):
    return (grad,)

def back_keep(v):
    return (v, None)

def back_low(kept, grad):
    return (low(grad),)
low.defvjp(low_keep, low_pass)
low_back.defvjp(back_keep, back_low)

def gru_cell(gate_input, hidden_part, previous):
    hidden_size = previous.shape[-1]
    update = jax.nn.sigmoid(gate_input[..., :hidden_size] + hidden_part[..., :hidden_size])
    reset_gate = jax.nn.sigmoid(gate_input[..., hidden_size:2 * hidden_size] + hidden_part[..., hidden_size:2 * hidden_size])
    candidate = jnp.tanh(gate_input[..., 2 * hidden_size:] + reset_gate * hidden_part[..., 2 * hidden_size:])
    return candidate + update * (previous - candidate)

def gru_layer(gate_input, initial, keep_mask, weight):

    def advance(state_now, inputs):
        gate_row, keep_row = inputs
        masked = state_now * keep_row[:, None]
        hidden_part = low_back(jnp.dot(low(masked), weight, precision=HIGHEST))
        updated = gru_cell(gate_row, hidden_part, masked)
        return (updated, updated)
    _, states = lax.scan(advance, initial, (gate_input, keep_mask))
    return states

def bpr_max(score_tgt, score_neg, valid_mask):
    batch_rows = score_tgt.shape[-1]
    diagonal = jnp.eye(batch_rows, dtype=bool)
    positive = lax.optimization_barrier(jnp.sum(jnp.where(diagonal, score_tgt, 0.0), axis=-1))
    all_scores = jnp.concatenate([score_tgt, score_neg], axis=-1)
    masked = jnp.concatenate([jnp.where(diagonal, -jnp.inf, score_tgt), score_neg], axis=-1)
    highest = lax.optimization_barrier(jnp.max(masked, axis=-1, keepdims=True))
    exponent = jnp.exp(masked - highest)
    weights = exponent / lax.optimization_barrier(jnp.sum(exponent, axis=-1, keepdims=True))
    inside = lax.optimization_barrier(jnp.sum(weights * jax.nn.sigmoid(positive[..., None] - all_scores), axis=-1))
    penalty = lax.optimization_barrier(jnp.sum(weights * all_scores * all_scores, axis=-1))
    return jnp.sum(valid_mask * (-jnp.log(inside) + BPREG * penalty))

def reference(carried, session_plan, item_ids, target_ids, reset_mask, valid_counts, negative_ids, input_table, output_table, output_bias, hidden_one, input_two, hidden_two, gate_biases):
    devices_all = SESS // B_DEV
    slot_all = jnp.arange(SESS, dtype=jnp.int32)
    loc_of = slot_all // B_DEV % N_LOC
    dest_index = (session_plan // B_DEV * N_LOC + loc_of) * B_DEV + session_plan % B_DEV
    source_index = jnp.zeros((SESS,), jnp.int32).at[dest_index].set(slot_all)
    keep_all = (1 - reset_mask).astype(jnp.float32)
    step_index = jnp.arange(STEPS, dtype=jnp.int32)

    def forward(carried_f, input_f, output_f, bias_f, hidden_one_f, input_two_f, hidden_two_f, gate_f):
        moved = carried_f[:, source_index]
        negative_rows = output_f[negative_ids]
        negative_bias = bias_f[negative_ids]

        def device_block(total, device_idx):
            start = device_idx * B_DEV
            items_blk = lax.dynamic_slice_in_dim(item_ids, start, B_DEV, 1)
            targets_blk = lax.dynamic_slice_in_dim(target_ids, start, B_DEV, 1)
            keep_blk = lax.dynamic_slice_in_dim(keep_all, start, B_DEV, 1)
            counts_blk = lax.dynamic_slice_in_dim(valid_counts, start, B_DEV, 0)
            state_blk = lax.dynamic_slice_in_dim(moved, start, B_DEV, 1)
            layer_one_in = low_back(input_f[items_blk] + gate_f[0])
            first = gru_layer(layer_one_in, state_blk[0], keep_blk, hidden_one_f)
            layer_two_in = low_back(jnp.einsum('tbh,hg->tbg', low(first), input_two_f, precision=HIGHEST) + gate_f[1])
            second = gru_layer(layer_two_in, state_blk[1], keep_blk, hidden_two_f)
            second_low = low(second)
            target_rows = low_back(output_f[targets_blk])
            target_bias = low_back(bias_f[targets_blk])
            score_tgt = low_back(jnp.einsum('tbh,tch->tbc', second_low, target_rows, precision=HIGHEST)) + target_bias[:, None, :]
            score_neg = low_back(jnp.einsum('tbh,nh->tbn', second_low, negative_rows, precision=HIGHEST)) + negative_bias
            valid_mask = (step_index[:, None] < counts_blk[None, :]).astype(jnp.float32)
            return (total + bpr_max(score_tgt, score_neg, valid_mask), None)
        total, _ = lax.scan(jax.checkpoint(device_block), jnp.zeros((), jnp.float32), jnp.arange(devices_all, dtype=jnp.int32))
        return total / STEPS
    floats = tuple((array.astype(jnp.float32) for array in (carried, input_table, output_table, output_bias, hidden_one, input_two, hidden_two, gate_biases)))
    loss, pullback = jax.vjp(forward, *floats)
    grads = pullback(jnp.ones_like(loss))
    return (grads[1], grads[2], grads[3], grads[4], grads[5], grads[6], grads[7], grads[0])
```

```python
import functools

import jax
import jax.numpy as jnp
from jax import lax
from jax.experimental import pallas as pl
from jax.experimental.pallas import tpu as pltpu
from jax.sharding import PartitionSpec as P

BPREG = 1.0
BF16 = jnp.bfloat16
F32 = jnp.float32
I32 = jnp.int32
LANES = 128
VMEM_LIMIT = 48 << 20


def swap(x, axis, bit):
    n = lax.axis_size(axis)
    return lax.ppermute(x, axis, [(i, i ^ bit) for i in range(n)])


def gather_xor(x, axis):
    blocks = {0: x}
    bit = lax.axis_size(axis) // 2
    while bit:
        for k in list(blocks):
            blocks[k | bit] = swap(blocks[k], axis, bit)
        bit //= 2
    return [blocks[k] for k in range(len(blocks))]


def send_xor(chunks, axis):
    return [chunks[0]] + [swap(chunks[j], axis, j) for j in range(1, len(chunks))]


def kernel_call(body, outs, ins, smem=0, scratch=(), flops=0):
    nbytes = sum(a.size * a.dtype.itemsize for a in ins)
    nbytes += sum(int(functools.reduce(lambda a, b: a * b, o.shape)) * o.dtype.itemsize for o in outs)
    return pl.pallas_call(
        body,
        out_shape=outs,
        in_specs=[pl.BlockSpec(memory_space=pltpu.SMEM)] * smem
        + [pl.BlockSpec(memory_space=pltpu.VMEM)] * (len(ins) - smem),
        scratch_shapes=list(scratch),
        compiler_params=pltpu.CompilerParams(vmem_limit_bytes=VMEM_LIMIT),
        cost_estimate=pl.CostEstimate(flops=flops, bytes_accessed=nbytes, transcendentals=0),
    )(*ins)


def shape(dims, dtype):
    return jax.ShapeDtypeStruct(dims, dtype)


def iota(dims, dim):
    return lax.broadcasted_iota(I32, dims, dim)


def dot(a, b, ca=1, cb=0):
    return lax.dot_general(a, b, (((ca,), (cb,)), ((), ())), preferred_element_type=F32)


def low(cond):
    return jnp.where(cond, 1.0, 0.0).astype(BF16)


def route_kernel(owners, rows, cap, batch, ccap, in_ref, tg_ref, plan_ref, s_in, s_tg, s_pl, req):
    width = 2 * cap + ccap

    def place(ids, span):
        n = ids.shape[0]
        owner_i = iota((n, owners), 1)
        member = (ids >= owner_i * span) & (ids < (owner_i + 1) * span)
        earlier = low(iota((n, n), 1) < iota((n, n), 0))
        before = dot(earlier, low(member))
        rank = jnp.sum(jnp.where(member, before, 0.0), axis=1, keepdims=True).astype(I32)
        owner = jnp.sum(jnp.where(member, owner_i, 0).astype(F32), axis=1, keepdims=True).astype(I32)
        return owner, rank

    def wanted(owner, rank, offset, value):
        n = owner.shape[0]
        hit = iota((n, owners * width), 1) == owner * width + offset + rank
        return jnp.sum(jnp.where(hit, value.astype(F32), 0.0), axis=0, keepdims=True)

    o_in, r_in = place(in_ref[...], rows)
    o_tg, r_tg = place(tg_ref[...], rows)
    o_pl, r_pl = place(plan_ref[...], batch)
    s_in[...] = o_in * cap + r_in
    s_tg[...] = o_tg * cap + r_tg
    s_pl[...] = o_pl * ccap + r_pl
    total = wanted(o_in, r_in, 0, in_ref[...] + 1)
    total += wanted(o_tg, r_tg, cap, tg_ref[...] + 1)
    total += wanted(o_pl, r_pl, 2 * cap, plan_ref[...] - o_pl * batch + 1)
    req[...] = total.astype(I32)


def extend(value, keep, hidden):
    lane = iota(value.shape, 1)
    return jnp.where(lane == hidden, 1.0, jnp.where(lane == hidden + 1, keep, value)).astype(BF16)


def run_steps(steps, batch, hidden, l, keep_ref, w_refs, x_of, start, state_ref, res, q_s):
    n_loc = len(w_refs)
    wide = start.shape[1]
    tail = jnp.zeros((batch, wide), F32)
    lane = iota((batch, wide), 1)
    prev = start
    for t in range(steps):
        at = pl.ds(t * batch, batch)
        keep = keep_ref[at, :]
        state_ref[at, :] = extend(prev, keep, hidden)
        p = prev * keep
        p_low = p.astype(BF16)
        for j in range(n_loc):
            q_s[l ^ j] = dot(p_low, w_refs[j][...])
        q = jnp.concatenate([q_s[i] for i in range(n_loc)] + [tail], axis=1)
        x = x_of(t)
        h2 = 2 * hidden
        z = jax.nn.sigmoid(x[:, :wide] + q[:, :wide])
        r = jax.nn.sigmoid(x[:, hidden : hidden + wide] + q[:, hidden : hidden + wide])
        qn = q[:, h2 : h2 + wide]
        n = jnp.tanh(x[:, h2 : h2 + wide] + r * qn)
        prev = jnp.where(lane < hidden, n + z * (p - n), 0.0)
        for ref, val in zip(res, (z, r, n, qn, p)):
            ref[at, :] = val
    state_ref[pl.ds(steps * batch, batch), :] = extend(prev, 0.0, hidden)


def first_kernel(
    dims, l_ref, keep_ref, slot_ref, land_ref, got_ref, rows_ref, *refs
):
    steps, batch, hidden, bias_row, n_loc = dims
    w_refs, refs = refs[:n_loc], refs[n_loc:]
    state_ref, start2_ref, z_ref, r_ref, n_ref, qn_ref, p_ref, q_s, b_s = refs
    wide = z_ref.shape[1]
    l = l_ref[0]
    for j in range(n_loc):
        b_s[l ^ j] = w_refs[j][bias_row : bias_row + 16, :].astype(F32)
    bias = jnp.concatenate([b_s[i][0:1, :] for i in range(n_loc)], axis=1)
    pad = jnp.zeros((batch, wide), F32)
    land = low(iota((batch, land_ref.shape[1]), 0) == land_ref[...])
    moved = dot(land, got_ref[...])
    start2_ref[...] = moved[:, wide:]

    def x_of(t):
        slot = slot_ref[pl.ds(t * batch, batch), :]
        pick = low(iota((batch, rows_ref.shape[0]), 1) == slot)
        return jnp.concatenate([dot(pick, rows_ref[...]) + bias, pad], axis=1)

    run_steps(
        steps, batch, hidden, l, keep_ref, w_refs, x_of, moved[:, :wide], state_ref,
        (z_ref, r_ref, n_ref, qn_ref, p_ref), q_s,
    )


def second_kernel(dims, l_ref, keep_ref, start_ref, below_ref, *refs):
    steps, batch, hidden, n_loc = dims
    in_refs, w_refs, refs = refs[:n_loc], refs[n_loc : 2 * n_loc], refs[2 * n_loc :]
    state_ref, z_ref, r_ref, n_ref, qn_ref, p_ref, q_s, x_s = refs
    wide = z_ref.shape[1]
    l = l_ref[0]
    below = below_ref[pl.ds(batch, steps * batch), :]
    for j in range(n_loc):
        x_s[l ^ j] = dot(below, in_refs[j][...])
    pad = jnp.zeros((batch, wide), F32)

    def x_of(t):
        return jnp.concatenate(
            [x_s[i][t * batch : (t + 1) * batch, :] for i in range(n_loc)] + [pad], axis=1
        )

    run_steps(
        steps, batch, hidden, l, keep_ref, w_refs, x_of, start_ref[...], state_ref,
        (z_ref, r_ref, n_ref, qn_ref, p_ref), q_s,
    )


def score_kernel(dims, valid_ref, slot_ref, state_ref, tg_ref, *refs):
    steps, batch, n_loc = dims
    neg_refs, refs = refs[:n_loc], refs[n_loc:]
    gn_refs, into_ref, send_ref, tgg_s = refs[:n_loc], refs[n_loc], refs[n_loc + 1], refs[n_loc + 2]
    diag = iota((batch, batch), 0) == iota((batch, batch), 1)
    slots = tg_ref.shape[0]
    for t in range(steps):
        at = pl.ds(t * batch, batch)
        second = state_ref[pl.ds((t + 1) * batch, batch), :]
        pick = low(iota((batch, slots), 1) == slot_ref[at, :])
        targets = dot(pick, tg_ref[...]).astype(BF16)
        st = dot(second, targets, 1, 1)
        sn = [dot(second, ref[...], 1, 1) for ref in neg_refs]
        pos = jnp.sum(jnp.where(diag, st, 0.0), axis=1, keepdims=True)
        top = jnp.max(jnp.where(diag, -jnp.inf, st), axis=1, keepdims=True)
        for s in sn:
            top = jnp.maximum(top, jnp.max(s, axis=1, keepdims=True))
        parts = [(st, jnp.where(diag, 0.0, jnp.exp(st - top)))]
        parts += [(s, jnp.exp(s - top)) for s in sn]
        mass = sum(jnp.sum(e, axis=1, keepdims=True) for _, e in parts)
        scale = 1.0 / mass
        parts = [(s, e * scale, jax.nn.sigmoid(pos - s)) for s, e in parts]
        inside = sum(jnp.sum(w * g, axis=1, keepdims=True) for _, w, g in parts)
        penalty = sum(jnp.sum(w * s * s, axis=1, keepdims=True) for s, w, _ in parts)
        slope = sum(jnp.sum(w * g * (1.0 - g), axis=1, keepdims=True) for _, w, g in parts)
        inv = 1.0 / inside
        weight = valid_ref[at, :]
        grads = [
            weight * w * (1.0 + BPREG * (s * s + 2.0 * s - penalty) - g * g * inv)
            for s, w, g in parts
        ]
        gt = grads[0] - jnp.where(diag, weight * slope * inv, 0.0)
        gt_low = gt.astype(BF16)
        into = dot(gt_low, targets)
        for j in range(n_loc):
            gn_low = grads[j + 1].astype(BF16)
            gn_refs[j][at, :] = gn_low
            into += dot(gn_low, neg_refs[j][...])
        into_ref[at, :] = into
        tgg_s[at, :] = dot(gt_low, second, 0, 0).astype(BF16)
    pick = low(iota((steps * batch, slots), 1) == slot_ref[...])
    send_ref[...] = dot(pick, tgg_s[...], 0, 0).astype(BF16)


def back_steps(steps, batch, hidden, l, keep_ref, w_refs, into_ref, res, dq_s, emit):
    n_loc = len(w_refs)
    chunk = dq_s.shape[2]
    wide = into_ref.shape[1]
    lane = iota((batch, wide), 1)
    z_ref, r_ref, n_ref, qn_ref, p_ref = res
    carry = jnp.zeros((batch, wide), F32)
    for t in reversed(range(steps)):
        at = pl.ds(t * batch, batch)
        g = jnp.where(lane < hidden, into_ref[at, :] + carry, 0.0)
        z, r, n, qn, p = (ref[at, :] for ref in (z_ref, r_ref, n_ref, qn_ref, p_ref))
        dc = g * (1.0 - z) * (1.0 - n * n)
        da_z = (g * (p - n) * z * (1.0 - z))[:, :hidden]
        da_r = (dc * qn * r * (1.0 - r))[:, :hidden]
        da_n = dc[:, :hidden]
        dq_n = (dc * r)[:, :hidden]
        da = jnp.concatenate([da_z, da_r, da_n], axis=1)
        dq = jnp.concatenate([da_z, da_r, dq_n], axis=1)
        emit(t, da, dq)
        for i in range(n_loc):
            dq_s[i] = dq[:, i * chunk : (i + 1) * chunk]
        dp = g * z
        for j in range(n_loc):
            dp += dot(dq_s[l ^ j].astype(BF16), w_refs[j][...], 1, 1)
        carry = dp * keep_ref[at, :]
    return jnp.where(lane < hidden, carry, 0.0)


def back_second_kernel(dims, l_ref, keep_ref, into_ref, *refs):
    steps, batch, hidden, n_loc = dims
    res, refs = refs[:5], refs[5:]
    in_refs, w_refs, refs = refs[:n_loc], refs[n_loc : 2 * n_loc], refs[2 * n_loc :]
    init_ref, first_ref, refs = refs[0], refs[1], refs[2:]
    ch_refs, refs = refs[:n_loc], refs[n_loc:]
    dq_s, da_all, dq_all = refs
    l = l_ref[0]
    chunk = dq_s.shape[2]

    def emit(t, da, dq):
        for i in range(n_loc):
            da_all[i, pl.ds(t * batch, batch), :] = da[:, i * chunk : (i + 1) * chunk]
            dq_all[i, pl.ds(t * batch, batch), :] = dq[:, i * chunk : (i + 1) * chunk]

    init_ref[...] = back_steps(
        steps, batch, hidden, l, keep_ref, w_refs, into_ref, res, dq_s, emit
    )
    rows = steps * batch
    total = None
    for j in range(n_loc):
        da_low = da_all[l ^ j].astype(BF16)
        ch_refs[j][pl.ds(0, rows), :] = da_low
        ch_refs[j][pl.ds(rows, rows), :] = dq_all[l ^ j].astype(BF16)
        part = dot(da_low, in_refs[j][...], 1, 1)
        total = part if total is None else total + part
    first_ref[...] = total


def back_first_kernel(dims, l_ref, keep_ref, slot_ref, land_ref, init2_ref, into_ref, *refs):
    steps, batch, hidden, n_loc = dims
    res, refs = refs[:5], refs[5:]
    w_refs, refs = refs[:n_loc], refs[n_loc:]
    send_ref, back_ref, refs = refs[0], refs[1], refs[2:]
    ch_refs, refs = refs[:n_loc], refs[n_loc:]
    dq_s, da_all, dq_all, bias_s = refs
    l = l_ref[0]
    chunk = dq_s.shape[2]
    wide = into_ref.shape[1]

    def emit(t, da, dq):
        da_all[pl.ds(t * batch, batch), :] = da.astype(BF16)
        for i in range(n_loc):
            dq_all[i, pl.ds(t * batch, batch), :] = dq[:, i * chunk : (i + 1) * chunk]

    init = back_steps(steps, batch, hidden, l, keep_ref, w_refs, into_ref, res, dq_s, emit)
    rows = steps * batch
    da = da_all[...]
    bias = jnp.sum(da.astype(F32), axis=0, keepdims=True)
    for i in range(n_loc):
        part = bias[:, i * chunk : (i + 1) * chunk]
        bias_s[i] = jnp.concatenate([part, jnp.zeros((15, chunk), F32)], axis=0)
    for j in range(n_loc):
        ch_refs[j][pl.ds(0, rows), :] = dq_all[l ^ j].astype(BF16)
        ch_refs[j][pl.ds(rows, 16), :] = bias_s[l ^ j].astype(BF16)
    pick = low(iota((rows, send_ref.shape[0]), 1) == slot_ref[...])
    send_ref[...] = dot(pick, da, 0, 0).astype(BF16)
    land = low(iota((batch, land_ref.shape[1]), 0) == land_ref[...])
    back_ref[:, :wide] = dot(land, init.astype(BF16), 0, 0).astype(BF16)
    back_ref[:, wide:] = dot(land, init2_ref[...].astype(BF16), 0, 0).astype(BF16)


def dense_two_kernel(dims, *refs):
    steps, batch, hidden, n_loc = dims
    rows = steps * batch
    a_refs, b_refs, ch_refs = refs[:n_loc], refs[n_loc : 2 * n_loc], refs[2 * n_loc : 3 * n_loc]
    out_ref = refs[3 * n_loc]
    wide = a_refs[0].shape[1]
    for which in range(2):
        total = None
        for j in range(n_loc):
            if which == 0:
                left = a_refs[j][pl.ds(batch, rows), :]
                right = ch_refs[j][pl.ds(0, rows), :]
            else:
                left = b_refs[j][pl.ds(0, rows), :]
                left = (left.astype(F32) * left[:, hidden + 1 : hidden + 2].astype(F32)).astype(BF16)
                right = ch_refs[j][pl.ds(rows, rows), :]
            part = dot(left, right, 0, 0)
            total = part if total is None else total + part
        out_ref[pl.ds(which * wide, wide), :] = total.astype(BF16)


def dense_one_kernel(dims, *refs):
    steps, batch, hidden, bias_row, n_loc = dims
    rows = steps * batch
    a_refs, ch_refs = refs[:n_loc], refs[n_loc : 2 * n_loc]
    out_ref = refs[2 * n_loc]
    total, bias = None, None
    for j in range(n_loc):
        left = a_refs[j][pl.ds(0, rows), :]
        left = (left.astype(F32) * left[:, hidden + 1 : hidden + 2].astype(F32)).astype(BF16)
        part = dot(left, ch_refs[j][pl.ds(0, rows), :], 0, 0)
        extra = ch_refs[j][pl.ds(rows, 16), :].astype(F32)
        total = part if total is None else total + part
        bias = extra if bias is None else bias + extra
    out_ref[...] = total.astype(BF16)
    out_ref[pl.ds(bias_row, 16), :] = bias.astype(BF16)


def neg_kernel(n_loc, *refs):
    gn_refs, b_refs, out_ref = refs[:n_loc], refs[n_loc : 2 * n_loc], refs[2 * n_loc]
    rows = gn_refs[0].shape[0]
    batch = b_refs[0].shape[0] - rows
    total = None
    for j in range(n_loc):
        part = dot(gn_refs[j][...], b_refs[j][pl.ds(batch, rows), :], 0, 0)
        total = part if total is None else total + part
    out_ref[...] = total.astype(BF16)


def on_device(
    carried,
    session_plan,
    item_ids,
    target_ids,
    reset_mask,
    valid_counts,
    negative_ids,
    input_table,
    output_table,
    output_bias,
    hidden_one,
    input_two,
    hidden_two,
    gate_biases,
):
    hidden = carried.shape[2]
    wide = -(-(hidden + 2) // LANES) * LANES
    bias_row = wide - 16
    steps, batch = item_ids.shape
    events = steps * batch
    owners = lax.axis_size("grp")
    n_loc = lax.axis_size("loc")
    grp = lax.axis_index("grp")
    loc = lax.axis_index("loc")
    rows = input_table.shape[0]
    base = grp * rows
    gates = input_table.shape[1]
    chunk = gates // n_loc
    cap = events // owners + events // (2 * owners)
    ccap = 4 * batch // owners
    slots, cslots = owners * cap, owners * ccap
    width = 2 * cap + ccap
    neg_own = negative_ids.shape[0] // owners // n_loc
    neg_part = owners * neg_own
    l_arr = loc.astype(I32).reshape(1)

    def pad_rows(w, extra, at):
        out = jnp.zeros((wide, w.shape[1]), BF16).at[: w.shape[0]].set(w)
        return out if extra is None else out.at[at].set(extra)

    w_one = gather_xor(pad_rows(hidden_one, gate_biases[0], bias_row), "loc")
    w_in = gather_xor(pad_rows(input_two, gate_biases[1], hidden), "loc")
    w_two = gather_xor(pad_rows(hidden_two, None, 0), "loc")

    slot_in, slot_tg, slot_pl, request = kernel_call(
        functools.partial(route_kernel, owners, rows, cap, batch, ccap),
        [
            shape((events, 1), I32),
            shape((events, 1), I32),
            shape((batch, 1), I32),
            shape((1, owners * width), I32),
        ],
        [item_ids.reshape(events, 1), target_ids.reshape(events, 1), session_plan.reshape(batch, 1)],
    )
    arrived = lax.all_to_all(
        request.reshape(owners, width), "grp", split_axis=0, concat_axis=0, tiled=True
    )
    in_ids = (arrived[:, :cap] - 1 - base).reshape(slots)
    tg_ids = arrived[:, cap : 2 * cap] - 1 - base
    land = (arrived[:, 2 * cap :] - 1).reshape(1, cslots)
    mine = lax.dynamic_slice(
        negative_ids.reshape(owners, n_loc, neg_own), (grp, loc, 0), (1, 1, neg_own)
    ).reshape(1, neg_own) - base
    out_ids = jnp.concatenate(
        [tg_ids, jnp.broadcast_to(mine, (owners, neg_own))], axis=1
    ).reshape(owners * (cap + neg_own))
    row_range = jnp.arange(rows, dtype=I32)

    pair = jnp.pad(carried.astype(BF16), ((0, 0), (0, 0), (0, wide - hidden)))
    pair = jnp.concatenate([pair[0], pair[1]], axis=1)
    pick_pl = (slot_pl == jnp.arange(cslots, dtype=I32)[None, :]).astype(BF16)
    got_c = lax.all_to_all(
        dot(pick_pl, pair, 0, 0).astype(BF16).reshape(owners, ccap, 2 * wide),
        "grp", split_axis=0, concat_axis=0, tiled=True,
    ).reshape(cslots, 2 * wide)

    pick_in = (in_ids[:, None] == row_range[None, :]).astype(BF16)
    got_rows = lax.all_to_all(
        dot(pick_in, input_table).astype(BF16).reshape(owners, cap, gates),
        "grp", split_axis=0, concat_axis=0, tiled=True,
    ).reshape(slots, gates)
    table_ext = jnp.concatenate(
        [output_table, output_bias[:, None], jnp.zeros((rows, wide - hidden - 1), BF16)], axis=1
    )
    pick_out = (out_ids[:, None] == row_range[None, :]).astype(BF16)
    got_out = lax.all_to_all(
        dot(pick_out, table_ext).astype(BF16).reshape(owners, cap + neg_own, wide),
        "grp", split_axis=0, concat_axis=0, tiled=True,
    )
    tg_rows = got_out[:, :cap].reshape(slots, wide)
    negs = gather_xor(got_out[:, cap:].reshape(neg_part, wide), "loc")

    keep = (1 - reset_mask).astype(F32).reshape(events, 1)
    valid = (jnp.arange(steps, dtype=I32)[:, None] < valid_counts[None, :]).astype(F32)
    valid = (valid / steps).reshape(events, 1)

    flop = 2 * events * wide * gates
    res_shapes = [shape((events, wide), F32)] * 5
    state_shape = shape(((steps + 1) * batch, wide), BF16)
    q_scratch = pltpu.VMEM((n_loc, batch, chunk), F32)
    all_scratch = pltpu.VMEM((n_loc, events, chunk), F32)

    state_a, start_two, *res_one = kernel_call(
        functools.partial(first_kernel, (steps, batch, hidden, bias_row, n_loc)),
        [state_shape, shape((batch, wide), F32)] + res_shapes,
        [l_arr, keep, slot_in, land, got_c, got_rows] + w_one,
        1,
        [q_scratch, pltpu.VMEM((n_loc, 16, chunk), F32)],
        flop,
    )
    states_a = gather_xor(state_a, "loc")
    state_b, *res_two = kernel_call(
        functools.partial(second_kernel, (steps, batch, hidden, n_loc)),
        [state_shape] + res_shapes,
        [l_arr, keep, start_two, state_a] + w_in + w_two,
        1,
        [q_scratch, all_scratch],
        2 * flop,
    )
    states_b = gather_xor(state_b, "loc")

    *g_neg, into_second, send_tg = kernel_call(
        functools.partial(score_kernel, (steps, batch, n_loc)),
        [shape((events, neg_part), BF16)] * n_loc
        + [shape((events, wide), F32), shape((slots, wide), BF16)],
        [valid, slot_tg, state_b, tg_rows] + negs,
        0,
        [pltpu.VMEM((events, wide), BF16)],
        flop,
    )
    g_neg = send_xor(g_neg, "loc")
    neg_grad = kernel_call(
        functools.partial(neg_kernel, n_loc), [shape((neg_part, wide), BF16)], g_neg + states_b
    )[0]
    got_out_g = lax.all_to_all(
        jnp.concatenate(
            [send_tg.reshape(owners, cap, wide), neg_grad.reshape(owners, neg_own, wide)], axis=1
        ),
        "grp", split_axis=0, concat_axis=0, tiled=True,
    ).reshape(owners * (cap + neg_own), wide)

    init_two, into_first, *ch_two = kernel_call(
        functools.partial(back_second_kernel, (steps, batch, hidden, n_loc)),
        [shape((batch, wide), F32), shape((events, wide), F32)]
        + [shape((2 * events, chunk), BF16)] * n_loc,
        [l_arr, keep, into_second] + res_two + w_in + w_two,
        1,
        [q_scratch, all_scratch, all_scratch],
        2 * flop,
    )
    ch_two = send_xor(ch_two, "loc")
    send_in, back_c, *ch_one = kernel_call(
        functools.partial(back_first_kernel, (steps, batch, hidden, n_loc)),
        [shape((slots, gates), BF16), shape((cslots, 2 * wide), BF16)]
        + [shape((events + 16, chunk), BF16)] * n_loc,
        [l_arr, keep, slot_in, land, init_two, into_first] + res_one + w_one,
        1,
        [q_scratch, pltpu.VMEM((events, gates), BF16), all_scratch, pltpu.VMEM((n_loc, 16, chunk), F32)],
        flop,
    )
    ch_one = send_xor(ch_one, "loc")

    dense_two = kernel_call(
        functools.partial(dense_two_kernel, (steps, batch, hidden, n_loc)),
        [shape((2 * wide, chunk), BF16)],
        states_a + states_b + ch_two,
        0, (), 2 * flop,
    )[0]
    dense_one = kernel_call(
        functools.partial(dense_one_kernel, (steps, batch, hidden, bias_row, n_loc)),
        [shape((wide, chunk), BF16)],
        states_a + ch_one,
        0, (), flop,
    )[0]

    def all_sum(x):
        share = lax.psum_scatter(x, "grp", scatter_dimension=0, tiled=True)
        return lax.all_gather(share, "grp", axis=0, tiled=True).astype(F32)

    got_in_g = lax.all_to_all(
        send_in.reshape(owners, cap, gates), "grp", split_axis=0, concat_axis=0, tiled=True
    ).reshape(slots, gates)
    got_back = lax.all_to_all(
        back_c.reshape(owners, ccap, 2 * wide), "grp", split_axis=0, concat_axis=0, tiled=True
    ).reshape(cslots, 2 * wide)
    own = rows // n_loc
    own_pad = -(-own // 16) * 16
    row_of = jnp.arange(own_pad, dtype=I32)
    part_of = loc ^ jnp.arange(n_loc, dtype=I32)
    target = jnp.where(row_of[None, :] < own, part_of[:, None] * own + row_of[None, :], rows)
    target = jnp.where(target < rows, target, -rows * (owners + 1)).reshape(n_loc * own_pad)

    def table_sum(ids, grads):
        match = (target[:, None] == ids[None, :]).astype(BF16)
        part = dot(match, grads).astype(BF16).reshape(n_loc, own_pad, grads.shape[1])
        parts = [part[j] for j in range(n_loc)]
        bit = 1
        while bit < n_loc:
            keep_p = [p for j, p in enumerate(parts) if not j & 1]
            send_p = jnp.stack([p for j, p in enumerate(parts) if j & 1])
            got_p = swap(send_p, "loc", bit)
            parts = [p.astype(F32) + got_p[i].astype(F32) for i, p in enumerate(keep_p)]
            bit *= 2
            if bit < n_loc:
                parts = [p.astype(BF16) for p in parts]
        return parts[0][:own]

    table_in = table_sum(in_ids, got_in_g)
    table_out = table_sum(out_ids, got_out_g)

    pair_two = all_sum(dense_two)
    grad_one = all_sum(dense_one)
    back = dot(pick_pl, got_back)
    grad_carried = jnp.stack([back[:, :hidden], back[:, wide : wide + hidden]])
    grad_biases = jnp.stack([grad_one[bias_row], pair_two[hidden]])
    return (
        table_in,
        table_out[:, :hidden],
        table_out[:, hidden],
        grad_one[:hidden],
        pair_two[:hidden],
        pair_two[wide : wide + hidden],
        grad_biases,
        grad_carried,
    )


def solution(mesh):
    in_specs = (
        P(None, ("grp", "loc"), None),
        P(("grp", "loc")),
        P(None, ("grp", "loc")),
        P(None, ("grp", "loc")),
        P(None, ("grp", "loc")),
        P(("grp", "loc")),
        P(),
        P("grp", None),
        P("grp", None),
        P("grp"),
        P(None, "loc"),
        P(None, "loc"),
        P(None, "loc"),
        P(None, "loc"),
    )
    out_specs = (
        P(("grp", "loc"), None),
        P(("grp", "loc"), None),
        P(("grp", "loc")),
        P(None, "loc"),
        P(None, "loc"),
        P(None, "loc"),
        P(None, "loc"),
        P(None, ("grp", "loc"), None),
    )
    return jax.shard_map(
        on_device, mesh=mesh, in_specs=in_specs, out_specs=out_specs, check_vma=False
    )
```

```python
import functools

import jax
import jax.numpy as jnp
from jax import lax
from jax.experimental import pallas as pl
from jax.experimental.pallas import tpu as pltpu
from jax.sharding import PartitionSpec as P

BPREG = 1.0
BF16 = jnp.bfloat16
F32 = jnp.float32
I32 = jnp.int32
LANES = 128
VMEM_LIMIT = 48 << 20


def swap(x, axis, bit):
    n = lax.axis_size(axis)
    return lax.ppermute(x, axis, [(i, i ^ bit) for i in range(n)])


def gather_xor(x, axis):
    blocks = {0: x}
    bit = lax.axis_size(axis) // 2
    while bit:
        for k in list(blocks):
            blocks[k | bit] = swap(blocks[k], axis, bit)
        bit //= 2
    return [blocks[k] for k in range(len(blocks))]


def send_xor(chunks, axis):
    return [chunks[0]] + [swap(chunks[j], axis, j) for j in range(1, len(chunks))]


def kernel_call(body, outs, ins, smem=0, scratch=(), us=1):
    nbytes = sum(a.size * a.dtype.itemsize for a in ins)
    nbytes += sum(int(functools.reduce(lambda a, b: a * b, o.shape)) * o.dtype.itemsize for o in outs)
    return pl.pallas_call(
        body,
        out_shape=outs,
        in_specs=[pl.BlockSpec(memory_space=pltpu.SMEM)] * smem
        + [pl.BlockSpec(memory_space=pltpu.VMEM)] * (len(ins) - smem),
        scratch_shapes=list(scratch),
        compiler_params=pltpu.CompilerParams(vmem_limit_bytes=VMEM_LIMIT),
        cost_estimate=pl.CostEstimate(flops=us * 10**9, bytes_accessed=nbytes, transcendentals=0),
    )(*ins)


def after(x, *deps):
    return lax.optimization_barrier((x,) + deps)[0]


def shape(dims, dtype):
    return jax.ShapeDtypeStruct(dims, dtype)


def iota(dims, dim):
    return lax.broadcasted_iota(I32, dims, dim)


def dot(a, b, ca=1, cb=0):
    return lax.dot_general(a, b, (((ca,), (cb,)), ((), ())), preferred_element_type=F32)


def low(cond):
    return jnp.where(cond, 1.0, 0.0).astype(BF16)


def route_kernel(owners, rows, cap, batch, ccap, in_ref, tg_ref, plan_ref, s_in, s_tg, s_pl, req):
    width = 2 * cap + ccap

    def place(ids, span):
        n = ids.shape[0]
        owner_i = iota((n, owners), 1)
        member = (ids >= owner_i * span) & (ids < (owner_i + 1) * span)
        earlier = low(iota((n, n), 1) < iota((n, n), 0))
        before = dot(earlier, low(member))
        rank = jnp.sum(jnp.where(member, before, 0.0), axis=1, keepdims=True).astype(I32)
        owner = jnp.sum(jnp.where(member, owner_i, 0).astype(F32), axis=1, keepdims=True).astype(I32)
        return owner, rank

    def wanted(owner, rank, offset, value):
        n = owner.shape[0]
        hit = iota((n, owners * width), 1) == owner * width + offset + rank
        return jnp.sum(jnp.where(hit, value.astype(F32), 0.0), axis=0, keepdims=True)

    o_in, r_in = place(in_ref[...], rows)
    o_tg, r_tg = place(tg_ref[...], rows)
    o_pl, r_pl = place(plan_ref[...], batch)
    s_in[...] = o_in * cap + r_in
    s_tg[...] = o_tg * cap + r_tg
    s_pl[...] = o_pl * ccap + r_pl
    total = wanted(o_in, r_in, 0, in_ref[...] + 1)
    total += wanted(o_tg, r_tg, cap, tg_ref[...] + 1)
    total += wanted(o_pl, r_pl, 2 * cap, plan_ref[...] - o_pl * batch + 1)
    req[...] = total.astype(I32)


def extend(value, keep, hidden):
    lane = iota(value.shape, 1)
    return jnp.where(lane == hidden, 1.0, jnp.where(lane == hidden + 1, keep, value)).astype(BF16)


def run_steps(steps, batch, hidden, l, keep_ref, w_refs, x_of, start, state_ref, res, q_s):
    n_loc = len(w_refs)
    wide = start.shape[1]
    tail = jnp.zeros((batch, wide), F32)
    lane = iota((batch, wide), 1)
    prev = start
    for t in range(steps):
        at = pl.ds(t * batch, batch)
        keep = keep_ref[at, :]
        state_ref[at, :] = extend(prev, keep, hidden)
        p = prev * keep
        p_low = p.astype(BF16)
        for j in range(n_loc):
            q_s[l ^ j] = dot(p_low, w_refs[j][...])[:, : q_s.shape[2]]
        q = jnp.concatenate([q_s[i] for i in range(n_loc)] + [tail], axis=1)
        x = x_of(t)
        h2 = 2 * hidden
        z = jax.nn.sigmoid(x[:, :wide] + q[:, :wide])
        r = jax.nn.sigmoid(x[:, hidden : hidden + wide] + q[:, hidden : hidden + wide])
        qn = q[:, h2 : h2 + wide]
        n = jnp.tanh(x[:, h2 : h2 + wide] + r * qn)
        prev = jnp.where(lane < hidden, n + z * (p - n), 0.0)
        for ref, val in zip(res, (z, r, n, qn, p)):
            ref[at, :] = val
    state_ref[pl.ds(steps * batch, batch), :] = extend(prev, 0.0, hidden)


def pad_kernel(at, n_in, l_ref, w_ref, *refs):
    refs, outs = refs[: n_in - 2], refs[n_in - 2 :]
    out_ref = outs[0]
    rows, cols = w_ref.shape
    out_ref[...] = jnp.zeros(out_ref.shape, BF16)
    out_ref[:rows, :cols] = w_ref[...]
    if at is not None:
        which, row = at
        tile = row // 16 * 16
        here = (iota((16, cols), 0) == row - tile).astype(F32)
        old = out_ref[tile : tile + 16, :cols].astype(F32)
        extra = refs[0][which : which + 1, :].astype(F32)
        out_ref[tile : tile + 16, :cols] = (old + here * extra).astype(BF16)
    if len(outs) == 2:
        half = outs[1].shape[0]
        side = l_ref[0] & 1
        outs[1][...] = out_ref[pl.ds(pl.multiple_of(side * half, half), half), :]


def gather_kernel(ids_ref, table_ref, out_ref):
    rows, cols = table_ref.shape
    pick = low(iota((ids_ref.shape[0], rows), 1) == ids_ref[...])
    if out_ref.shape[1] > cols:
        out_ref[...] = jnp.zeros(out_ref.shape, BF16)
    out_ref[:, :cols] = dot(pick, table_ref[...]).astype(BF16)


def gather_biased_kernel(ids_ref, table_ref, bias_ref, out_ref):
    n, wide = out_ref.shape
    rows, cols = table_ref.shape
    pick = low(iota((n, rows), 1) == ids_ref[...])
    parts = [dot(pick, table_ref[...]), dot(pick, bias_ref[...])[:, :1]]
    parts.append(jnp.zeros((n, wide - cols - 1), F32))
    out_ref[...] = jnp.concatenate(parts, axis=1).astype(BF16)


def pack_kernel(slot_ref, carried_ref, one_ref, two_ref):
    pick = low(iota((slot_ref.shape[0], one_ref.shape[0]), 1) == slot_ref[...])
    hidden = carried_ref.shape[2]
    for layer, ref in enumerate((one_ref, two_ref)):
        ref[...] = jnp.zeros(ref.shape, BF16)
        ref[:, :hidden] = dot(pick, carried_ref[layer].astype(BF16), 0, 0).astype(BF16)


def table_kernel(own, pairs, l_ref, *refs):
    mine_ref, far_ref, near_ref = refs[2 * pairs :]
    pad = mine_ref.shape[0]
    l = l_ref[0]
    for j, (ref, at) in enumerate(((mine_ref, None), (near_ref, 0), (far_ref, None), (near_ref, 1))):
        part = None
        for ids_ref, got_ref in zip(refs[:pairs], refs[pairs : 2 * pairs]):
            row = iota((pad, ids_ref.shape[1]), 0)
            hit = (row < own) & (row + (l ^ j) * own == ids_ref[...])
            term = dot(low(hit), got_ref[...])
            part = term if part is None else part + term
        if at is None:
            ref[...] = part
        else:
            ref[at, :, :] = part.astype(BF16)


def table_add_kernel(mine_ref, far_ref, got_ref, sum_ref, send_ref):
    sum_ref[...] = mine_ref[...] + got_ref[0].astype(F32)
    send_ref[...] = (far_ref[...] + got_ref[1].astype(F32)).astype(BF16)


def table_out_kernel(sum_ref, got_ref, out_ref):
    rows, cols = out_ref.shape
    out_ref[...] = (sum_ref[...] + got_ref[...].astype(F32))[:rows, :cols]


def carry_kernel(slot_ref, got_ref, out_ref):
    hidden = out_ref.shape[2]
    wide = got_ref.shape[1] // 2
    pick = low(iota((slot_ref.shape[0], got_ref.shape[0]), 1) == slot_ref[...])
    back = dot(pick, got_ref[...])
    out_ref[0] = back[:, :hidden]
    out_ref[1] = back[:, wide : wide + hidden]


def split_kernel(bit, l_ref, a_ref, b_ref, keep_ref, send_ref):
    half = keep_ref.shape[0]
    side = (l_ref[0] >> bit) & 1
    for ref, at in ((keep_ref, side), (send_ref, 1 - side)):
        rows = pl.ds(pl.multiple_of(at * half, half), half)
        ref[...] = (a_ref[rows, :].astype(F32) + b_ref[rows, :].astype(F32)).astype(BF16)


def add_kernel(a_ref, b_ref, out_ref):
    out_ref[...] = (a_ref[...].astype(F32) + b_ref[...].astype(F32)).astype(BF16)


def join_kernel(bit, l_ref, a_ref, b_ref, out_ref):
    half = a_ref.shape[0]
    side = (l_ref[0] >> bit) & 1
    for ref, at in ((a_ref, side), (b_ref, 1 - side)):
        out_ref[pl.ds(pl.multiple_of(at * half, half), half), :] = ref[...]


def final_kernel(hidden, bias_row, l_ref, a_ref, b_ref, out_ref, bias_ref):
    side = l_ref[0] & 1
    cols = out_ref.shape[1]
    half = a_ref.shape[0]
    at = (bias_row - half) // 16 * 16
    for first, second, when in ((a_ref, b_ref, 0), (b_ref, a_ref, 1)):

        @pl.when(side == when)
        def _():
            out_ref[:half, :] = first[...].astype(F32)[:, :cols]
            out_ref[half:, :] = second[...].astype(F32)[: hidden - half, :cols]
            row = bias_row - half - at
            bias_ref[...] = second[at : at + 16, :].astype(F32)[row : row + 1, :cols]


def first_kernel(
    dims, l_ref, keep_ref, slot_ref, land_ref, got_ref, rows_ref, *refs
):
    steps, batch, hidden, bias_row, n_loc = dims
    w_refs, refs = refs[:n_loc], refs[n_loc:]
    state_ref, z_ref, r_ref, n_ref, qn_ref, p_ref, q_s, b_s, x_s = refs
    wide = z_ref.shape[1]
    l = l_ref[0]
    pick = low(iota((steps * batch, rows_ref.shape[0]), 1) == slot_ref[...])
    x_s[...] = dot(pick, rows_ref[...])
    for j in range(n_loc):
        b_s[l ^ j] = w_refs[j][bias_row : bias_row + 16, :].astype(F32)[:, : b_s.shape[2]]
    bias = jnp.concatenate([b_s[i][0:1, :] for i in range(n_loc)], axis=1)
    pad = jnp.zeros((batch, wide), F32)
    land = low(iota((batch, land_ref.shape[1]), 0) == land_ref[...])
    moved = dot(land, got_ref[...])

    def x_of(t):
        gates = bias.shape[1]
        return jnp.concatenate([x_s[pl.ds(t * batch, batch), :][:, :gates] + bias, pad], axis=1)

    run_steps(
        steps, batch, hidden, l, keep_ref, w_refs, x_of, moved, state_ref,
        (z_ref, r_ref, n_ref, qn_ref, p_ref), q_s,
    )


def second_kernel(dims, l_ref, keep_ref, land_ref, got_ref, below_ref, *refs):
    steps, batch, hidden, n_loc = dims
    in_refs, w_refs, refs = refs[:n_loc], refs[n_loc : 2 * n_loc], refs[2 * n_loc :]
    state_ref, z_ref, r_ref, n_ref, qn_ref, p_ref, q_s, x_s = refs
    wide = z_ref.shape[1]
    l = l_ref[0]
    land = low(iota((batch, land_ref.shape[1]), 0) == land_ref[...])
    moved = dot(land, got_ref[...])
    below = below_ref[pl.ds(batch, steps * batch), :]
    for j in range(n_loc):
        x_s[l ^ j] = dot(below, in_refs[j][...])[:, : x_s.shape[2]]
    pad = jnp.zeros((batch, wide), F32)

    def x_of(t):
        return jnp.concatenate(
            [x_s[i][t * batch : (t + 1) * batch, :] for i in range(n_loc)] + [pad], axis=1
        )

    run_steps(
        steps, batch, hidden, l, keep_ref, w_refs, x_of, moved, state_ref,
        (z_ref, r_ref, n_ref, qn_ref, p_ref), q_s,
    )


def score_kernel(dims, valid_ref, slot_ref, state_ref, tg_ref, *refs):
    steps, batch, n_loc = dims
    rows = steps * batch
    neg_refs, refs = refs[:n_loc], refs[n_loc:]
    gn_refs, into_ref, send_ref = refs[:n_loc], refs[n_loc], refs[n_loc + 1]
    sn_s, tgt_s, tgg_s = refs[n_loc + 2 :]
    diag = iota((batch, batch), 0) == iota((batch, batch), 1)
    slots = tg_ref.shape[0]
    pick = low(iota((rows, slots), 1) == slot_ref[...])
    tgt_s[...] = dot(pick, tg_ref[...]).astype(BF16)
    every = state_ref[pl.ds(batch, rows), :]
    for j in range(n_loc):
        sn_s[j] = dot(every, neg_refs[j][...], 1, 1)
    for t in range(steps):
        at = pl.ds(t * batch, batch)
        second = state_ref[pl.ds((t + 1) * batch, batch), :]
        targets = tgt_s[at, :]
        st = dot(second, targets, 1, 1)
        sn = [sn_s[j, at, :] for j in range(n_loc)]
        pos = jnp.sum(jnp.where(diag, st, 0.0), axis=1, keepdims=True)
        top = jnp.max(jnp.where(diag, -jnp.inf, st), axis=1, keepdims=True)
        for s in sn:
            top = jnp.maximum(top, jnp.max(s, axis=1, keepdims=True))
        parts = [(st, jnp.where(diag, 0.0, jnp.exp(st - top)))]
        parts += [(s, jnp.exp(s - top)) for s in sn]
        mass = sum(jnp.sum(e, axis=1, keepdims=True) for _, e in parts)
        scale = 1.0 / mass
        parts = [(s, e * scale, jax.nn.sigmoid(pos - s)) for s, e in parts]
        inside = sum(jnp.sum(w * g, axis=1, keepdims=True) for _, w, g in parts)
        penalty = sum(jnp.sum(w * s * s, axis=1, keepdims=True) for s, w, _ in parts)
        slope = sum(jnp.sum(w * g * (1.0 - g), axis=1, keepdims=True) for _, w, g in parts)
        inv = 1.0 / inside
        weight = valid_ref[at, :]
        grads = [
            weight * w * (1.0 + BPREG * (s * s + 2.0 * s - penalty) - g * g * inv)
            for s, w, g in parts
        ]
        gt = grads[0] - jnp.where(diag, weight * slope * inv, 0.0)
        gt_low = gt.astype(BF16)
        into_ref[at, :] = dot(gt_low, targets)
        for j in range(n_loc):
            gn_refs[j][at, :] = grads[j + 1].astype(BF16)
        tgg_s[at, :] = dot(gt_low, second, 0, 0).astype(BF16)
    total = into_ref[...]
    for j in range(n_loc):
        total += dot(gn_refs[j][...], neg_refs[j][...])
    into_ref[...] = total
    send_ref[...] = dot(pick, tgg_s[...], 0, 0).astype(BF16)


def back_steps(steps, batch, hidden, chunk, l, keep_ref, w_refs, into_ref, res, dq_s, emit):
    n_loc = len(w_refs)
    dq_s[...] = jnp.zeros(dq_s.shape, F32)
    wide = into_ref.shape[1]
    lane = iota((batch, wide), 1)
    z_ref, r_ref, n_ref, qn_ref, p_ref = res
    carry = jnp.zeros((batch, wide), F32)
    for t in reversed(range(steps)):
        at = pl.ds(t * batch, batch)
        g = jnp.where(lane < hidden, into_ref[at, :] + carry, 0.0)
        z, r, n, qn, p = (ref[at, :] for ref in (z_ref, r_ref, n_ref, qn_ref, p_ref))
        dc = g * (1.0 - z) * (1.0 - n * n)
        da_z = (g * (p - n) * z * (1.0 - z))[:, :hidden]
        da_r = (dc * qn * r * (1.0 - r))[:, :hidden]
        da_n = dc[:, :hidden]
        dq_n = (dc * r)[:, :hidden]
        da = jnp.concatenate([da_z, da_r, da_n], axis=1)
        dq = jnp.concatenate([da_z, da_r, dq_n], axis=1)
        emit(t, da, dq)
        for i in range(n_loc):
            dq_s[i, :, :chunk] = dq[:, i * chunk : (i + 1) * chunk]
        dp = g * z
        for j in range(n_loc):
            dp += dot(dq_s[l ^ j].astype(BF16), w_refs[j][...], 1, 1)
        carry = dp * keep_ref[at, :]
    return jnp.where(lane < hidden, carry, 0.0)


def back_second_kernel(dims, l_ref, keep_ref, into_ref, *refs):
    steps, batch, hidden, chunk, n_loc = dims
    res, refs = refs[:5], refs[5:]
    in_refs, w_refs, refs = refs[:n_loc], refs[n_loc : 2 * n_loc], refs[2 * n_loc :]
    init_ref, first_ref, refs = refs[0], refs[1], refs[2:]
    ch_refs, refs = refs[:n_loc], refs[n_loc:]
    dq_s, da_all, dq_all = refs
    l = l_ref[0]
    da_all[...] = jnp.zeros(da_all.shape, F32)
    dq_all[...] = jnp.zeros(dq_all.shape, F32)

    def emit(t, da, dq):
        for i in range(n_loc):
            da_all[i, pl.ds(t * batch, batch), :chunk] = da[:, i * chunk : (i + 1) * chunk]
            dq_all[i, pl.ds(t * batch, batch), :chunk] = dq[:, i * chunk : (i + 1) * chunk]

    init_ref[...] = back_steps(
        steps, batch, hidden, chunk, l, keep_ref, w_refs, into_ref, res, dq_s, emit
    )
    rows = steps * batch
    total = None
    for j in range(n_loc):
        da_low = da_all[l ^ j].astype(BF16)
        ch_refs[j][pl.ds(0, rows), :] = da_low
        ch_refs[j][pl.ds(rows, rows), :] = dq_all[l ^ j].astype(BF16)
        part = dot(da_low, in_refs[j][...], 1, 1)
        total = part if total is None else total + part
    first_ref[...] = total


def back_first_kernel(dims, l_ref, keep_ref, slot_ref, land_ref, init2_ref, into_ref, *refs):
    steps, batch, hidden, chunk, n_loc = dims
    res, refs = refs[:5], refs[5:]
    w_refs, refs = refs[:n_loc], refs[n_loc:]
    send_ref, back_ref, refs = refs[0], refs[1], refs[2:]
    ch_refs, refs = refs[:n_loc], refs[n_loc:]
    dq_s, da_all, dq_all, bias_s = refs
    l = l_ref[0]
    wide = into_ref.shape[1]
    cols = da_all.shape[1]
    dq_all[...] = jnp.zeros(dq_all.shape, F32)
    bias_s[...] = jnp.zeros(bias_s.shape, F32)

    def emit(t, da, dq):
        da_all[pl.ds(t * batch, batch), :] = da.astype(BF16)
        for i in range(n_loc):
            dq_all[i, pl.ds(t * batch, batch), :chunk] = dq[:, i * chunk : (i + 1) * chunk]

    init = back_steps(steps, batch, hidden, chunk, l, keep_ref, w_refs, into_ref, res, dq_s, emit)
    rows = steps * batch
    da = da_all[...]
    bias = jnp.sum(da.astype(F32), axis=0, keepdims=True)
    for i in range(n_loc):
        part = bias[:, i * chunk : (i + 1) * chunk]
        bias_s[i, 0:1, :chunk] = part
    for j in range(n_loc):
        ch_refs[j][pl.ds(0, rows), :] = dq_all[l ^ j].astype(BF16)
        ch_refs[j][pl.ds(rows, 16), :] = bias_s[l ^ j].astype(BF16)
    pick = low(iota((rows, send_ref.shape[0]), 1) == slot_ref[...])
    if send_ref.shape[1] > cols:
        send_ref[...] = jnp.zeros(send_ref.shape, BF16)
    send_ref[:, :cols] = dot(pick, da, 0, 0).astype(BF16)
    land = low(iota((batch, land_ref.shape[1]), 0) == land_ref[...])
    back_ref[:, :wide] = dot(land, init.astype(BF16), 0, 0).astype(BF16)
    back_ref[:, wide:] = dot(land, init2_ref[...].astype(BF16), 0, 0).astype(BF16)


def scaled(ref, rows, hidden):
    left = ref[pl.ds(0, rows), :].astype(F32)
    return (left * left[:, hidden + 1 : hidden + 2]).astype(BF16)


def dense_kernel(dims, l_ref, *refs):
    steps, batch, hidden, skip, at, bias_row, n_loc = dims
    rows = steps * batch
    left_refs, ch_refs = refs[:n_loc], refs[n_loc : 2 * n_loc]
    keep_ref, send_ref, all_s = refs[2 * n_loc :]
    half = keep_ref.shape[0]
    side = l_ref[0] & 1
    total, bias = None, None
    for j in range(n_loc):
        left = left_refs[j][pl.ds(batch, rows), :] if skip else scaled(left_refs[j], rows, hidden)
        part = dot(left, ch_refs[j][pl.ds(at, rows), :], 0, 0)
        total = part if total is None else total + part
        if bias_row is not None:
            extra = ch_refs[j][pl.ds(rows, 16), :].astype(F32)
            bias = extra if bias is None else bias + extra
    all_s[...] = total.astype(BF16)
    if bias_row is not None:
        all_s[pl.ds(bias_row, 16), :] = bias.astype(BF16)
    keep_ref[...] = all_s[pl.ds(pl.multiple_of(side * half, half), half), :]
    send_ref[...] = all_s[pl.ds(pl.multiple_of((1 - side) * half, half), half), :]


def neg_kernel(n_loc, owners, *refs):
    gn_refs, b_refs, out_ref = refs[:n_loc], refs[n_loc : 2 * n_loc], refs[2 * n_loc]
    rows = gn_refs[0].shape[0]
    batch = b_refs[0].shape[0] - rows
    total = None
    for j in range(n_loc):
        part = dot(gn_refs[j][...], b_refs[j][pl.ds(batch, rows), :], 0, 0)
        total = part if total is None else total + part
    own = out_ref.shape[0] // owners
    places = [(g >> 1) + (g & 1) * (owners // 2) for g in range(owners)]
    blocks = [total[p * own : (p + 1) * own, :] for p in places]
    out_ref[...] = jnp.concatenate(blocks, axis=0).astype(BF16)


def on_device(
    carried,
    session_plan,
    item_ids,
    target_ids,
    reset_mask,
    valid_counts,
    negative_ids,
    input_table,
    output_table,
    output_bias,
    hidden_one,
    input_two,
    hidden_two,
    gate_biases,
):
    hidden = carried.shape[2]
    wide = -(-(hidden + 2) // LANES) * LANES
    bias_row = wide - 16
    steps, batch = item_ids.shape
    events = steps * batch
    owners = lax.axis_size("grp")
    n_loc = lax.axis_size("loc")
    grp = lax.axis_index("grp")
    loc = lax.axis_index("loc")
    rows = input_table.shape[0]
    base = grp * rows
    gates = input_table.shape[1]
    chunk = gates // n_loc
    cap = events // owners + events // (2 * owners)
    ccap = 4 * batch // owners
    slots, cslots = owners * cap, owners * ccap
    width = 2 * cap + ccap
    neg_own = negative_ids.shape[0] // owners // n_loc
    neg_part = owners * neg_own
    l_arr = loc.astype(I32).reshape(1)

    cpad = -(-chunk // LANES) * LANES
    gpad = -(-gates // LANES) * LANES
    w_shape = shape((wide, cpad), BF16)

    g_arr = grp.astype(I32).reshape(1)
    bits = owners.bit_length() - 1

    def padded(w, at, halved):
        ins = [g_arr, w] if at is None else [g_arr, w, gate_biases]
        outs = [w_shape, shape((wide // 2, cpad), BF16)] if halved else [w_shape]
        return kernel_call(functools.partial(pad_kernel, at, len(ins)), outs, ins, 1)

    def near(x):
        return swap(x, "loc", 1)

    def across(x):
        return swap(x, "loc", 2)

    def join(bit, kept, got):
        return kernel_call(
            functools.partial(join_kernel, bit),
            [shape((2 * kept.shape[0],) + kept.shape[1:], BF16)],
            [g_arr, kept, got], 1,
        )[0]

    p_one = padded(hidden_one, (0, bias_row), False)[0]
    y_one = across(p_one)

    bias_col = output_bias[:, None]

    def gathered(ids, table, cols, *bias):
        n = ids.shape[0]
        return kernel_call(
            gather_biased_kernel if bias else gather_kernel,
            [shape((n, cols), BF16)], [ids.reshape(n, 1), table, *bias], 0, (), 2,
        )[0]

    mine = lax.dynamic_slice(
        negative_ids.reshape(owners, n_loc, neg_own), (grp, loc, 0), (1, 1, neg_own)
    ).reshape(neg_own) - base
    negs_by = [gathered(after(mine, p_one), output_table, wide, bias_col)]
    for bit in list(range(1, bits)) + [0]:
        got = swap(negs_by[-1], "grp", 1 << bit)
        negs_by.append(join(bit, negs_by[-1], got))
    negs = negs_by[-1]

    slot_in, slot_tg, slot_pl, request = kernel_call(
        functools.partial(route_kernel, owners, rows, cap, batch, ccap),
        [
            shape((events, 1), I32),
            shape((events, 1), I32),
            shape((batch, 1), I32),
            shape((1, owners * width), I32),
        ],
        [
            after(item_ids, p_one).reshape(events, 1),
            target_ids.reshape(events, 1),
            session_plan.reshape(batch, 1),
        ],
    )

    def to_owners(x):
        got = lax.all_to_all(
            x.reshape((owners, x.shape[0] // owners) + x.shape[1:]),
            "grp", split_axis=0, concat_axis=0, tiled=True,
        )
        return got.reshape(x.shape)

    arrived = to_owners(request.reshape(owners, width))
    in_ids = (arrived[:, :cap] - 1 - base).reshape(slots)
    tg_ids = (arrived[:, cap : 2 * cap] - 1 - base).reshape(slots)
    land = (arrived[:, 2 * cap :] - 1).reshape(1, cslots)

    pack_one, pack_two = kernel_call(
        pack_kernel, [shape((cslots, wide), BF16)] * 2, [slot_pl, carried], 0, (), 2
    )
    p_in, h_in = padded(input_two, (1, hidden), True)
    p_two, h_two = padded(hidden_two, None, True)
    got_c = to_owners(after(pack_one, arrived, negs_by[1]))
    reply_in = gathered(in_ids, input_table, gpad)
    y_in = across(after(h_in, y_one))
    got_rows = to_owners(after(reply_in, got_c, negs_by[-2]))
    y_two = across(after(h_two, y_in))
    got_c2 = to_owners(after(pack_two, got_rows))
    reply_tg = gathered(tg_ids, output_table, wide, bias_col)
    tg_rows = to_owners(after(reply_tg, got_c2))
    y_neg = across(after(negs, y_two))
    y_in = join(0, y_in, swap(y_in, "grp", 1))
    y_two = join(0, y_two, swap(y_two, "grp", 1))

    w_one = [p_one, near(p_one), y_one, near(y_one)]
    w_in = [p_in, near(p_in), y_in, near(y_in)]
    w_two = [p_two, near(p_two), y_two, near(y_two)]
    negs = [negs, near(negs), y_neg, near(y_neg)]

    keep = (1 - reset_mask).astype(F32).reshape(events, 1)
    valid = (jnp.arange(steps, dtype=I32)[:, None] < valid_counts[None, :]).astype(F32)
    valid = (valid / steps).reshape(events, 1)

    res_shapes = [shape((events, wide), F32)] * 5
    state_shape = shape(((steps + 1) * batch, wide), BF16)
    q_scratch = pltpu.VMEM((n_loc, batch, chunk), F32)
    dq_scratch = pltpu.VMEM((n_loc, batch, cpad), F32)
    x_scratch = pltpu.VMEM((n_loc, events, chunk), F32)
    all_scratch = pltpu.VMEM((n_loc, events, cpad), F32)

    state_a, *res_one = kernel_call(
        functools.partial(first_kernel, (steps, batch, hidden, bias_row, n_loc)),
        [state_shape] + res_shapes,
        [l_arr, keep, slot_in, land, got_c, got_rows] + w_one,
        1,
        [q_scratch, pltpu.VMEM((n_loc, 16, chunk), F32), pltpu.VMEM((events, gpad), F32)],
        12,
    )
    state_b, *res_two = kernel_call(
        functools.partial(second_kernel, (steps, batch, hidden, n_loc)),
        [state_shape] + res_shapes,
        [l_arr, keep, land, got_c2, state_a] + w_in + w_two,
        1,
        [q_scratch, x_scratch],
        15,
    )
    y_b = across(after(state_b, y_neg))

    *g_neg, into_second, send_tg = kernel_call(
        functools.partial(score_kernel, (steps, batch, n_loc)),
        [shape((events, neg_part), BF16)] * n_loc
        + [shape((events, wide), F32), shape((slots, wide), BF16)],
        [valid, slot_tg, state_b, tg_rows] + negs,
        0,
        [
            pltpu.VMEM((n_loc, events, neg_part), F32),
            pltpu.VMEM((events, wide), BF16),
            pltpu.VMEM((events, wide), BF16),
        ],
        12,
    )
    g_neg = send_xor(g_neg, "loc")
    init_two, into_first, *ch_two = kernel_call(
        functools.partial(back_second_kernel, (steps, batch, hidden, chunk, n_loc)),
        [shape((batch, wide), F32), shape((events, wide), F32)]
        + [shape((2 * events, cpad), BF16)] * n_loc,
        [l_arr, keep, into_second] + res_two + w_in + w_two,
        1,
        [dq_scratch, all_scratch, all_scratch],
        17,
    )
    ch_two = send_xor(ch_two, "loc")
    y_a = across(after(state_a, into_second))
    got_tg_g = to_owners(send_tg)
    y_b = after(y_b, into_first)
    states_b = [state_b, near(state_b), y_b, near(y_b)]
    neg_grad = kernel_call(
        functools.partial(neg_kernel, n_loc, owners),
        [shape((neg_part, wide), BF16)],
        [after(g_neg[0], into_first)] + g_neg[1:] + states_b,
        0, (), 2,
    )[0]
    got_neg_g = to_owners(after(neg_grad, got_tg_g))
    y_a = after(y_a, neg_grad)
    states_a = [state_a, near(state_a), y_a, near(y_a)]

    send_in, back_c, *ch_one = kernel_call(
        functools.partial(back_first_kernel, (steps, batch, hidden, chunk, n_loc)),
        [shape((slots, gpad), BF16), shape((cslots, 2 * wide), BF16)]
        + [shape((events + 16, cpad), BF16)] * n_loc,
        [l_arr, keep, slot_in, land, init_two, after(into_first, neg_grad)] + res_one + w_one,
        1,
        [
            dq_scratch,
            pltpu.VMEM((events, gates), BF16),
            all_scratch,
            pltpu.VMEM((n_loc, 16, cpad), F32),
        ],
        16,
    )
    got_in_g = to_owners(after(send_in, got_neg_g, *ch_two[2:]))
    got_back = to_owners(after(back_c, got_in_g))
    ch_one = send_xor(ch_one, "loc")

    def all_sum(kept, sent):
        rest = kept.shape[0]
        for bit in range(bits):
            got = swap(sent, "grp", 1 << bit)
            if bit < bits - 2:
                rest //= 2
                kept, sent = kernel_call(
                    functools.partial(split_kernel, bit + 1),
                    [shape((rest, cpad), BF16)] * 2,
                    [g_arr, kept, got],
                    1,
                )
            else:
                kept = kernel_call(add_kernel, [shape((rest, cpad), BF16)], [kept, got])[0]
                sent = kept
        for bit in reversed(range(1, bits - 1)):
            kept = join(bit, kept, swap(kept, "grp", 1 << bit))
        return kept, swap(kept, "grp", 1)

    half_shape = shape((wide // 2, cpad), BF16)

    def dense(lefts, chunks, skip, at, bias_at, bias_row):
        parts = kernel_call(
            functools.partial(dense_kernel, (steps, batch, hidden, skip, at, bias_at, n_loc)),
            [half_shape] * 2,
            [g_arr] + lefts + chunks,
            1, [pltpu.VMEM((wide, cpad), BF16)], 6,
        )
        kept, got = all_sum(*parts)
        return kernel_call(
            functools.partial(final_kernel, hidden, bias_row),
            [shape((hidden, chunk), F32), shape((1, chunk), F32)],
            [g_arr, kept, got],
            1, (), 2,
        )

    grad_in, bias_in = dense(states_a, ch_two, True, 0, None, hidden)
    grad_two, _ = dense(states_b, ch_two, False, events, None, hidden)
    grad_one, bias_one = dense(states_a, ch_one, False, 0, bias_row, bias_row)

    own = rows // n_loc
    own_pad = -(-own // 16) * 16

    def table_sum(ids, grads, cols, *wait):
        across_cols = grads[0].shape[1]
        full = shape((own_pad, across_cols), F32)
        sent = shape((own_pad, across_cols), BF16)
        mine_p, far_p, near_p = kernel_call(
            functools.partial(table_kernel, own, len(ids)),
            [full, full, shape((2, own_pad, across_cols), BF16)],
            [l_arr] + [i.reshape(1, i.shape[0]) for i in ids] + grads,
            1, (), 4,
        )
        total, far_s = kernel_call(
            table_add_kernel, [full, sent], [after(mine_p, *wait), far_p, near(near_p)]
        )
        return kernel_call(table_out_kernel, [shape((own, cols), F32)], [total, across(far_s)])[0]

    table_in = table_sum([in_ids], [got_in_g], gates, got_back)
    neg_ids = jnp.broadcast_to(mine[None, :], (owners, neg_own)).reshape(neg_part)
    table_out = table_sum([tg_ids, neg_ids], [got_tg_g, got_neg_g], wide)
    grad_carried = kernel_call(
        carry_kernel, [shape((2, batch, hidden), F32)], [slot_pl, got_back]
    )[0]
    return (
        table_in,
        table_out[:, :hidden],
        table_out[:, hidden],
        grad_one,
        grad_in,
        grad_two,
        jnp.concatenate([bias_one, bias_in], axis=0),
        grad_carried,
    )


def solution(mesh):
    in_specs = (
        P(None, ("grp", "loc"), None),
        P(("grp", "loc")),
        P(None, ("grp", "loc")),
        P(None, ("grp", "loc")),
        P(None, ("grp", "loc")),
        P(("grp", "loc")),
        P(),
        P("grp", None),
        P("grp", None),
        P("grp"),
        P(None, "loc"),
        P(None, "loc"),
        P(None, "loc"),
        P(None, "loc"),
    )
    out_specs = (
        P(("grp", "loc"), None),
        P(("grp", "loc"), None),
        P(("grp", "loc")),
        P(None, "loc"),
        P(None, "loc"),
        P(None, "loc"),
        P(None, "loc"),
        P(None, ("grp", "loc"), None),
    )
    return jax.shard_map(
        on_device, mesh=mesh, in_specs=in_specs, out_specs=out_specs, check_vma=False
    )
```

```python
import functools

import jax
import jax.numpy as jnp
import numpy as np
from jax import lax
from jax.experimental import pallas as pl
from jax.experimental.pallas import tpu as pltpu
from jax.sharding import PartitionSpec as P

BPREG = 1.0
BF16 = jnp.bfloat16
F32 = jnp.float32
I32 = jnp.int32
LANES = 128
VMEM_LIMIT = 48 << 20


def swap(x, axis, bit):
    n = lax.axis_size(axis)
    return lax.ppermute(x, axis, [(i, i ^ bit) for i in range(n)])


def gather_xor(x, axis):
    blocks = {0: x}
    bit = lax.axis_size(axis) // 2
    while bit:
        for k in list(blocks):
            blocks[k | bit] = swap(blocks[k], axis, bit)
        bit //= 2
    return [blocks[k] for k in range(len(blocks))]


def send_xor(chunks, axis):
    return [chunks[0]] + [swap(chunks[j], axis, j) for j in range(1, len(chunks))]


def kernel_call(body, outs, ins, smem=0, scratch=(), us=1, left=0, left_outs=0):
    vmem, place = pl.BlockSpec(memory_space=pltpu.VMEM), pl.BlockSpec(memory_space=pl.ANY)
    nbytes = sum(a.size * a.dtype.itemsize for a in ins)
    nbytes += sum(int(functools.reduce(lambda a, b: a * b, o.shape)) * o.dtype.itemsize for o in outs)
    return pl.pallas_call(
        body,
        out_shape=outs,
        in_specs=[pl.BlockSpec(memory_space=pltpu.SMEM)] * smem
        + [vmem] * (len(ins) - smem - left)
        + [place] * left,
        out_specs=[vmem] * (len(outs) - left_outs) + [place] * left_outs,
        scratch_shapes=list(scratch),
        compiler_params=pltpu.CompilerParams(vmem_limit_bytes=VMEM_LIMIT),
        cost_estimate=pl.CostEstimate(flops=us * 10**9, bytes_accessed=nbytes, transcendentals=0),
    )(*ins)


def after(x, *deps):
    return lax.optimization_barrier((x,) + deps)[0]


def shape(dims, dtype):
    return jax.ShapeDtypeStruct(dims, dtype)


def iota(dims, dim):
    return lax.broadcasted_iota(I32, dims, dim)


def dot(a, b, ca=1, cb=0):
    return lax.dot_general(a, b, (((ca,), (cb,)), ((), ())), preferred_element_type=F32)


class Loader:
    def __init__(self, copies):
        self.copies = copies
        self.waited = set()
        for group in copies.values():
            for copy in group:
                copy.start()

    def ready(self, slot):
        if slot not in self.waited:
            self.waited.add(slot)
            for copy in self.copies[slot]:
                copy.wait()


class Weights(Loader):
    def __init__(self, refs, buf, sem, side=None):
        n = buf.shape[0]
        pieces = (len(refs) - n // 2) // (n // 2)
        copies, k = {}, 0
        for j in range(n):
            row, copies[j] = 0, []
            for _ in range(1 if j < n // 2 else pieces):
                size = refs[k].shape[0]
                at = row
                if side is not None and j >= n // 2:
                    at = pl.multiple_of((side if row == 0 else 1 - side) * size, size)
                part = buf.at[j, pl.ds(at, size), :]
                copies[j].append(pltpu.make_async_copy(refs[k], part, sem.at[k]))
                row, k = row + size, k + 1
        self.buf = buf
        super().__init__(copies)

    def __getitem__(self, j):
        self.ready(j)
        return self.buf[j]


def step_copies(ref, buf, sem, steps, batch, out):
    copies = {}
    for t in reversed(range(steps)):
        at = (slice(None), pl.ds(t * batch, batch), slice(None))
        pair = (buf.at[at], ref.at[at]) if out else (ref.at[at], buf.at[at])
        copies[t] = [pltpu.make_async_copy(*pair, sem.at[t])]
    return copies


def low(cond):
    return jnp.where(cond, 1.0, 0.0).astype(BF16)


def start_kernel(dims, in_ref, tg_ref, plan_ref, carried_ref, s_in, s_tg, s_pl, out_ref):
    owners, rows, cap, batch, ccap = dims
    hidden = carried_ref.shape[2]
    wide = out_ref.shape[1] // 2
    spare = wide - hidden

    def place(ids, span):
        n = ids.shape[0]
        owner_i = iota((n, owners), 1)
        member = (ids >= owner_i * span) & (ids < (owner_i + 1) * span)
        earlier = low(iota((n, n), 1) < iota((n, n), 0))
        before = dot(earlier, low(member))
        rank = jnp.sum(jnp.where(member, before, 0.0), axis=1, keepdims=True).astype(I32)
        owner = jnp.sum(jnp.where(member, owner_i, 0).astype(F32), axis=1, keepdims=True).astype(I32)
        return owner, rank

    def digits(owner, rank, first, value):
        n = owner.shape[0]
        turn = sum((rank >= k * ccap).astype(I32) for k in range(1, -(-cap // ccap)))
        row = owner * ccap + rank - turn * ccap
        hit = low(iota((n, owners * ccap), 1) == row)
        lane = iota((n, LANES), 1)
        high, rest = (value >> 8).astype(F32), (value & 255).astype(F32)
        at = first + 2 * turn
        code = jnp.where(lane == at, high, jnp.where(lane == at + 1, rest, 0.0))
        return dot(hit, code.astype(BF16), 0, 0)

    o_in, r_in = place(in_ref[...], rows)
    o_tg, r_tg = place(tg_ref[...], rows)
    o_pl, r_pl = place(plan_ref[...], batch)
    s_in[...] = o_in * cap + r_in
    s_tg[...] = o_tg * cap + r_tg
    s_pl[...] = o_pl * ccap + r_pl
    turns = -(-cap // ccap)
    code = digits(o_in, r_in, 0, in_ref[...] + 1)
    code += digits(o_tg, r_tg, 2 * turns, tg_ref[...] + 1)
    code += digits(o_pl, r_pl, 4 * turns, plan_ref[...] - o_pl * batch + 1)
    pick = low(iota((batch, owners * ccap), 1) == o_pl * ccap + r_pl)
    parts = [dot(pick, carried_ref[k].astype(BF16), 0, 0) for k in range(2)]
    parts = [parts[0], code[:, :spare], parts[1], jnp.zeros((owners * ccap, spare), F32)]
    out_ref[...] = jnp.concatenate(parts, axis=1).astype(BF16)


def decode(got_ref, row_ref, turn_ref, hidden, first):
    wide = got_ref.shape[1] // 2
    block = got_ref[:, wide - LANES : wide]
    n = row_ref.shape[0]
    found = dot(low(iota((n, block.shape[0]), 1) == row_ref[...]), block)
    at = hidden - wide + LANES + first + 2 * turn_ref[...]
    lane = iota((n, LANES), 1)
    worth = jnp.where(lane == at, 256.0, jnp.where(lane == at + 1, 1.0, 0.0))
    return jnp.sum(found * worth, axis=1, keepdims=True).astype(I32)


def landing(land_ref, got_ref, layer, batch, hidden):
    wide = got_ref.shape[1] // 2
    land = low(iota((land_ref.shape[0], batch), 1) == land_ref[...])
    moved = dot(land, got_ref[:, layer * wide : (layer + 1) * wide], 0, 0)
    return jnp.where(iota(moved.shape, 1) < hidden, moved, 0.0)


def extend(value, keep, hidden):
    lane = iota(value.shape, 1)
    return jnp.where(lane == hidden, 1.0, jnp.where(lane == hidden + 1, keep, value)).astype(BF16)


def run_steps(steps, batch, hidden, l, keep_ref, weights, x_of, start, state_ref, res, q_s):
    res_ref, res_s, res_sem = res
    n_loc = q_s.shape[0]
    wide = start.shape[1]
    tail = jnp.zeros((batch, wide), F32)
    lane = iota((batch, wide), 1)
    prev = start
    writes = step_copies(res_ref, res_s, res_sem, steps, batch, True)
    for t in range(steps):
        at = pl.ds(t * batch, batch)
        keep = keep_ref[at, :]
        state_ref[at, :] = extend(prev, keep, hidden)
        p = prev * keep
        p_low = p.astype(BF16)
        for j in range(n_loc):
            q_s[l ^ j] = dot(p_low, weights[j])[:, : q_s.shape[2]]
        q = jnp.concatenate([q_s[i] for i in range(n_loc)] + [tail], axis=1)
        x = x_of(t)
        h2 = 2 * hidden
        z = jax.nn.sigmoid(x[:, :wide] + q[:, :wide])
        r = jax.nn.sigmoid(x[:, hidden : hidden + wide] + q[:, hidden : hidden + wide])
        qn = q[:, h2 : h2 + wide]
        n = jnp.tanh(x[:, h2 : h2 + wide] + r * qn)
        prev = jnp.where(lane < hidden, n + z * (p - n), 0.0)
        for k, val in enumerate((z, r, n, qn, p)):
            res_s[k, at, :] = val
        writes[t][0].start()
    state_ref[pl.ds(steps * batch, batch), :] = extend(prev, 0.0, hidden)
    for t in range(steps):
        writes[t][0].wait()


def pad_kernel(at, n_in, l_ref, w_ref, *refs):
    refs, outs = refs[: n_in - 2], refs[n_in - 2 :]
    out_ref = outs[0]
    rows, cols = w_ref.shape
    out_ref[...] = jnp.zeros(out_ref.shape, BF16)
    out_ref[:rows, :cols] = w_ref[...]
    if at is not None:
        which, row = at
        tile = row // 16 * 16
        here = (iota((16, cols), 0) == row - tile).astype(F32)
        old = out_ref[tile : tile + 16, :cols].astype(F32)
        extra = refs[0][which : which + 1, :].astype(F32)
        out_ref[tile : tile + 16, :cols] = (old + here * extra).astype(BF16)
    if len(outs) == 2:
        half = outs[1].shape[0]
        side = l_ref[1] & 1
        outs[1][...] = out_ref[pl.ds(pl.multiple_of(side * half, half), half), :]
    else:
        first = outs[1].shape[0]
        outs[1][...] = out_ref[:first, :]
        outs[2][...] = out_ref[first:, :]


def gather_in_kernel(dims, base_ref, got_ref, row_ref, turn_ref, table_ref, out_ref, ids_ref, land_ref):
    hidden, turns = dims
    rows, cols = table_ref.shape
    wide = got_ref.shape[1] // 2
    ids = decode(got_ref, row_ref, turn_ref, hidden, 0) - 1 - base_ref[0]
    ids_ref[...] = ids
    at = hidden - wide + LANES + 4 * turns + 1
    land = got_ref[:, wide - LANES : wide].astype(F32)[:, at : at + 1]
    land_ref[...] = land.astype(I32) - 1
    pick = low(iota((ids.shape[0], rows), 1) == ids)
    if out_ref.shape[1] > cols:
        out_ref[...] = jnp.zeros(out_ref.shape, BF16)
    out_ref[:, :cols] = dot(pick, table_ref[...]).astype(BF16)


def biased_rows(ids, table_ref, bias_ref, wide):
    n = ids.shape[0]
    rows, cols = table_ref.shape
    pick = low(iota((n, rows), 1) == ids)
    parts = [dot(pick, table_ref[...]), dot(pick, bias_ref[...])[:, :1]]
    parts.append(jnp.zeros((n, wide - cols - 1), F32))
    return jnp.concatenate(parts, axis=1).astype(BF16)


def gather_tg_kernel(dims, base_ref, got_ref, row_ref, turn_ref, table_ref, bias_ref, out_ref, ids_ref):
    hidden, turns = dims
    ids = decode(got_ref, row_ref, turn_ref, hidden, 2 * turns) - 1 - base_ref[0]
    ids_ref[...] = ids
    out_ref[...] = biased_rows(ids, table_ref, bias_ref, out_ref.shape[1])


def gather_neg_kernel(ids_ref, table_ref, bias_ref, out_ref):
    out_ref[...] = biased_rows(ids_ref[...], table_ref, bias_ref, out_ref.shape[1])


def table_kernel(own, pairs, l_ref, *refs):
    mine_ref, far_ref, near_ref = refs[2 * pairs :]
    pad = mine_ref.shape[0]
    l = l_ref[0]
    for j, (ref, at) in enumerate(((mine_ref, None), (near_ref, 0), (far_ref, None), (near_ref, 1))):
        part = None
        for ids_ref, got_ref in zip(refs[:pairs], refs[pairs : 2 * pairs]):
            row = iota((pad, ids_ref.shape[1]), 0)
            hit = (row < own) & (row + (l ^ j) * own == ids_ref[...])
            term = dot(low(hit), got_ref[...])
            part = term if part is None else part + term
        if at is None:
            ref[...] = part
        else:
            ref[at, :, :] = part.astype(BF16)


def table_add_kernel(mine_ref, far_ref, got_ref, sum_ref, send_ref):
    sum_ref[...] = mine_ref[...] + got_ref[0].astype(F32)
    send_ref[...] = (far_ref[...] + got_ref[1].astype(F32)).astype(BF16)


def table_out_kernel(sum_ref, got_ref, out_ref):
    rows, cols = out_ref.shape
    out_ref[...] = (sum_ref[...] + got_ref[...].astype(F32))[:rows, :cols]


def carry_kernel(slot_ref, got_ref, out_ref):
    hidden = out_ref.shape[2]
    wide = got_ref.shape[1] // 2
    pick = low(iota((slot_ref.shape[0], got_ref.shape[0]), 1) == slot_ref[...])
    back = dot(pick, got_ref[...])
    out_ref[0] = back[:, :hidden]
    out_ref[1] = back[:, wide : wide + hidden]


def split_kernel(bit, l_ref, a_ref, b_ref, keep_ref, send_ref):
    half = keep_ref.shape[0]
    side = (l_ref[0] >> bit) & 1
    for ref, at in ((keep_ref, side), (send_ref, 1 - side)):
        rows = pl.ds(pl.multiple_of(at * half, half), half)
        ref[...] = (a_ref[rows, :].astype(F32) + b_ref[rows, :].astype(F32)).astype(BF16)


def add_kernel(a_ref, b_ref, out_ref):
    out_ref[...] = (a_ref[...].astype(F32) + b_ref[...].astype(F32)).astype(BF16)


def join_kernel(bit, l_ref, a_ref, b_ref, out_ref):
    half = a_ref.shape[0]
    side = (l_ref[0] >> bit) & 1
    for ref, at in ((a_ref, side), (b_ref, 1 - side)):
        out_ref[pl.ds(pl.multiple_of(at * half, half), half), :] = ref[...]


def final_kernel(hidden, bias_row, l_ref, a_ref, b_ref, out_ref, bias_ref):
    side = l_ref[0] & 1
    cols = out_ref.shape[1]
    half = a_ref.shape[0]
    at = (bias_row - half) // 16 * 16
    for first, second, when in ((a_ref, b_ref, 0), (b_ref, a_ref, 1)):

        @pl.when(side == when)
        def _():
            out_ref[:half, :] = first[...].astype(F32)[:, :cols]
            out_ref[half:, :] = second[...].astype(F32)[: hidden - half, :cols]
            row = bias_row - half - at
            bias_ref[...] = second[at : at + 16, :].astype(F32)[row : row + 1, :cols]


def first_kernel(dims, n_w, l_ref, keep_ref, slot_ref, land_ref, got_ref, rows_ref, *refs):
    steps, batch, hidden, bias_row, n_loc = dims
    w_refs, refs = refs[:n_w], refs[n_w:]
    state_ref, res_ref, w_buf, w_sem, res_s, res_sem, q_s, b_s, x_s = refs
    wide = res_s.shape[2]
    l = l_ref[0]
    weights = Weights(w_refs, w_buf, w_sem)
    pick = low(iota((steps * batch, rows_ref.shape[0]), 1) == slot_ref[...])
    x_s[...] = dot(pick, rows_ref[...])
    moved = landing(land_ref, got_ref, 0, batch, hidden)
    for j in range(n_loc):
        weights.ready(j)
        b_s[l ^ j] = w_buf[j, bias_row : bias_row + 16, :].astype(F32)[:, : b_s.shape[2]]
    bias = jnp.concatenate([b_s[i][0:1, :] for i in range(n_loc)], axis=1)
    pad = jnp.zeros((batch, wide), F32)

    def x_of(t):
        gates = bias.shape[1]
        return jnp.concatenate([x_s[pl.ds(t * batch, batch), :][:, :gates] + bias, pad], axis=1)

    run_steps(
        steps, batch, hidden, l, keep_ref, weights, x_of, moved, state_ref,
        (res_ref, res_s, res_sem), q_s,
    )


def second_kernel(dims, n_in, n_w, l_ref, keep_ref, land_ref, got_ref, below_ref, *refs):
    steps, batch, hidden, n_loc = dims
    in_refs, w_refs, refs = refs[:n_in], refs[n_in : n_in + n_w], refs[n_in + n_w :]
    state_ref, res_ref, in_buf, in_sem, w_buf, w_sem, res_s, res_sem, q_s, x_s = refs
    wide = res_s.shape[2]
    l = l_ref[0]
    inputs = Weights(in_refs, in_buf, in_sem, l_ref[1] & 1)
    weights = Weights(w_refs, w_buf, w_sem, l_ref[1] & 1)
    moved = landing(land_ref, got_ref, 1, batch, hidden)
    below = below_ref[pl.ds(batch, steps * batch), :]
    for j in range(n_loc):
        x_s[l ^ j] = dot(below, inputs[j])[:, : x_s.shape[2]]
    pad = jnp.zeros((batch, wide), F32)

    def x_of(t):
        return jnp.concatenate(
            [x_s[i][t * batch : (t + 1) * batch, :] for i in range(n_loc)] + [pad], axis=1
        )

    run_steps(
        steps, batch, hidden, l, keep_ref, weights, x_of, moved, state_ref,
        (res_ref, res_s, res_sem), q_s,
    )


def score_kernel(dims, valid_ref, slot_ref, state_ref, tg_ref, *refs):
    steps, batch, n_loc = dims
    rows = steps * batch
    neg_refs, refs = refs[:n_loc], refs[n_loc:]
    gn_refs, into_ref, send_ref = refs[:n_loc], refs[n_loc], refs[n_loc + 1]
    sn_s, tgt_s, tgg_s, neg_buf, neg_sem = refs[n_loc + 2 :]
    negs = Loader(
        {
            j: [pltpu.make_async_copy(neg_refs[j], neg_buf.at[j], neg_sem.at[j])]
            for j in range(n_loc)
        }
    )
    diag = iota((batch, batch), 0) == iota((batch, batch), 1)
    slots = tg_ref.shape[0]
    pick = low(iota((rows, slots), 1) == slot_ref[...])
    tgt_s[...] = dot(pick, tg_ref[...]).astype(BF16)
    every = state_ref[pl.ds(batch, rows), :]
    for j in range(n_loc):
        negs.ready(j)
        sn_s[j] = dot(every, neg_buf[j], 1, 1)
    for t in range(steps):
        at = pl.ds(t * batch, batch)
        second = state_ref[pl.ds((t + 1) * batch, batch), :]
        targets = tgt_s[at, :]
        st = dot(second, targets, 1, 1)
        sn = [sn_s[j, at, :] for j in range(n_loc)]
        pos = jnp.sum(jnp.where(diag, st, 0.0), axis=1, keepdims=True)
        top = jnp.max(jnp.where(diag, -jnp.inf, st), axis=1, keepdims=True)
        for s in sn:
            top = jnp.maximum(top, jnp.max(s, axis=1, keepdims=True))
        parts = [(st, jnp.where(diag, 0.0, jnp.exp(st - top)))]
        parts += [(s, jnp.exp(s - top)) for s in sn]
        mass = sum(jnp.sum(e, axis=1, keepdims=True) for _, e in parts)
        scale = 1.0 / mass
        parts = [(s, e * scale, jax.nn.sigmoid(pos - s)) for s, e in parts]
        inside = sum(jnp.sum(w * g, axis=1, keepdims=True) for _, w, g in parts)
        penalty = sum(jnp.sum(w * s * s, axis=1, keepdims=True) for s, w, _ in parts)
        slope = sum(jnp.sum(w * g * (1.0 - g), axis=1, keepdims=True) for _, w, g in parts)
        inv = 1.0 / inside
        weight = valid_ref[at, :]
        grads = [
            weight * w * (1.0 + BPREG * (s * s + 2.0 * s - penalty) - g * g * inv)
            for s, w, g in parts
        ]
        gt = grads[0] - jnp.where(diag, weight * slope * inv, 0.0)
        gt_low = gt.astype(BF16)
        into_ref[at, :] = dot(gt_low, targets)
        for j in range(n_loc):
            gn_refs[j][at, :] = grads[j + 1].astype(BF16)
        tgg_s[at, :] = dot(gt_low, second, 0, 0).astype(BF16)
    total = into_ref[...]
    for j in range(n_loc):
        total += dot(gn_refs[j][...], neg_buf[j])
    into_ref[...] = total
    send_ref[...] = dot(pick, tgg_s[...], 0, 0).astype(BF16)


def back_steps(steps, batch, hidden, chunk, l, keep_ref, weights, into_ref, res, dq_s, emit):
    loader, res_s = res
    n_loc = dq_s.shape[0]
    dq_s[...] = jnp.zeros(dq_s.shape, F32)
    wide = into_ref.shape[1]
    lane = iota((batch, wide), 1)
    carry = jnp.zeros((batch, wide), F32)
    for t in reversed(range(steps)):
        at = pl.ds(t * batch, batch)
        g = jnp.where(lane < hidden, into_ref[at, :] + carry, 0.0)
        loader.ready(t)
        z, r, n, qn, p = (res_s[k, at, :] for k in range(5))
        dc = g * (1.0 - z) * (1.0 - n * n)
        da_z = (g * (p - n) * z * (1.0 - z))[:, :hidden]
        da_r = (dc * qn * r * (1.0 - r))[:, :hidden]
        da_n = dc[:, :hidden]
        dq_n = (dc * r)[:, :hidden]
        da = jnp.concatenate([da_z, da_r, da_n], axis=1)
        dq = jnp.concatenate([da_z, da_r, dq_n], axis=1)
        emit(t, da, dq)
        for i in range(n_loc):
            dq_s[i, :, :chunk] = dq[:, i * chunk : (i + 1) * chunk]
        dp = g * z
        for j in range(n_loc):
            dp += dot(dq_s[l ^ j].astype(BF16), weights[j], 1, 1)
        carry = dp * keep_ref[at, :]
    return jnp.where(lane < hidden, carry, 0.0)


def back_second_kernel(dims, n_in, n_w, l_ref, keep_ref, into_ref, *refs):
    steps, batch, hidden, chunk, n_loc = dims
    res_ref, refs = refs[0], refs[1:]
    in_refs, w_refs, refs = refs[:n_in], refs[n_in : n_in + n_w], refs[n_in + n_w :]
    init_ref, first_ref, refs = refs[0], refs[1], refs[2:]
    ch_refs, refs = refs[: 2 * n_loc], refs[2 * n_loc :]
    dq_s, da_all, dq_all, in_buf, in_sem, w_buf, w_sem, res_s, res_sem = refs
    l = l_ref[0]
    loader = Loader(step_copies(res_ref, res_s, res_sem, steps, batch, False))
    weights = Weights(w_refs, w_buf, w_sem, l_ref[1] & 1)
    inputs = Weights(in_refs, in_buf, in_sem, l_ref[1] & 1)
    da_all[...] = jnp.zeros(da_all.shape, F32)
    dq_all[...] = jnp.zeros(dq_all.shape, F32)

    def emit(t, da, dq):
        for i in range(n_loc):
            da_all[i, pl.ds(t * batch, batch), :chunk] = da[:, i * chunk : (i + 1) * chunk]
            dq_all[i, pl.ds(t * batch, batch), :chunk] = dq[:, i * chunk : (i + 1) * chunk]

    init_ref[...] = back_steps(
        steps, batch, hidden, chunk, l, keep_ref, weights, into_ref, (loader, res_s), dq_s, emit
    )
    rows = steps * batch
    total = None
    for j in range(n_loc):
        da_low = da_all[l ^ j].astype(BF16)
        ch_refs[j][...] = da_low
        ch_refs[n_loc + j][...] = dq_all[l ^ j].astype(BF16)
        part = dot(da_low, inputs[j], 1, 1)
        total = part if total is None else total + part
    first_ref[...] = total


def back_first_kernel(dims, n_w, l_ref, keep_ref, into_ref, *refs):
    steps, batch, hidden, chunk, n_loc = dims
    res_ref, refs = refs[0], refs[1:]
    w_refs, refs = refs[:n_w], refs[n_w:]
    init_ref, da_all, refs = refs[0], refs[1], refs[2:]
    ch_refs, refs = refs[:n_loc], refs[n_loc:]
    dq_s, dq_all, bias_s, w_buf, w_sem, res_s, res_sem = refs
    l = l_ref[0]
    loader = Loader(step_copies(res_ref, res_s, res_sem, steps, batch, False))
    weights = Weights(w_refs, w_buf, w_sem)
    dq_all[...] = jnp.zeros(dq_all.shape, F32)
    bias_s[...] = jnp.zeros(bias_s.shape, F32)

    def emit(t, da, dq):
        da_all[pl.ds(t * batch, batch), :] = da.astype(BF16)
        for i in range(n_loc):
            dq_all[i, pl.ds(t * batch, batch), :chunk] = dq[:, i * chunk : (i + 1) * chunk]

    init_ref[...] = back_steps(
        steps, batch, hidden, chunk, l, keep_ref, weights, into_ref, (loader, res_s), dq_s, emit
    )
    rows = steps * batch
    bias = jnp.sum(da_all[...].astype(F32), axis=0, keepdims=True)
    for i in range(n_loc):
        bias_s[i, 0:1, :chunk] = bias[:, i * chunk : (i + 1) * chunk]
    for j in range(n_loc):
        ch_refs[j][pl.ds(0, rows), :] = dq_all[l ^ j].astype(BF16)
        ch_refs[j][pl.ds(rows, 16), :] = bias_s[l ^ j].astype(BF16)


def return_kernel(slot_ref, land_ref, da_ref, init_ref, init2_ref, send_ref, back_ref):
    rows, cols = da_ref.shape
    wide = init_ref.shape[1]
    pick = low(iota((rows, send_ref.shape[0]), 1) == slot_ref[...])
    sent = dot(pick, da_ref[...], 0, 0).astype(BF16)
    send_ref[:, :cols] = sent
    if send_ref.shape[1] > cols:
        rest = send_ref.shape[1] - cols
        send_ref[:, cols:] = jnp.zeros((send_ref.shape[0], rest), BF16)
    land = low(iota((land_ref.shape[0], init_ref.shape[0]), 1) == land_ref[...])
    back_ref[:, :wide] = dot(land, init_ref[...].astype(BF16)).astype(BF16)
    back_ref[:, wide:] = dot(land, init2_ref[...].astype(BF16)).astype(BF16)


def scaled(ref, rows, hidden):
    left = ref[pl.ds(0, rows), :].astype(F32)
    return (left * left[:, hidden + 1 : hidden + 2]).astype(BF16)


def dense_kernel(dims, l_ref, *refs):
    steps, batch, hidden, skip, bias_row, n_loc = dims
    rows = steps * batch
    left_refs, ch_refs = refs[:n_loc], refs[n_loc : 2 * n_loc]
    keep_ref, send_ref, all_s = refs[2 * n_loc :]
    half = keep_ref.shape[0]
    side = l_ref[0] & 1
    total, bias = None, None
    for j in range(n_loc):
        left = left_refs[j][pl.ds(batch, rows), :] if skip else scaled(left_refs[j], rows, hidden)
        part = dot(left, ch_refs[j][pl.ds(0, rows), :], 0, 0)
        total = part if total is None else total + part
        if bias_row is not None:
            extra = ch_refs[j][pl.ds(rows, 16), :].astype(F32)
            bias = extra if bias is None else bias + extra
    all_s[...] = total.astype(BF16)
    if bias_row is not None:
        all_s[pl.ds(bias_row, 16), :] = bias.astype(BF16)
    keep_ref[...] = all_s[pl.ds(pl.multiple_of(side * half, half), half), :]
    send_ref[...] = all_s[pl.ds(pl.multiple_of((1 - side) * half, half), half), :]


def neg_kernel(n_loc, owners, *refs):
    gn_refs, b_refs, out_ref = refs[:n_loc], refs[n_loc : 2 * n_loc], refs[2 * n_loc]
    rows = gn_refs[0].shape[0]
    batch = b_refs[0].shape[0] - rows
    total = None
    for j in range(n_loc):
        part = dot(gn_refs[j][...], b_refs[j][pl.ds(batch, rows), :], 0, 0)
        total = part if total is None else total + part
    own = out_ref.shape[0] // owners
    places = [(g >> 1) + (g & 1) * (owners // 2) for g in range(owners)]
    blocks = [total[p * own : (p + 1) * own, :] for p in places]
    out_ref[...] = jnp.concatenate(blocks, axis=0).astype(BF16)


def on_device(
    carried,
    session_plan,
    item_ids,
    target_ids,
    reset_mask,
    valid_counts,
    negative_ids,
    input_table,
    output_table,
    output_bias,
    hidden_one,
    input_two,
    hidden_two,
    gate_biases,
):
    hidden = carried.shape[2]
    wide = -(-(hidden + 2) // LANES) * LANES
    bias_row = wide - 16
    steps, batch = item_ids.shape
    events = steps * batch
    owners = lax.axis_size("grp")
    n_loc = lax.axis_size("loc")
    grp = lax.axis_index("grp")
    loc = lax.axis_index("loc")
    rows = input_table.shape[0]
    base = grp * rows
    gates = input_table.shape[1]
    chunk = gates // n_loc
    cap = events // owners + events // (2 * owners)
    ccap = 4 * batch // owners
    slots, cslots = owners * cap, owners * ccap
    neg_own = negative_ids.shape[0] // owners // n_loc
    neg_part = owners * neg_own
    l_arr = jnp.stack([loc, grp]).astype(I32)

    cpad = -(-chunk // LANES) * LANES
    gpad = -(-gates // LANES) * LANES
    w_shape = shape((wide, cpad), BF16)

    g_arr = grp.astype(I32).reshape(1)
    bits = owners.bit_length() - 1

    def padded(w, at, first):
        ins = [l_arr, w] if at is None else [l_arr, w, gate_biases]
        outs = [w_shape, shape((first, cpad), BF16)]
        if 2 * first < wide:
            outs.append(shape((wide - first, cpad), BF16))
        return kernel_call(functools.partial(pad_kernel, at, len(ins)), outs, ins, 1)

    def near(x):
        return swap(x, "loc", 1)

    def across(x):
        return swap(x, "loc", 2)

    def join(bit, kept, got, index=g_arr):
        return kernel_call(
            functools.partial(join_kernel, bit),
            [shape((2 * kept.shape[0],) + kept.shape[1:], BF16)],
            [index, kept, got], 1,
        )[0]

    p_one, *one_pieces = padded(hidden_one, (0, bias_row), wide // 8)
    y_one = [across(one_pieces[0])]
    y_one.append(across(after(one_pieces[1], y_one[0])))

    slot_in, slot_tg, slot_pl, packed = kernel_call(
        functools.partial(start_kernel, (owners, rows, cap, batch, ccap)),
        [
            shape((events, 1), I32),
            shape((events, 1), I32),
            shape((batch, 1), I32),
            shape((cslots, 2 * wide), BF16),
        ],
        [
            after(item_ids, p_one).reshape(events, 1),
            target_ids.reshape(events, 1),
            session_plan.reshape(batch, 1),
            carried,
        ],
        0, (), 3,
    )

    def to_owners(x):
        got = lax.all_to_all(
            x.reshape((owners, x.shape[0] // owners) + x.shape[1:]),
            "grp", split_axis=0, concat_axis=0, tiled=True,
        )
        return got.reshape(x.shape)

    got_c = to_owners(after(packed, y_one[0]))

    bias_col = output_bias[:, None]
    mine = lax.dynamic_slice(
        negative_ids.reshape(owners, n_loc, neg_own), (grp, loc, 0), (1, 1, neg_own)
    ).reshape(neg_own) - base
    negs_own = kernel_call(
        gather_neg_kernel,
        [shape((neg_own, wide), BF16)],
        [after(mine, p_one).reshape(neg_own, 1), output_table, bias_col],
    )[0]
    negs_half = negs_own
    for bit in range(1, bits):
        negs_half = join(bit, negs_half, swap(negs_half, "grp", 1 << bit))
    negs = join(0, negs_half, swap(negs_half, "grp", 1))

    place = np.arange(slots)
    turns = -(-cap // ccap)
    place_row = jnp.asarray((place // cap * ccap + place % cap % ccap)[:, None], I32)
    place_turn = jnp.asarray((place % cap // ccap)[:, None], I32)
    base_arr = base.astype(I32).reshape(1)
    ids_shape = shape((slots, 1), I32)
    reply_in, in_ids, land = kernel_call(
        functools.partial(gather_in_kernel, (hidden, turns)),
        [shape((slots, gpad), BF16), ids_shape, shape((cslots, 1), I32)],
        [base_arr, got_c, place_row, place_turn, input_table],
        1, (), 4,
    )
    p_in, h_in = padded(input_two, (1, hidden), wide // 2)
    p_two, h_two = padded(hidden_two, None, wide // 2)
    y_in = across(after(h_in, y_one[1]))
    got_rows = to_owners(after(reply_in, negs_half, y_one[1]))
    y_two = across(after(h_two, y_in))
    y_in = [y_in, swap(y_in, "grp", 1)]
    y_neg = across(after(negs, y_two))
    y_two = [y_two, swap(y_two, "grp", 1)]
    reply_tg, tg_ids = kernel_call(
        functools.partial(gather_tg_kernel, (hidden, turns)),
        [shape((slots, wide), BF16), ids_shape],
        [base_arr, got_c, place_row, place_turn, output_table, bias_col],
        1, (), 3,
    )
    tg_rows = to_owners(after(reply_tg, got_rows))

    def four(own, pieces):
        return [own, near(own), *pieces, *(near(p) for p in pieces)]

    w_one = four(p_one, y_one)

    keep = (1 - reset_mask).astype(F32).reshape(events, 1)
    valid = (jnp.arange(steps, dtype=I32)[:, None] < valid_counts[None, :]).astype(F32)
    valid = (valid / steps).reshape(events, 1)

    res_shape = shape((5, events, wide), F32)
    n_w = 2 + n_loc
    w_scratch = [pltpu.VMEM((n_loc, wide, cpad), BF16), pltpu.SemaphoreType.DMA((n_w,))]
    res_scratch = [pltpu.VMEM((5, events, wide), F32), pltpu.SemaphoreType.DMA((steps,))]
    state_shape = shape(((steps + 1) * batch, wide), BF16)
    q_scratch = pltpu.VMEM((n_loc, batch, chunk), F32)
    dq_scratch = pltpu.VMEM((n_loc, batch, cpad), F32)
    x_scratch = pltpu.VMEM((n_loc, events, chunk), F32)
    all_scratch = pltpu.VMEM((n_loc, events, cpad), F32)

    state_a, res_one = kernel_call(
        functools.partial(first_kernel, (steps, batch, hidden, bias_row, n_loc), n_w),
        [state_shape, res_shape],
        [l_arr, keep, slot_in, land, got_c, after(got_rows, reply_tg, negs, y_two[0], y_in[1])] + w_one,
        1,
        w_scratch
        + res_scratch
        + [q_scratch, pltpu.VMEM((n_loc, 16, chunk), F32), pltpu.VMEM((events, gpad), F32)],
        12, n_w, 1,
    )
    w_in = four(p_in, [after(y, state_a) for y in y_in])
    w_two = four(p_two, [after(y, state_a) for y in y_two])
    state_b, res_two = kernel_call(
        functools.partial(second_kernel, (steps, batch, hidden, n_loc), n_w, n_w),
        [state_shape, res_shape],
        [l_arr, keep, land, got_c, after(state_a, y_neg)] + w_in + w_two,
        1,
        w_scratch + w_scratch + res_scratch + [q_scratch, x_scratch],
        15, 2 * n_w, 1,
    )
    y_b = across(after(state_b, y_neg))

    y_neg = after(y_neg, state_b)
    negs = [negs, near(negs), y_neg, near(y_neg)]
    *g_neg, into_second, send_tg = kernel_call(
        functools.partial(score_kernel, (steps, batch, n_loc)),
        [shape((events, neg_part), BF16)] * n_loc
        + [shape((events, wide), F32), shape((slots, wide), BF16)],
        [valid, slot_tg, state_b, tg_rows] + negs,
        0,
        [
            pltpu.VMEM((n_loc, events, neg_part), F32),
            pltpu.VMEM((events, wide), BF16),
            pltpu.VMEM((events, wide), BF16),
            pltpu.VMEM((n_loc, neg_part, wide), BF16),
            pltpu.SemaphoreType.DMA((n_loc,)),
        ],
        12, n_loc,
    )
    init_two, into_first, *ch_two = kernel_call(
        functools.partial(back_second_kernel, (steps, batch, hidden, chunk, n_loc), n_w, n_w),
        [shape((batch, wide), F32), shape((events, wide), F32)]
        + [shape((events, cpad), BF16)] * (2 * n_loc),
        [l_arr, keep, after(into_second, y_b), res_two] + w_in + w_two,
        1,
        [dq_scratch, all_scratch, all_scratch] + w_scratch + w_scratch + res_scratch,
        17, 2 * n_w + 1,
    )
    def send_after(chunks, *deps):
        return send_xor([after(c, *deps) for c in chunks], "loc")

    ch_in, ch_two = send_xor(ch_two[:n_loc], "loc"), send_xor(ch_two[n_loc:], "loc")
    y_a = across(after(state_a, into_second))
    got_tg_g = to_owners(send_tg)
    init_one, da_one, *ch_one = kernel_call(
        functools.partial(back_first_kernel, (steps, batch, hidden, chunk, n_loc), n_w),
        [shape((batch, wide), F32), shape((events, gates), BF16)]
        + [shape((events + 16, cpad), BF16)] * n_loc,
        [l_arr, keep, after(into_first, y_a), res_one] + w_one,
        1,
        [dq_scratch, all_scratch, pltpu.VMEM((n_loc, 16, cpad), F32)] + w_scratch + res_scratch,
        13, n_w + 1,
    )
    send_in, back_c = kernel_call(
        return_kernel,
        [shape((slots, gpad), BF16), shape((cslots, 2 * wide), BF16)],
        [slot_in, land, after(da_one, *ch_in[2:]), init_one, init_two],
        0, (), 3,
    )
    got_in_g = to_owners(after(send_in, got_tg_g))
    ch_one = send_xor(ch_one, "loc")
    g_neg = send_after(g_neg, *ch_one[2:])

    y_a, y_b = after(y_a, send_in), after(y_b, send_in)
    states_a = [state_a, near(state_a), y_a, near(y_a)]
    states_b = [state_b, near(state_b), y_b, near(y_b)]

    neg_grad = kernel_call(
        functools.partial(neg_kernel, n_loc, owners),
        [shape((neg_part, wide), BF16)],
        g_neg + states_b,
        0, (), 2,
    )[0]

    def all_sums(makers, waits):
        def one(make):
            kept, sent = make()
            rest = kept.shape[0]
            for bit in range(bits):
                got = yield sent, 1 << bit
                if bit < bits - 2:
                    rest //= 2
                    kept, sent = kernel_call(
                        functools.partial(split_kernel, bit + 1),
                        [shape((rest, cpad), BF16)] * 2,
                        [g_arr, kept, got],
                        1,
                    )
                else:
                    kept = kernel_call(add_kernel, [shape((rest, cpad), BF16)], [kept, got])[0]
                    sent = kept
            for bit in reversed(range(1, bits - 1)):
                kept = join(bit, kept, (yield kept, 1 << bit))
            got = yield kept, 1
            return kept, got

        chains = [one(make) for make in makers]
        results, asks, before, step = [None] * len(chains), {}, (), 0
        while None in results:
            if step < len(chains):
                asks[step] = next(chains[step])
            wait = tuple(before) + tuple(waits.get(step, lambda: ())())
            answers = {
                k: swap(after(ask[0], *wait) if wait else ask[0], "grp", ask[1])
                for k, ask in asks.items()
            }
            asks, before = {}, list(answers.values())
            for k, answer in answers.items():
                try:
                    asks[k] = chains[k].send(answer)
                except StopIteration as done:
                    results[k] = done.value
            step += 1
        return results

    half_shape = shape((wide // 2, cpad), BF16)

    def product(lefts, chunks, skip, bias_at):
        return kernel_call(
            functools.partial(dense_kernel, (steps, batch, hidden, skip, bias_at, n_loc)),
            [half_shape] * 2,
            [g_arr] + lefts + chunks,
            1, [pltpu.VMEM((wide, cpad), BF16)], 5,
        )

    def finish(parts, bias_row):
        return kernel_call(
            functools.partial(final_kernel, hidden, bias_row),
            [shape((hidden, chunk), F32), shape((1, chunk), F32)],
            [g_arr, *parts],
            1, (), 2,
        )

    sums = {}

    def made(name, *args):
        def make():
            sums[name] = product(*args)
            return sums[name]

        return make

    def start_back():
        sums["back"] = to_owners(after(back_c, got_in_g, sums["one"][0]))
        return ()

    def bring_back():
        return (sums["back"],)

    in_parts, two_parts, one_parts = all_sums(
        [
            made("in", states_a, ch_in, True, None),
            made("two", states_b, ch_two, False, None),
            made("one", states_a, ch_one, False, bias_row),
        ],
        {1: lambda: tuple(ch_one[2:]), 2: start_back, 3: lambda: (got_in_g,), 5: bring_back},
    )
    got_back = sums["back"]
    got_neg_g = to_owners(after(neg_grad, got_back))
    grad_in, bias_in = finish(in_parts, hidden)
    grad_two, _ = finish(two_parts, hidden)
    grad_one, bias_one = finish(one_parts, bias_row)

    own = rows // n_loc
    own_pad = -(-own // 16) * 16

    def table_sum(ids, grads, cols, *wait):
        across_cols = grads[0].shape[1]
        full = shape((own_pad, across_cols), F32)
        sent = shape((own_pad, across_cols), BF16)
        mine_p, far_p, near_p = kernel_call(
            functools.partial(table_kernel, own, len(ids)),
            [full, full, shape((2, own_pad, across_cols), BF16)],
            [l_arr] + [i.reshape(1, i.size) for i in ids] + grads,
            1, (), 4,
        )
        total, far_s = kernel_call(
            table_add_kernel, [full, sent], [after(mine_p, *wait), far_p, near(near_p)]
        )
        return kernel_call(table_out_kernel, [shape((own, cols), F32)], [total, across(far_s)])[0]

    table_in = table_sum([in_ids], [got_in_g], gates, got_back)
    neg_ids = jnp.broadcast_to(mine[None, :], (owners, neg_own)).reshape(neg_part)
    table_out = table_sum([tg_ids, neg_ids], [got_tg_g, got_neg_g], wide)
    grad_carried = kernel_call(
        carry_kernel, [shape((2, batch, hidden), F32)], [slot_pl, got_back]
    )[0]
    return (
        table_in,
        table_out[:, :hidden],
        table_out[:, hidden],
        grad_one,
        grad_in,
        grad_two,
        jnp.concatenate([bias_one, bias_in], axis=0),
        grad_carried,
    )


def solution(mesh):
    in_specs = (
        P(None, ("grp", "loc"), None),
        P(("grp", "loc")),
        P(None, ("grp", "loc")),
        P(None, ("grp", "loc")),
        P(None, ("grp", "loc")),
        P(("grp", "loc")),
        P(),
        P("grp", None),
        P("grp", None),
        P("grp"),
        P(None, "loc"),
        P(None, "loc"),
        P(None, "loc"),
        P(None, "loc"),
    )
    out_specs = (
        P(("grp", "loc"), None),
        P(("grp", "loc"), None),
        P(("grp", "loc")),
        P(None, "loc"),
        P(None, "loc"),
        P(None, "loc"),
        P(None, "loc"),
        P(None, ("grp", "loc"), None),
    )
    return jax.shard_map(
        on_device, mesh=mesh, in_specs=in_specs, out_specs=out_specs, check_vma=False
    )
```

```python
import functools

import jax
import jax.numpy as jnp
import numpy as np
from jax import lax
from jax.experimental import pallas as pl
from jax.experimental.pallas import tpu as pltpu
from jax.sharding import PartitionSpec as P

BPREG = 1.0
BF16 = jnp.bfloat16
F32 = jnp.float32
I32 = jnp.int32
LANES = 128
VMEM_LIMIT = 48 << 20


def swap(x, axis, bit):
    n = lax.axis_size(axis)
    return lax.ppermute(x, axis, [(i, i ^ bit) for i in range(n)])


def gather_xor(x, axis):
    blocks = {0: x}
    bit = lax.axis_size(axis) // 2
    while bit:
        for k in list(blocks):
            blocks[k | bit] = swap(blocks[k], axis, bit)
        bit //= 2
    return [blocks[k] for k in range(len(blocks))]


def send_xor(chunks, axis):
    return [chunks[0]] + [swap(chunks[j], axis, j) for j in range(1, len(chunks))]


def kernel_call(body, outs, ins, smem=0, scratch=(), us=1, left=0, left_outs=0):
    vmem, place = pl.BlockSpec(memory_space=pltpu.VMEM), pl.BlockSpec(memory_space=pl.ANY)
    nbytes = sum(a.size * a.dtype.itemsize for a in ins)
    nbytes += sum(int(functools.reduce(lambda a, b: a * b, o.shape)) * o.dtype.itemsize for o in outs)
    return pl.pallas_call(
        body,
        out_shape=outs,
        in_specs=[pl.BlockSpec(memory_space=pltpu.SMEM)] * smem
        + [vmem] * (len(ins) - smem - left)
        + [place] * left,
        out_specs=[vmem] * (len(outs) - left_outs) + [place] * left_outs,
        scratch_shapes=list(scratch),
        compiler_params=pltpu.CompilerParams(vmem_limit_bytes=VMEM_LIMIT),
        cost_estimate=pl.CostEstimate(flops=us * 10**9, bytes_accessed=nbytes, transcendentals=0),
    )(*ins)


def after(x, *deps):
    return lax.optimization_barrier((x,) + deps)[0]


def shape(dims, dtype):
    return jax.ShapeDtypeStruct(dims, dtype)


def iota(dims, dim):
    return lax.broadcasted_iota(I32, dims, dim)


def dot(a, b, ca=1, cb=0):
    return lax.dot_general(a, b, (((ca,), (cb,)), ((), ())), preferred_element_type=F32)


class Loader:
    def __init__(self, copies):
        self.copies = copies
        self.waited = set()
        for group in copies.values():
            for copy in group:
                copy.start()

    def ready(self, slot):
        if slot not in self.waited:
            self.waited.add(slot)
            for copy in self.copies[slot]:
                copy.wait()


class Weights(Loader):
    def __init__(self, refs, buf, sem, side=None):
        n = buf.shape[0]
        pieces = (len(refs) - n // 2) // (n // 2)
        copies, k = {}, 0
        for j in range(n):
            row, copies[j] = 0, []
            for _ in range(1 if j < n // 2 else pieces):
                size = refs[k].shape[0]
                at = row
                if side is not None and j >= n // 2:
                    at = pl.multiple_of((side if row == 0 else 1 - side) * size, size)
                part = buf.at[j, pl.ds(at, size), :]
                copies[j].append(pltpu.make_async_copy(refs[k], part, sem.at[k]))
                row, k = row + size, k + 1
        self.buf = buf
        super().__init__(copies)

    def __getitem__(self, j):
        self.ready(j)
        return self.buf[j]


def step_copies(ref, buf, sem, steps, batch, out):
    copies = {}
    for t in reversed(range(steps)):
        at = (slice(None), pl.ds(t * batch, batch), slice(None))
        pair = (buf.at[at], ref.at[at]) if out else (ref.at[at], buf.at[at])
        copies[t] = [pltpu.make_async_copy(*pair, sem.at[t])]
    return copies


def low(cond):
    return jnp.where(cond, 1.0, 0.0).astype(BF16)


def start_kernel(dims, in_ref, tg_ref, plan_ref, carried_ref, s_in, s_tg, s_pl, out_ref):
    owners, rows, cap, batch, ccap = dims
    hidden = carried_ref.shape[2]
    wide = out_ref.shape[1] // 2
    spare = wide - hidden

    def place(ids, span):
        n = ids.shape[0]
        owner_i = iota((n, owners), 1)
        member = (ids >= owner_i * span) & (ids < (owner_i + 1) * span)
        earlier = low(iota((n, n), 1) < iota((n, n), 0))
        before = dot(earlier, low(member))
        rank = jnp.sum(jnp.where(member, before, 0.0), axis=1, keepdims=True).astype(I32)
        owner = jnp.sum(jnp.where(member, owner_i, 0).astype(F32), axis=1, keepdims=True).astype(I32)
        return owner, rank

    def digits(owner, rank, first, value):
        n = owner.shape[0]
        turn = sum((rank >= k * ccap).astype(I32) for k in range(1, -(-cap // ccap)))
        row = owner * ccap + rank - turn * ccap
        hit = low(iota((n, owners * ccap), 1) == row)
        lane = iota((n, LANES), 1)
        high, rest = (value >> 8).astype(F32), (value & 255).astype(F32)
        at = first + 2 * turn
        code = jnp.where(lane == at, high, jnp.where(lane == at + 1, rest, 0.0))
        return dot(hit, code.astype(BF16), 0, 0)

    o_in, r_in = place(in_ref[...], rows)
    o_tg, r_tg = place(tg_ref[...], rows)
    o_pl, r_pl = place(plan_ref[...], batch)
    s_in[...] = o_in * cap + r_in
    s_tg[...] = o_tg * cap + r_tg
    s_pl[...] = o_pl * ccap + r_pl
    turns = -(-cap // ccap)
    code = digits(o_in, r_in, 0, in_ref[...] + 1)
    code += digits(o_tg, r_tg, 2 * turns, tg_ref[...] + 1)
    code += digits(o_pl, r_pl, 4 * turns, plan_ref[...] - o_pl * batch + 1)
    pick = low(iota((batch, owners * ccap), 1) == o_pl * ccap + r_pl)
    parts = [dot(pick, carried_ref[k].astype(BF16), 0, 0) for k in range(2)]
    parts = [parts[0], code[:, :spare], parts[1], jnp.zeros((owners * ccap, spare), F32)]
    out_ref[...] = jnp.concatenate(parts, axis=1).astype(BF16)


def decode(got_ref, row_ref, turn_ref, hidden, first):
    wide = got_ref.shape[1] // 2
    block = got_ref[:, wide - LANES : wide]
    n = row_ref.shape[0]
    found = dot(low(iota((n, block.shape[0]), 1) == row_ref[...]), block)
    at = hidden - wide + LANES + first + 2 * turn_ref[...]
    lane = iota((n, LANES), 1)
    worth = jnp.where(lane == at, 256.0, jnp.where(lane == at + 1, 1.0, 0.0))
    return jnp.sum(found * worth, axis=1, keepdims=True).astype(I32)


def landing(land_ref, got_ref, layer, batch, hidden):
    wide = got_ref.shape[1] // 2
    land = low(iota((land_ref.shape[0], batch), 1) == land_ref[...])
    moved = dot(land, got_ref[:, layer * wide : (layer + 1) * wide], 0, 0)
    return jnp.where(iota(moved.shape, 1) < hidden, moved, 0.0)


def cut(hidden, chunk, n_loc):
    gates = []
    for g in range(3):
        parts = []
        for i in range(n_loc):
            lo, hi = max(g * hidden, i * chunk), min((g + 1) * hidden, (i + 1) * chunk)
            if lo < hi:
                parts.append((i, lo - i * chunk, hi - i * chunk))
        gates.append(parts)
    return gates


def gate_of(g, chunks, hidden, chunk, wide):
    parts = [chunks[i][:, lo:hi] for i, lo, hi in cut(hidden, chunk, len(chunks))[g]]
    pad = jnp.zeros((parts[0].shape[0], wide - hidden), parts[0].dtype)
    return jnp.concatenate(parts + [pad], axis=1)


def chunk_of(i, gates, hidden, chunk, n_loc, cpad):
    parts = []
    for g, places in enumerate(cut(hidden, chunk, n_loc)):
        for k, lo, hi in places:
            if k == i:
                at = i * chunk + lo - g * hidden
                parts.append(gates[g][:, at : at + hi - lo])
    pad = jnp.zeros((parts[0].shape[0], cpad - chunk), parts[0].dtype)
    return jnp.concatenate(parts + [pad], axis=1)


def extend(value, keep, hidden):
    lane = iota(value.shape, 1)
    return jnp.where(lane == hidden, 1.0, jnp.where(lane == hidden + 1, keep, value)).astype(BF16)


def run_steps(steps, batch, hidden, l, keep_ref, weights, gates_of, start, state_ref, res, q_s):
    res_ref, res_s, res_sem = res
    n_loc = q_s.shape[0]
    wide = start.shape[1]
    lane = iota((batch, wide), 1)
    prev = start
    writes = step_copies(res_ref, res_s, res_sem, steps, batch, True)
    for t in range(steps):
        at = pl.ds(t * batch, batch)
        keep = keep_ref[at, :]
        state_ref[at, :] = extend(prev, keep, hidden)
        p = prev * keep
        p_low = p.astype(BF16)
        for j in range(n_loc):
            q_s[l ^ j] = dot(p_low, weights[j])
        in_z, in_r, in_n, qn = gates_of(t, [q_s[i] for i in range(n_loc)])
        z = jax.nn.sigmoid(in_z)
        r = jax.nn.sigmoid(in_r)
        n = jnp.tanh(in_n + r * qn)
        prev = jnp.where(lane < hidden, n + z * (p - n), 0.0)
        for k, val in enumerate((z, r, n, qn, p)):
            res_s[k, at, :] = val
        writes[t][0].start()
    state_ref[pl.ds(steps * batch, batch), :] = extend(prev, 0.0, hidden)
    for t in range(steps):
        writes[t][0].wait()


def pad_kernel(at, n_in, l_ref, w_ref, *refs):
    refs, outs = refs[: n_in - 2], refs[n_in - 2 :]
    out_ref = outs[0]
    rows, cols = w_ref.shape
    out_ref[...] = jnp.zeros(out_ref.shape, BF16)
    out_ref[:rows, :cols] = w_ref[...]
    if at is not None:
        which, row = at
        tile = row // 16 * 16
        here = (iota((16, cols), 0) == row - tile).astype(F32)
        old = out_ref[tile : tile + 16, :cols].astype(F32)
        extra = refs[0][which : which + 1, :].astype(F32)
        out_ref[tile : tile + 16, :cols] = (old + here * extra).astype(BF16)
    if len(outs) == 2:
        half = outs[1].shape[0]
        side = l_ref[1] & 1
        outs[1][...] = out_ref[pl.ds(pl.multiple_of(side * half, half), half), :]
    else:
        first = outs[1].shape[0]
        outs[1][...] = out_ref[:first, :]
        outs[2][...] = out_ref[first:, :]


def gather_in_kernel(dims, base_ref, got_ref, row_ref, turn_ref, table_ref, out_ref, ids_ref, land_ref):
    hidden, turns = dims
    rows, cols = table_ref.shape
    wide = got_ref.shape[1] // 2
    ids = decode(got_ref, row_ref, turn_ref, hidden, 0) - 1 - base_ref[0]
    ids_ref[...] = ids
    at = hidden - wide + LANES + 4 * turns + 1
    land = got_ref[:, wide - LANES : wide].astype(F32)[:, at : at + 1]
    land_ref[...] = land.astype(I32) - 1
    pick = low(iota((ids.shape[0], rows), 1) == ids)
    found = dot(pick, table_ref[...])
    for g in range(3):
        part = found[:, g * hidden : (g + 1) * hidden]
        pad = jnp.zeros((part.shape[0], wide - hidden), F32)
        out_ref[:, g * wide : (g + 1) * wide] = jnp.concatenate([part, pad], axis=1).astype(BF16)


def biased_rows(ids, table_ref, bias_ref, wide):
    n = ids.shape[0]
    rows, cols = table_ref.shape
    pick = low(iota((n, rows), 1) == ids)
    parts = [dot(pick, table_ref[...]), dot(pick, bias_ref[...])[:, :1]]
    parts.append(jnp.zeros((n, wide - cols - 1), F32))
    return jnp.concatenate(parts, axis=1).astype(BF16)


def gather_tg_kernel(dims, base_ref, got_ref, row_ref, turn_ref, table_ref, bias_ref, out_ref, ids_ref):
    hidden, turns = dims
    ids = decode(got_ref, row_ref, turn_ref, hidden, 2 * turns) - 1 - base_ref[0]
    ids_ref[...] = ids
    out_ref[...] = biased_rows(ids, table_ref, bias_ref, out_ref.shape[1])


def gather_neg_kernel(ids_ref, table_ref, bias_ref, out_ref):
    out_ref[...] = biased_rows(ids_ref[...], table_ref, bias_ref, out_ref.shape[1])


def table_kernel(own, pairs, l_ref, *refs):
    mine_ref, far_ref, near_ref = refs[2 * pairs :]
    pad = mine_ref.shape[0]
    l = l_ref[0]
    for j, (ref, at) in enumerate(((mine_ref, None), (near_ref, 0), (far_ref, None), (near_ref, 1))):
        part = None
        for ids_ref, got_ref in zip(refs[:pairs], refs[pairs : 2 * pairs]):
            row = iota((pad, ids_ref.shape[1]), 0)
            hit = (row < own) & (row + (l ^ j) * own == ids_ref[...])
            term = dot(low(hit), got_ref[...])
            part = term if part is None else part + term
        if at is None:
            ref[...] = part
        else:
            ref[at, :, :] = part.astype(BF16)


def table_add_kernel(mine_ref, far_ref, got_ref, sum_ref, send_ref):
    sum_ref[...] = mine_ref[...] + got_ref[0].astype(F32)
    send_ref[...] = (far_ref[...] + got_ref[1].astype(F32)).astype(BF16)


def table_out_kernel(parts, sum_ref, got_ref, out_ref):
    rows, cols = out_ref.shape
    total = (sum_ref[...] + got_ref[...].astype(F32))[:rows]
    wide = total.shape[1] // parts
    size = cols // parts
    split = [total[:, g * wide : g * wide + size] for g in range(parts)]
    out_ref[...] = jnp.concatenate(split, axis=1)


def carry_kernel(slot_ref, got_ref, out_ref):
    hidden = out_ref.shape[2]
    wide = got_ref.shape[1] // 2
    pick = low(iota((slot_ref.shape[0], got_ref.shape[0]), 1) == slot_ref[...])
    back = dot(pick, got_ref[...])
    out_ref[0] = back[:, :hidden]
    out_ref[1] = back[:, wide : wide + hidden]


def split_kernel(bit, l_ref, a_ref, b_ref, keep_ref, send_ref):
    half = keep_ref.shape[0]
    side = (l_ref[0] >> bit) & 1
    for ref, at in ((keep_ref, side), (send_ref, 1 - side)):
        rows = pl.ds(pl.multiple_of(at * half, half), half)
        ref[...] = (a_ref[rows, :].astype(F32) + b_ref[rows, :].astype(F32)).astype(BF16)


def add_kernel(a_ref, b_ref, out_ref):
    out_ref[...] = (a_ref[...].astype(F32) + b_ref[...].astype(F32)).astype(BF16)


def join_kernel(bit, l_ref, a_ref, b_ref, out_ref):
    half = a_ref.shape[0]
    side = (l_ref[0] >> bit) & 1
    for ref, at in ((a_ref, side), (b_ref, 1 - side)):
        out_ref[pl.ds(pl.multiple_of(at * half, half), half), :] = ref[...]


def final_kernel(hidden, bias_row, l_ref, a_ref, b_ref, out_ref, bias_ref):
    side = l_ref[0] & 1
    cols = out_ref.shape[1]
    half = a_ref.shape[0]
    at = (bias_row - half) // 16 * 16
    for first, second, when in ((a_ref, b_ref, 0), (b_ref, a_ref, 1)):

        @pl.when(side == when)
        def _():
            out_ref[:half, :] = first[...].astype(F32)[:, :cols]
            out_ref[half:, :] = second[...].astype(F32)[: hidden - half, :cols]
            row = bias_row - half - at
            bias_ref[...] = second[at : at + 16, :].astype(F32)[row : row + 1, :cols]


def first_kernel(dims, n_w, l_ref, keep_ref, slot_ref, land_ref, got_ref, rows_ref, *refs):
    steps, batch, hidden, bias_row, n_loc = dims
    w_refs, refs = refs[:n_w], refs[n_w:]
    state_ref, res_ref, w_buf, w_sem, res_s, res_sem, q_s, b_s, x_s = refs
    wide = res_s.shape[2]
    l = l_ref[0]
    weights = Weights(w_refs, w_buf, w_sem)
    chunk = b_s.shape[2]
    pick = low(iota((steps * batch, rows_ref.shape[0]), 1) == slot_ref[...])
    rows = dot(pick, rows_ref[...])
    moved = landing(land_ref, got_ref, 0, batch, hidden)
    for j in range(n_loc):
        weights.ready(j)
        b_s[l ^ j] = w_buf[j, bias_row : bias_row + 16, :].astype(F32)[:, :chunk]
    bias = [b_s[i][0:1, :] for i in range(n_loc)]
    bias = [gate_of(g, bias, hidden, chunk, wide) for g in range(3)]
    x_s[...] = rows + jnp.concatenate(bias, axis=1)

    def gates_of(t, q):
        x = x_s[pl.ds(t * batch, batch), :]
        gates = [gate_of(g, q, hidden, chunk, wide) for g in range(3)]
        return x[:, :wide] + gates[0], x[:, wide : 2 * wide] + gates[1], x[:, 2 * wide :], gates[2]

    run_steps(
        steps, batch, hidden, l, keep_ref, weights, gates_of, moved, state_ref,
        (res_ref, res_s, res_sem), q_s,
    )


def second_kernel(dims, n_in, n_w, l_ref, keep_ref, land_ref, got_ref, below_ref, *refs):
    steps, batch, hidden, chunk, n_loc = dims
    in_refs, w_refs, refs = refs[:n_in], refs[n_in : n_in + n_w], refs[n_in + n_w :]
    state_ref, res_ref, in_buf, in_sem, w_buf, w_sem, res_s, res_sem, q_s, x_s = refs
    wide = res_s.shape[2]
    l = l_ref[0]
    inputs = Weights(in_refs, in_buf, in_sem, l_ref[1] & 1)
    weights = Weights(w_refs, w_buf, w_sem, l_ref[1] & 1)
    moved = landing(land_ref, got_ref, 1, batch, hidden)
    below = below_ref[pl.ds(batch, steps * batch), :]
    for j in range(n_loc):
        x_s[l ^ j] = dot(below, inputs[j])

    def gates_of(t, q):
        x = [x_s[i, pl.ds(t * batch, batch), :] for i in range(n_loc)]
        both = [x[i] + q[i] for i in range(n_loc)]
        sizes = (hidden, chunk, wide)
        return (
            gate_of(0, both, *sizes), gate_of(1, both, *sizes), gate_of(2, x, *sizes), gate_of(2, q, *sizes)
        )

    run_steps(
        steps, batch, hidden, l, keep_ref, weights, gates_of, moved, state_ref,
        (res_ref, res_s, res_sem), q_s,
    )


def score_kernel(dims, valid_ref, slot_ref, state_ref, tg_ref, *refs):
    steps, batch, n_loc = dims
    rows = steps * batch
    neg_refs, refs = refs[:n_loc], refs[n_loc:]
    gn_refs, into_ref, send_ref = refs[:n_loc], refs[n_loc], refs[n_loc + 1]
    sn_s, tgt_s, tgg_s, neg_buf, neg_sem = refs[n_loc + 2 :]
    negs = Loader(
        {
            j: [pltpu.make_async_copy(neg_refs[j], neg_buf.at[j], neg_sem.at[j])]
            for j in range(n_loc)
        }
    )
    diag = iota((batch, batch), 0) == iota((batch, batch), 1)
    slots = tg_ref.shape[0]
    pick = low(iota((rows, slots), 1) == slot_ref[...])
    tgt_s[...] = dot(pick, tg_ref[...]).astype(BF16)
    every = state_ref[pl.ds(batch, rows), :]
    for j in range(n_loc):
        negs.ready(j)
        sn_s[j] = dot(every, neg_buf[j], 1, 1)
    for t in range(steps):
        at = pl.ds(t * batch, batch)
        second = state_ref[pl.ds((t + 1) * batch, batch), :]
        targets = tgt_s[at, :]
        st = dot(second, targets, 1, 1)
        sn = [sn_s[j, at, :] for j in range(n_loc)]
        pos = jnp.sum(jnp.where(diag, st, 0.0), axis=1, keepdims=True)
        top = jnp.max(jnp.where(diag, -jnp.inf, st), axis=1, keepdims=True)
        for s in sn:
            top = jnp.maximum(top, jnp.max(s, axis=1, keepdims=True))
        parts = [(st, jnp.where(diag, 0.0, jnp.exp(st - top)))]
        parts += [(s, jnp.exp(s - top)) for s in sn]
        mass = sum(jnp.sum(e, axis=1, keepdims=True) for _, e in parts)
        scale = 1.0 / mass
        parts = [(s, e * scale, jax.nn.sigmoid(pos - s)) for s, e in parts]
        inside = sum(jnp.sum(w * g, axis=1, keepdims=True) for _, w, g in parts)
        penalty = sum(jnp.sum(w * s * s, axis=1, keepdims=True) for s, w, _ in parts)
        slope = sum(jnp.sum(w * g * (1.0 - g), axis=1, keepdims=True) for _, w, g in parts)
        inv = 1.0 / inside
        weight = valid_ref[at, :]
        grads = [
            weight * w * (1.0 + BPREG * (s * s + 2.0 * s - penalty) - g * g * inv)
            for s, w, g in parts
        ]
        gt = grads[0] - jnp.where(diag, weight * slope * inv, 0.0)
        gt_low = gt.astype(BF16)
        into_ref[at, :] = dot(gt_low, targets)
        for j in range(n_loc):
            gn_refs[j][at, :] = grads[j + 1].astype(BF16)
        tgg_s[at, :] = dot(gt_low, second, 0, 0).astype(BF16)
    total = into_ref[...]
    for j in range(n_loc):
        total += dot(gn_refs[j][...], neg_buf[j])
    into_ref[...] = total
    send_ref[...] = dot(pick, tgg_s[...], 0, 0).astype(BF16)


def back_steps(steps, batch, hidden, l, keep_ref, weights, into_ref, res, dq_s, chunks_of):
    loader, res_s = res
    n_loc = dq_s.shape[0]
    wide = into_ref.shape[1]
    lane = iota((batch, wide), 1)
    carry = jnp.zeros((batch, wide), F32)
    for t in reversed(range(steps)):
        at = pl.ds(t * batch, batch)
        g = jnp.where(lane < hidden, into_ref[at, :] + carry, 0.0)
        loader.ready(t)
        z, r, n, qn, p = (res_s[k, at, :] for k in range(5))
        dc = g * (1.0 - z) * (1.0 - n * n)
        da_z = g * (p - n) * z * (1.0 - z)
        da_r = dc * qn * r * (1.0 - r)
        for i, value in enumerate(chunks_of(t, da_z, da_r, dc, dc * r)):
            dq_s[i] = value.astype(BF16)
        dp = g * z
        for j in range(n_loc):
            dp += dot(dq_s[l ^ j], weights[j], 1, 1)
        carry = dp * keep_ref[at, :]
    return jnp.where(lane < hidden, carry, 0.0)


def back_second_kernel(dims, n_in, n_w, l_ref, keep_ref, into_ref, *refs):
    steps, batch, hidden, chunk, n_loc = dims
    res_ref, refs = refs[0], refs[1:]
    in_refs, w_refs, refs = refs[:n_in], refs[n_in : n_in + n_w], refs[n_in + n_w :]
    init_ref, first_ref, refs = refs[0], refs[1], refs[2:]
    ch_refs, refs = refs[: 2 * n_loc], refs[2 * n_loc :]
    dq_s, da_all, dq_all, in_buf, in_sem, w_buf, w_sem, res_s, res_sem = refs
    l = l_ref[0]
    loader = Loader(step_copies(res_ref, res_s, res_sem, steps, batch, False))
    weights = Weights(w_refs, w_buf, w_sem, l_ref[1] & 1)
    inputs = Weights(in_refs, in_buf, in_sem, l_ref[1] & 1)
    sizes = (hidden, chunk, n_loc, dq_s.shape[2])

    def chunks_of(t, da_z, da_r, da_n, dq_n):
        at = pl.ds(t * batch, batch)
        out = []
        for i in range(n_loc):
            dq = chunk_of(i, (da_z, da_r, dq_n), *sizes)
            same = (i + 1) * chunk <= 2 * hidden
            da = dq if same else chunk_of(i, (da_z, da_r, da_n), *sizes)
            da_all[i, at, :] = da.astype(BF16)
            dq_all[i, at, :] = dq.astype(BF16)
            out.append(dq)
        return out

    init_ref[...] = back_steps(
        steps, batch, hidden, l, keep_ref, weights, into_ref, (loader, res_s), dq_s, chunks_of
    )
    rows = steps * batch
    total = None
    for j in range(n_loc):
        da_low = da_all[l ^ j]
        ch_refs[j][...] = da_low
        ch_refs[n_loc + j][...] = dq_all[l ^ j]
        part = dot(da_low, inputs[j], 1, 1)
        total = part if total is None else total + part
    first_ref[...] = total


def back_first_kernel(dims, n_w, l_ref, keep_ref, into_ref, *refs):
    steps, batch, hidden, chunk, n_loc = dims
    res_ref, refs = refs[0], refs[1:]
    w_refs, refs = refs[:n_w], refs[n_w:]
    init_ref, da_all, refs = refs[0], refs[1], refs[2:]
    ch_refs, refs = refs[:n_loc], refs[n_loc:]
    dq_s, dq_all, bias_s, w_buf, w_sem, res_s, res_sem = refs
    l = l_ref[0]
    loader = Loader(step_copies(res_ref, res_s, res_sem, steps, batch, False))
    weights = Weights(w_refs, w_buf, w_sem)
    wide = into_ref.shape[1]
    sizes = (hidden, chunk, n_loc, dq_s.shape[2])
    bias_s[...] = jnp.zeros(bias_s.shape, F32)

    def chunks_of(t, da_z, da_r, da_n, dq_n):
        at = pl.ds(t * batch, batch)
        for g, da in enumerate((da_z, da_r, da_n)):
            da_all[at, g * wide : (g + 1) * wide] = da.astype(BF16)
        out = [chunk_of(i, (da_z, da_r, dq_n), *sizes) for i in range(n_loc)]
        for i, dq in enumerate(out):
            dq_all[i, at, :] = dq.astype(BF16)
        return out

    init_ref[...] = back_steps(
        steps, batch, hidden, l, keep_ref, weights, into_ref, (loader, res_s), dq_s, chunks_of
    )
    rows = steps * batch
    bias = jnp.sum(da_all[...].astype(F32), axis=0, keepdims=True)
    bias = [bias[:, g * wide : (g + 1) * wide] for g in range(3)]
    for i in range(n_loc):
        bias_s[i, 0:1, :] = chunk_of(i, bias, *sizes)
    for j in range(n_loc):
        ch_refs[j][pl.ds(0, rows), :] = dq_all[l ^ j]
        ch_refs[j][pl.ds(rows, 16), :] = bias_s[l ^ j].astype(BF16)


def return_kernel(slot_ref, land_ref, da_ref, init_ref, init2_ref, send_ref, back_ref):
    rows, cols = da_ref.shape
    wide = init_ref.shape[1]
    pick = low(iota((rows, send_ref.shape[0]), 1) == slot_ref[...])
    send_ref[...] = dot(pick, da_ref[...], 0, 0).astype(BF16)
    land = low(iota((land_ref.shape[0], init_ref.shape[0]), 1) == land_ref[...])
    back_ref[:, :wide] = dot(land, init_ref[...].astype(BF16)).astype(BF16)
    back_ref[:, wide:] = dot(land, init2_ref[...].astype(BF16)).astype(BF16)


def scaled(ref, rows, hidden):
    left = ref[pl.ds(0, rows), :].astype(F32)
    return (left * left[:, hidden + 1 : hidden + 2]).astype(BF16)


def dense_kernel(dims, l_ref, *refs):
    steps, batch, hidden, skip, bias_row, n_loc = dims
    rows = steps * batch
    left_refs, ch_refs = refs[:n_loc], refs[n_loc : 2 * n_loc]
    keep_ref, send_ref, all_s = refs[2 * n_loc :]
    half = keep_ref.shape[0]
    side = l_ref[0] & 1
    total, bias = None, None
    for j in range(n_loc):
        left = left_refs[j][pl.ds(batch, rows), :] if skip else scaled(left_refs[j], rows, hidden)
        part = dot(left, ch_refs[j][pl.ds(0, rows), :], 0, 0)
        total = part if total is None else total + part
        if bias_row is not None:
            extra = ch_refs[j][pl.ds(rows, 16), :].astype(F32)
            bias = extra if bias is None else bias + extra
    all_s[...] = total.astype(BF16)
    if bias_row is not None:
        all_s[pl.ds(bias_row, 16), :] = bias.astype(BF16)
    keep_ref[...] = all_s[pl.ds(pl.multiple_of(side * half, half), half), :]
    send_ref[...] = all_s[pl.ds(pl.multiple_of((1 - side) * half, half), half), :]


def neg_kernel(n_loc, owners, *refs):
    gn_refs, b_refs, out_ref = refs[:n_loc], refs[n_loc : 2 * n_loc], refs[2 * n_loc]
    rows = gn_refs[0].shape[0]
    batch = b_refs[0].shape[0] - rows
    total = None
    for j in range(n_loc):
        part = dot(gn_refs[j][...], b_refs[j][pl.ds(batch, rows), :], 0, 0)
        total = part if total is None else total + part
    own = out_ref.shape[0] // owners
    places = [(g >> 1) + (g & 1) * (owners // 2) for g in range(owners)]
    blocks = [total[p * own : (p + 1) * own, :] for p in places]
    out_ref[...] = jnp.concatenate(blocks, axis=0).astype(BF16)


def on_device(
    carried,
    session_plan,
    item_ids,
    target_ids,
    reset_mask,
    valid_counts,
    negative_ids,
    input_table,
    output_table,
    output_bias,
    hidden_one,
    input_two,
    hidden_two,
    gate_biases,
):
    hidden = carried.shape[2]
    wide = -(-(hidden + 2) // LANES) * LANES
    bias_row = wide - 16
    steps, batch = item_ids.shape
    events = steps * batch
    owners = lax.axis_size("grp")
    n_loc = lax.axis_size("loc")
    grp = lax.axis_index("grp")
    loc = lax.axis_index("loc")
    rows = input_table.shape[0]
    base = grp * rows
    gates = input_table.shape[1]
    chunk = gates // n_loc
    cap = events // owners + events // (2 * owners)
    ccap = 4 * batch // owners
    slots, cslots = owners * cap, owners * ccap
    neg_own = negative_ids.shape[0] // owners // n_loc
    neg_part = owners * neg_own
    l_arr = jnp.stack([loc, grp]).astype(I32)

    cpad = -(-chunk // LANES) * LANES
    gpad = 3 * wide
    w_shape = shape((wide, cpad), BF16)

    g_arr = grp.astype(I32).reshape(1)
    bits = owners.bit_length() - 1

    def padded(w, at, first):
        ins = [l_arr, w] if at is None else [l_arr, w, gate_biases]
        outs = [w_shape, shape((first, cpad), BF16)]
        if 2 * first < wide:
            outs.append(shape((wide - first, cpad), BF16))
        return kernel_call(functools.partial(pad_kernel, at, len(ins)), outs, ins, 1)

    def near(x):
        return swap(x, "loc", 1)

    def across(x):
        return swap(x, "loc", 2)

    def join(bit, kept, got, index=g_arr):
        return kernel_call(
            functools.partial(join_kernel, bit),
            [shape((2 * kept.shape[0],) + kept.shape[1:], BF16)],
            [index, kept, got], 1,
        )[0]

    p_one, *one_pieces = padded(hidden_one, (0, bias_row), wide // 8)
    y_one = [across(one_pieces[0])]
    y_one.append(across(after(one_pieces[1], y_one[0])))

    slot_in, slot_tg, slot_pl, packed = kernel_call(
        functools.partial(start_kernel, (owners, rows, cap, batch, ccap)),
        [
            shape((events, 1), I32),
            shape((events, 1), I32),
            shape((batch, 1), I32),
            shape((cslots, 2 * wide), BF16),
        ],
        [
            after(item_ids, p_one).reshape(events, 1),
            target_ids.reshape(events, 1),
            session_plan.reshape(batch, 1),
            carried,
        ],
        0, (), 3,
    )

    def to_owners(x):
        got = lax.all_to_all(
            x.reshape((owners, x.shape[0] // owners) + x.shape[1:]),
            "grp", split_axis=0, concat_axis=0, tiled=True,
        )
        return got.reshape(x.shape)

    got_c = to_owners(after(packed, y_one[0]))

    bias_col = output_bias[:, None]
    mine = lax.dynamic_slice(
        negative_ids.reshape(owners, n_loc, neg_own), (grp, loc, 0), (1, 1, neg_own)
    ).reshape(neg_own) - base
    negs_own = kernel_call(
        gather_neg_kernel,
        [shape((neg_own, wide), BF16)],
        [after(mine, p_one).reshape(neg_own, 1), output_table, bias_col],
    )[0]
    negs_half = negs_own
    for bit in range(1, bits):
        negs_half = join(bit, negs_half, swap(negs_half, "grp", 1 << bit))
    negs = join(0, negs_half, swap(negs_half, "grp", 1))

    place = np.arange(slots)
    turns = -(-cap // ccap)
    place_row = jnp.asarray((place // cap * ccap + place % cap % ccap)[:, None], I32)
    place_turn = jnp.asarray((place % cap // ccap)[:, None], I32)
    base_arr = base.astype(I32).reshape(1)
    ids_shape = shape((slots, 1), I32)
    reply_in, in_ids, land = kernel_call(
        functools.partial(gather_in_kernel, (hidden, turns)),
        [shape((slots, gpad), BF16), ids_shape, shape((cslots, 1), I32)],
        [base_arr, got_c, place_row, place_turn, input_table],
        1, (), 4,
    )
    p_in, h_in = padded(input_two, (1, hidden), wide // 2)
    p_two, h_two = padded(hidden_two, None, wide // 2)
    y_in = across(after(h_in, y_one[1]))
    got_rows = to_owners(after(reply_in, negs_half, y_one[1]))
    y_two = across(after(h_two, y_in))
    y_in = [y_in, swap(y_in, "grp", 1)]
    y_neg = across(after(negs, y_two))
    y_two = [y_two, swap(y_two, "grp", 1)]
    reply_tg, tg_ids = kernel_call(
        functools.partial(gather_tg_kernel, (hidden, turns)),
        [shape((slots, wide), BF16), ids_shape],
        [base_arr, got_c, place_row, place_turn, output_table, bias_col],
        1, (), 3,
    )
    tg_rows = to_owners(after(reply_tg, got_rows))

    def four(own, pieces):
        return [own, near(own), *pieces, *(near(p) for p in pieces)]

    w_one = four(p_one, y_one)

    keep = (1 - reset_mask).astype(F32).reshape(events, 1)
    valid = (jnp.arange(steps, dtype=I32)[:, None] < valid_counts[None, :]).astype(F32)
    valid = (valid / steps).reshape(events, 1)

    res_shape = shape((5, events, wide), F32)
    n_w = 2 + n_loc
    w_scratch = [pltpu.VMEM((n_loc, wide, cpad), BF16), pltpu.SemaphoreType.DMA((n_w,))]
    res_scratch = [pltpu.VMEM((5, events, wide), F32), pltpu.SemaphoreType.DMA((steps,))]
    state_shape = shape(((steps + 1) * batch, wide), BF16)
    q_scratch = pltpu.VMEM((n_loc, batch, cpad), F32)
    dq_scratch = pltpu.VMEM((n_loc, batch, cpad), BF16)
    x_scratch = pltpu.VMEM((n_loc, events, cpad), F32)
    all_scratch = pltpu.VMEM((n_loc, events, cpad), BF16)

    state_a, res_one = kernel_call(
        functools.partial(first_kernel, (steps, batch, hidden, bias_row, n_loc), n_w),
        [state_shape, res_shape],
        [l_arr, keep, slot_in, land, got_c, after(got_rows, reply_tg, negs, y_two[0], y_in[1])] + w_one,
        1,
        w_scratch
        + res_scratch
        + [q_scratch, pltpu.VMEM((n_loc, 16, chunk), F32), pltpu.VMEM((events, gpad), F32)],
        12, n_w, 1,
    )
    w_in = four(p_in, [after(y, state_a) for y in y_in])
    w_two = four(p_two, [after(y, state_a) for y in y_two])
    state_b, res_two = kernel_call(
        functools.partial(second_kernel, (steps, batch, hidden, chunk, n_loc), n_w, n_w),
        [state_shape, res_shape],
        [l_arr, keep, land, got_c, after(state_a, y_neg)] + w_in + w_two,
        1,
        w_scratch + w_scratch + res_scratch + [q_scratch, x_scratch],
        15, 2 * n_w, 1,
    )
    y_b = across(after(state_b, y_neg))

    y_neg = after(y_neg, state_b)
    negs = [negs, near(negs), y_neg, near(y_neg)]
    *g_neg, into_second, send_tg = kernel_call(
        functools.partial(score_kernel, (steps, batch, n_loc)),
        [shape((events, neg_part), BF16)] * n_loc
        + [shape((events, wide), F32), shape((slots, wide), BF16)],
        [valid, slot_tg, state_b, tg_rows] + negs,
        0,
        [
            pltpu.VMEM((n_loc, events, neg_part), F32),
            pltpu.VMEM((events, wide), BF16),
            pltpu.VMEM((events, wide), BF16),
            pltpu.VMEM((n_loc, neg_part, wide), BF16),
            pltpu.SemaphoreType.DMA((n_loc,)),
        ],
        12, n_loc,
    )
    init_two, into_first, *ch_two = kernel_call(
        functools.partial(back_second_kernel, (steps, batch, hidden, chunk, n_loc), n_w, n_w),
        [shape((batch, wide), F32), shape((events, wide), F32)]
        + [shape((events, cpad), BF16)] * (2 * n_loc),
        [l_arr, keep, after(into_second, y_b), res_two] + w_in + w_two,
        1,
        [dq_scratch, all_scratch, all_scratch] + w_scratch + w_scratch + res_scratch,
        17, 2 * n_w + 1,
    )
    def send_after(chunks, *deps):
        return send_xor([after(c, *deps) for c in chunks], "loc")

    ch_in, ch_two = send_xor(ch_two[:n_loc], "loc"), send_xor(ch_two[n_loc:], "loc")
    y_a = across(after(state_a, into_second))
    got_tg_g = to_owners(send_tg)
    init_one, da_one, *ch_one = kernel_call(
        functools.partial(back_first_kernel, (steps, batch, hidden, chunk, n_loc), n_w),
        [shape((batch, wide), F32), shape((events, gpad), BF16)]
        + [shape((events + 16, cpad), BF16)] * n_loc,
        [l_arr, keep, after(into_first, y_a), res_one] + w_one,
        1,
        [dq_scratch, all_scratch, pltpu.VMEM((n_loc, 16, cpad), F32)] + w_scratch + res_scratch,
        13, n_w + 1,
    )
    send_in, back_c = kernel_call(
        return_kernel,
        [shape((slots, gpad), BF16), shape((cslots, 2 * wide), BF16)],
        [slot_in, land, after(da_one, *ch_in[2:]), init_one, init_two],
        0, (), 3,
    )
    got_in_g = to_owners(after(send_in, got_tg_g))
    ch_one = send_xor(ch_one, "loc")
    g_neg = send_after(g_neg, *ch_one[2:])

    y_a, y_b = after(y_a, send_in), after(y_b, send_in)
    states_a = [state_a, near(state_a), y_a, near(y_a)]
    states_b = [state_b, near(state_b), y_b, near(y_b)]

    neg_grad = kernel_call(
        functools.partial(neg_kernel, n_loc, owners),
        [shape((neg_part, wide), BF16)],
        g_neg + states_b,
        0, (), 2,
    )[0]

    def all_sums(makers, waits):
        def one(make):
            kept, sent = make()
            rest = kept.shape[0]
            for bit in range(bits):
                got = yield sent, 1 << bit
                if bit < bits - 2:
                    rest //= 2
                    kept, sent = kernel_call(
                        functools.partial(split_kernel, bit + 1),
                        [shape((rest, cpad), BF16)] * 2,
                        [g_arr, kept, got],
                        1,
                    )
                else:
                    kept = kernel_call(add_kernel, [shape((rest, cpad), BF16)], [kept, got])[0]
                    sent = kept
            for bit in reversed(range(1, bits - 1)):
                kept = join(bit, kept, (yield kept, 1 << bit))
            got = yield kept, 1
            return kept, got

        chains = [one(make) for make in makers]
        results, asks, before, step = [None] * len(chains), {}, (), 0
        while None in results:
            if step < len(chains):
                asks[step] = next(chains[step])
            wait = tuple(before) + tuple(waits.get(step, lambda: ())())
            answers = {
                k: swap(after(ask[0], *wait) if wait else ask[0], "grp", ask[1])
                for k, ask in asks.items()
            }
            asks, before = {}, list(answers.values())
            for k, answer in answers.items():
                try:
                    asks[k] = chains[k].send(answer)
                except StopIteration as done:
                    results[k] = done.value
            step += 1
        return results

    half_shape = shape((wide // 2, cpad), BF16)

    def product(lefts, chunks, skip, bias_at):
        return kernel_call(
            functools.partial(dense_kernel, (steps, batch, hidden, skip, bias_at, n_loc)),
            [half_shape] * 2,
            [g_arr] + lefts + chunks,
            1, [pltpu.VMEM((wide, cpad), BF16)], 5,
        )

    def finish(parts, bias_row):
        return kernel_call(
            functools.partial(final_kernel, hidden, bias_row),
            [shape((hidden, chunk), F32), shape((1, chunk), F32)],
            [g_arr, *parts],
            1, (), 2,
        )

    sums = {}

    def made(name, *args):
        def make():
            sums[name] = product(*args)
            return sums[name]

        return make

    def start_back():
        sums["back"] = to_owners(after(back_c, got_in_g, sums["one"][0]))
        return ()

    def bring_back():
        return (sums["back"],)

    in_parts, two_parts, one_parts = all_sums(
        [
            made("in", states_a, ch_in, True, None),
            made("two", states_b, ch_two, False, None),
            made("one", states_a, ch_one, False, bias_row),
        ],
        {1: lambda: tuple(ch_one[2:]), 2: start_back, 3: lambda: (got_in_g,), 5: bring_back},
    )
    got_back = sums["back"]
    got_neg_g = to_owners(after(neg_grad, got_back))
    grad_in, bias_in = finish(in_parts, hidden)
    grad_two, _ = finish(two_parts, hidden)
    grad_one, bias_one = finish(one_parts, bias_row)

    own = rows // n_loc
    own_pad = -(-own // 16) * 16

    def table_sum(ids, grads, cols, parts, *wait):
        across_cols = grads[0].shape[1]
        full = shape((own_pad, across_cols), F32)
        sent = shape((own_pad, across_cols), BF16)
        mine_p, far_p, near_p = kernel_call(
            functools.partial(table_kernel, own, len(ids)),
            [full, full, shape((2, own_pad, across_cols), BF16)],
            [l_arr] + [i.reshape(1, i.size) for i in ids] + grads,
            1, (), 4,
        )
        total, far_s = kernel_call(
            table_add_kernel, [full, sent], [after(mine_p, *wait), far_p, near(near_p)]
        )
        return kernel_call(
            functools.partial(table_out_kernel, parts),
            [shape((own, cols), F32)],
            [total, across(far_s)],
        )[0]

    table_in = table_sum([in_ids], [got_in_g], gates, 3, got_back)
    neg_ids = jnp.broadcast_to(mine[None, :], (owners, neg_own)).reshape(neg_part)
    table_out = table_sum([tg_ids, neg_ids], [got_tg_g, got_neg_g], wide, 1)
    grad_carried = kernel_call(
        carry_kernel, [shape((2, batch, hidden), F32)], [slot_pl, got_back]
    )[0]
    return (
        table_in,
        table_out[:, :hidden],
        table_out[:, hidden],
        grad_one,
        grad_in,
        grad_two,
        jnp.concatenate([bias_one, bias_in], axis=0),
        grad_carried,
    )


def solution(mesh):
    in_specs = (
        P(None, ("grp", "loc"), None),
        P(("grp", "loc")),
        P(None, ("grp", "loc")),
        P(None, ("grp", "loc")),
        P(None, ("grp", "loc")),
        P(("grp", "loc")),
        P(),
        P("grp", None),
        P("grp", None),
        P("grp"),
        P(None, "loc"),
        P(None, "loc"),
        P(None, "loc"),
        P(None, "loc"),
    )
    out_specs = (
        P(("grp", "loc"), None),
        P(("grp", "loc"), None),
        P(("grp", "loc")),
        P(None, "loc"),
        P(None, "loc"),
        P(None, "loc"),
        P(None, "loc"),
        P(None, ("grp", "loc"), None),
    )
    return jax.shard_map(
        on_device, mesh=mesh, in_specs=in_specs, out_specs=out_specs, check_vma=False
    )
```

```python
import functools

import jax
import jax.numpy as jnp
import numpy as np
from jax import lax
from jax.experimental import pallas as pl
from jax.experimental.pallas import tpu as pltpu
from jax.sharding import PartitionSpec as P

BPREG = 1.0
BF16 = jnp.bfloat16
F32 = jnp.float32
I32 = jnp.int32
LANES = 128
VMEM_LIMIT = 48 << 20


def swap(x, axis, bit):
    n = lax.axis_size(axis)
    return lax.ppermute(x, axis, [(i, i ^ bit) for i in range(n)])


def gather_xor(x, axis):
    blocks = {0: x}
    bit = lax.axis_size(axis) // 2
    while bit:
        for k in list(blocks):
            blocks[k | bit] = swap(blocks[k], axis, bit)
        bit //= 2
    return [blocks[k] for k in range(len(blocks))]


def send_xor(chunks, axis):
    return [chunks[0]] + [swap(chunks[j], axis, j) for j in range(1, len(chunks))]


def kernel_call(body, outs, ins, smem=0, scratch=(), us=1, left=0, left_outs=0):
    vmem, place = pl.BlockSpec(memory_space=pltpu.VMEM), pl.BlockSpec(memory_space=pl.ANY)
    nbytes = sum(a.size * a.dtype.itemsize for a in ins)
    nbytes += sum(int(functools.reduce(lambda a, b: a * b, o.shape)) * o.dtype.itemsize for o in outs)
    return pl.pallas_call(
        body,
        out_shape=outs,
        in_specs=[pl.BlockSpec(memory_space=pltpu.SMEM)] * smem
        + [vmem] * (len(ins) - smem - left)
        + [place] * left,
        out_specs=[vmem] * (len(outs) - left_outs) + [place] * left_outs,
        scratch_shapes=list(scratch),
        compiler_params=pltpu.CompilerParams(vmem_limit_bytes=VMEM_LIMIT),
        cost_estimate=pl.CostEstimate(flops=us * 10**9, bytes_accessed=nbytes, transcendentals=0),
    )(*ins)


def after(x, *deps):
    return lax.optimization_barrier((x,) + deps)[0]


def shape(dims, dtype):
    return jax.ShapeDtypeStruct(dims, dtype)


def iota(dims, dim):
    return lax.broadcasted_iota(I32, dims, dim)


def dot(a, b, ca=1, cb=0):
    return lax.dot_general(a, b, (((ca,), (cb,)), ((), ())), preferred_element_type=F32)


class Loader:
    def __init__(self, copies):
        self.copies = copies
        self.waited = set()
        for group in copies.values():
            for copy in group:
                copy.start()

    def ready(self, slot):
        if slot not in self.waited:
            self.waited.add(slot)
            for copy in self.copies[slot]:
                copy.wait()


class Weights(Loader):
    def __init__(self, refs, buf, sem, side=None):
        n = buf.shape[0]
        pieces = (len(refs) - n // 2) // (n // 2)
        copies, k = {}, 0
        for j in range(n):
            row, copies[j] = 0, []
            for _ in range(1 if j < n // 2 else pieces):
                size = refs[k].shape[0]
                at = row
                if side is not None and j >= n // 2:
                    at = pl.multiple_of((side if row == 0 else 1 - side) * size, size)
                part = buf.at[j, pl.ds(at, size), :]
                copies[j].append(pltpu.make_async_copy(refs[k], part, sem.at[k]))
                row, k = row + size, k + 1
        self.buf = buf
        super().__init__(copies)

    def __getitem__(self, j):
        self.ready(j)
        return self.buf[j]


def step_copies(ref, buf, sem, steps, batch, out):
    copies = {}
    for t in reversed(range(steps)):
        at = (slice(None), pl.ds(t * batch, batch), slice(None))
        pair = (buf.at[at], ref.at[at]) if out else (ref.at[at], buf.at[at])
        copies[t] = [pltpu.make_async_copy(*pair, sem.at[t])]
    return copies


def low(cond):
    return jnp.where(cond, 1.0, 0.0).astype(BF16)


def start_kernel(dims, in_ref, tg_ref, plan_ref, carried_ref, s_in, s_tg, s_pl, out_ref):
    owners, rows, cap, batch, ccap = dims
    hidden = carried_ref.shape[2]
    wide = out_ref.shape[1] // 2
    spare = wide - hidden

    def place(ids, span):
        n = ids.shape[0]
        owner_i = iota((n, owners), 1)
        member = (ids >= owner_i * span) & (ids < (owner_i + 1) * span)
        earlier = low(iota((n, n), 1) < iota((n, n), 0))
        before = dot(earlier, low(member))
        rank = jnp.sum(jnp.where(member, before, 0.0), axis=1, keepdims=True).astype(I32)
        owner = jnp.sum(jnp.where(member, owner_i, 0).astype(F32), axis=1, keepdims=True).astype(I32)
        return owner, rank

    def digits(owner, rank, first, value):
        n = owner.shape[0]
        turn = sum((rank >= k * ccap).astype(I32) for k in range(1, -(-cap // ccap)))
        row = owner * ccap + rank - turn * ccap
        hit = low(iota((n, owners * ccap), 1) == row)
        lane = iota((n, LANES), 1)
        high, rest = (value >> 8).astype(F32), (value & 255).astype(F32)
        at = first + 2 * turn
        code = jnp.where(lane == at, high, jnp.where(lane == at + 1, rest, 0.0))
        return dot(hit, code.astype(BF16), 0, 0)

    o_in, r_in = place(in_ref[...], rows)
    o_tg, r_tg = place(tg_ref[...], rows)
    o_pl, r_pl = place(plan_ref[...], batch)
    s_in[...] = o_in * cap + r_in
    s_tg[...] = o_tg * cap + r_tg
    s_pl[...] = o_pl * ccap + r_pl
    turns = -(-cap // ccap)
    code = digits(o_in, r_in, 0, in_ref[...] + 1)
    code += digits(o_tg, r_tg, 2 * turns, tg_ref[...] + 1)
    code += digits(o_pl, r_pl, 4 * turns, plan_ref[...] - o_pl * batch + 1)
    pick = low(iota((batch, owners * ccap), 1) == o_pl * ccap + r_pl)
    parts = [dot(pick, carried_ref[k].astype(BF16), 0, 0) for k in range(2)]
    parts = [parts[0], code[:, :spare], parts[1], jnp.zeros((owners * ccap, spare), F32)]
    out_ref[...] = jnp.concatenate(parts, axis=1).astype(BF16)


def decode(got_ref, row_ref, turn_ref, hidden, first):
    wide = got_ref.shape[1] // 2
    block = got_ref[:, wide - LANES : wide]
    n = row_ref.shape[0]
    found = dot(low(iota((n, block.shape[0]), 1) == row_ref[...]), block)
    at = hidden - wide + LANES + first + 2 * turn_ref[...]
    lane = iota((n, LANES), 1)
    worth = jnp.where(lane == at, 256.0, jnp.where(lane == at + 1, 1.0, 0.0))
    return jnp.sum(found * worth, axis=1, keepdims=True).astype(I32)


def landing(land_ref, got_ref, layer, batch, hidden):
    wide = got_ref.shape[1] // 2
    land = low(iota((land_ref.shape[0], batch), 1) == land_ref[...])
    moved = dot(land, got_ref[:, layer * wide : (layer + 1) * wide], 0, 0)
    return jnp.where(iota(moved.shape, 1) < hidden, moved, 0.0)


def cut(hidden, chunk, n_loc):
    gates = []
    for g in range(3):
        parts = []
        for i in range(n_loc):
            lo, hi = max(g * hidden, i * chunk), min((g + 1) * hidden, (i + 1) * chunk)
            if lo < hi:
                parts.append((i, lo - i * chunk, hi - i * chunk))
        gates.append(parts)
    return gates


def gate_of(g, chunks, hidden, chunk, wide):
    parts = [chunks[i][:, lo:hi] for i, lo, hi in cut(hidden, chunk, len(chunks))[g]]
    pad = jnp.zeros((parts[0].shape[0], wide - hidden), parts[0].dtype)
    return jnp.concatenate(parts + [pad], axis=1)


def chunk_of(i, gates, hidden, chunk, n_loc, cpad):
    parts = []
    for g, places in enumerate(cut(hidden, chunk, n_loc)):
        for k, lo, hi in places:
            if k == i:
                at = i * chunk + lo - g * hidden
                parts.append(gates[g][:, at : at + hi - lo])
    pad = jnp.zeros((parts[0].shape[0], cpad - chunk), parts[0].dtype)
    return jnp.concatenate(parts + [pad], axis=1)


def extend(value, keep, hidden):
    lane = iota(value.shape, 1)
    return jnp.where(lane == hidden, 1.0, jnp.where(lane == hidden + 1, keep, value)).astype(BF16)


def run_steps(steps, batch, hidden, l, keep_ref, weights, gates_of, start, state_ref, res, q_s):
    res_ref, res_s, res_sem = res
    n_loc = q_s.shape[0]
    wide = start.shape[1]
    lane = iota((batch, wide), 1)
    prev = start
    writes = step_copies(res_ref, res_s, res_sem, steps, batch, True)
    for t in range(steps):
        at = pl.ds(t * batch, batch)
        keep = keep_ref[at, :]
        state_ref[at, :] = extend(prev, keep, hidden)
        p = prev * keep
        p_low = p.astype(BF16)
        for j in range(n_loc):
            q_s[l ^ j] = dot(p_low, weights[j])
        in_z, in_r, in_n, qn = gates_of(t, [q_s[i] for i in range(n_loc)])
        z = jax.nn.sigmoid(in_z)
        r = jax.nn.sigmoid(in_r)
        n = jnp.tanh(in_n + r * qn)
        prev = jnp.where(lane < hidden, n + z * (p - n), 0.0)
        for k, val in enumerate((z, r, n, qn, p)):
            res_s[k, at, :] = val
        writes[t][0].start()
    state_ref[pl.ds(steps * batch, batch), :] = extend(prev, 0.0, hidden)
    for t in range(steps):
        writes[t][0].wait()


def pad_kernel(at, n_in, l_ref, w_ref, *refs):
    refs, outs = refs[: n_in - 2], refs[n_in - 2 :]
    out_ref = outs[0]
    rows, cols = w_ref.shape
    out_ref[...] = jnp.zeros(out_ref.shape, BF16)
    out_ref[:rows, :cols] = w_ref[...]
    if at is not None:
        which, row = at
        tile = row // 16 * 16
        here = (iota((16, cols), 0) == row - tile).astype(F32)
        old = out_ref[tile : tile + 16, :cols].astype(F32)
        extra = refs[0][which : which + 1, :].astype(F32)
        out_ref[tile : tile + 16, :cols] = (old + here * extra).astype(BF16)
    if len(outs) == 1:
        pass
    elif len(outs) == 2:
        half = outs[1].shape[0]
        side = l_ref[1] & 1
        outs[1][...] = out_ref[pl.ds(pl.multiple_of(side * half, half), half), :]
    else:
        first = outs[1].shape[0]
        outs[1][...] = out_ref[:first, :]
        outs[2][...] = out_ref[first:, :]


def gather_in_kernel(dims, base_ref, got_ref, row_ref, turn_ref, table_ref, out_ref, ids_ref, land_ref):
    hidden, turns = dims
    rows, cols = table_ref.shape
    wide = got_ref.shape[1] // 2
    ids = decode(got_ref, row_ref, turn_ref, hidden, 0) - 1 - base_ref[0]
    ids_ref[...] = ids
    at = hidden - wide + LANES + 4 * turns + 1
    land = got_ref[:, wide - LANES : wide].astype(F32)[:, at : at + 1]
    land_ref[...] = land.astype(I32) - 1
    pick = low(iota((ids.shape[0], rows), 1) == ids)
    found = dot(pick, table_ref[...])
    for g in range(3):
        part = found[:, g * hidden : (g + 1) * hidden]
        pad = jnp.zeros((part.shape[0], wide - hidden), F32)
        out_ref[:, g * wide : (g + 1) * wide] = jnp.concatenate([part, pad], axis=1).astype(BF16)


def biased_rows(ids, table_ref, bias_ref, wide):
    n = ids.shape[0]
    rows, cols = table_ref.shape
    pick = low(iota((n, rows), 1) == ids)
    parts = [dot(pick, table_ref[...]), dot(pick, bias_ref[...])[:, :1]]
    parts.append(jnp.zeros((n, wide - cols - 1), F32))
    return jnp.concatenate(parts, axis=1).astype(BF16)


def gather_tg_kernel(dims, base_ref, got_ref, row_ref, turn_ref, table_ref, bias_ref, out_ref, ids_ref):
    hidden, turns = dims
    ids = decode(got_ref, row_ref, turn_ref, hidden, 2 * turns) - 1 - base_ref[0]
    ids_ref[...] = ids
    out_ref[...] = biased_rows(ids, table_ref, bias_ref, out_ref.shape[1])


def gather_neg_kernel(ids_ref, table_ref, bias_ref, out_ref):
    out_ref[...] = biased_rows(ids_ref[...], table_ref, bias_ref, out_ref.shape[1])


def table_kernel(own, pairs, l_ref, *refs):
    mine_ref, far_ref, near_ref = refs[2 * pairs :]
    pad = mine_ref.shape[0]
    l = l_ref[0]
    for j, (ref, at) in enumerate(((mine_ref, None), (near_ref, 0), (far_ref, None), (near_ref, 1))):
        part = None
        for ids_ref, got_ref in zip(refs[:pairs], refs[pairs : 2 * pairs]):
            row = iota((pad, ids_ref.shape[1]), 0)
            hit = (row < own) & (row + (l ^ j) * own == ids_ref[...])
            term = dot(low(hit), got_ref[...])
            part = term if part is None else part + term
        if at is None:
            ref[...] = part
        else:
            ref[at, :, :] = part.astype(BF16)


def table_add_kernel(mine_ref, far_ref, got_ref, sum_ref, send_ref):
    sum_ref[...] = mine_ref[...] + got_ref[0].astype(F32)
    send_ref[...] = (far_ref[...] + got_ref[1].astype(F32)).astype(BF16)


def table_out_kernel(parts, sum_ref, got_ref, out_ref):
    rows, cols = out_ref.shape
    total = (sum_ref[...] + got_ref[...].astype(F32))[:rows]
    wide = total.shape[1] // parts
    size = cols // parts
    split = [total[:, g * wide : g * wide + size] for g in range(parts)]
    out_ref[...] = jnp.concatenate(split, axis=1)


def carry_kernel(slot_ref, got_ref, out_ref):
    hidden = out_ref.shape[2]
    wide = got_ref.shape[1] // 2
    pick = low(iota((slot_ref.shape[0], got_ref.shape[0]), 1) == slot_ref[...])
    back = dot(pick, got_ref[...])
    out_ref[0] = back[:, :hidden]
    out_ref[1] = back[:, wide : wide + hidden]


def split_kernel(bit, l_ref, a_ref, b_ref, keep_ref, send_ref):
    half = keep_ref.shape[0]
    side = (l_ref[0] >> bit) & 1
    for ref, at in ((keep_ref, side), (send_ref, 1 - side)):
        rows = pl.ds(pl.multiple_of(at * half, half), half)
        ref[...] = (a_ref[rows, :].astype(F32) + b_ref[rows, :].astype(F32)).astype(BF16)


def add_kernel(a_ref, b_ref, out_ref):
    out_ref[...] = (a_ref[...].astype(F32) + b_ref[...].astype(F32)).astype(BF16)


def join_kernel(bit, l_ref, a_ref, b_ref, out_ref):
    half = a_ref.shape[0]
    side = (l_ref[0] >> bit) & 1
    for ref, at in ((a_ref, side), (b_ref, 1 - side)):
        out_ref[pl.ds(pl.multiple_of(at * half, half), half), :] = ref[...]


def final_kernel(hidden, bias_row, l_ref, a_ref, b_ref, out_ref, bias_ref):
    side = l_ref[0] & 1
    cols = out_ref.shape[1]
    half = a_ref.shape[0]
    at = (bias_row - half) // 16 * 16
    for first, second, when in ((a_ref, b_ref, 0), (b_ref, a_ref, 1)):

        @pl.when(side == when)
        def _():
            out_ref[:half, :] = first[...].astype(F32)[:, :cols]
            out_ref[half:, :] = second[...].astype(F32)[: hidden - half, :cols]
            row = bias_row - half - at
            bias_ref[...] = second[at : at + 16, :].astype(F32)[row : row + 1, :cols]


def first_kernel(dims, n_w, l_ref, keep_ref, slot_ref, land_ref, got_ref, rows_ref, *refs):
    steps, batch, hidden, bias_row, n_loc = dims
    w_refs, refs = refs[:n_w], refs[n_w:]
    state_ref, res_ref, w_buf, w_sem, res_s, res_sem, q_s, b_s, x_s = refs
    wide = res_s.shape[2]
    l = l_ref[0]
    weights = Weights(w_refs, w_buf, w_sem)
    chunk = b_s.shape[2]
    pick = low(iota((steps * batch, rows_ref.shape[0]), 1) == slot_ref[...])
    rows = dot(pick, rows_ref[...])
    moved = landing(land_ref, got_ref, 0, batch, hidden)
    for j in range(n_loc):
        weights.ready(j)
        b_s[l ^ j] = w_buf[j, bias_row : bias_row + 16, :].astype(F32)[:, :chunk]
    bias = [b_s[i][0:1, :] for i in range(n_loc)]
    bias = [gate_of(g, bias, hidden, chunk, wide) for g in range(3)]
    x_s[...] = rows + jnp.concatenate(bias, axis=1)

    def gates_of(t, q):
        x = x_s[pl.ds(t * batch, batch), :]
        gates = [gate_of(g, q, hidden, chunk, wide) for g in range(3)]
        return x[:, :wide] + gates[0], x[:, wide : 2 * wide] + gates[1], x[:, 2 * wide :], gates[2]

    run_steps(
        steps, batch, hidden, l, keep_ref, weights, gates_of, moved, state_ref,
        (res_ref, res_s, res_sem), q_s,
    )


def second_kernel(dims, n_in, n_w, l_ref, keep_ref, land_ref, got_ref, below_ref, *refs):
    steps, batch, hidden, chunk, n_loc = dims
    in_refs, w_refs, refs = refs[:n_in], refs[n_in : n_in + n_w], refs[n_in + n_w :]
    state_ref, res_ref, in_buf, in_sem, w_buf, w_sem, res_s, res_sem, q_s, x_s = refs
    wide = res_s.shape[2]
    l = l_ref[0]
    inputs = Weights(in_refs, in_buf, in_sem, l_ref[1] & 1)
    weights = Weights(w_refs, w_buf, w_sem)
    moved = landing(land_ref, got_ref, 1, batch, hidden)
    below = below_ref[pl.ds(batch, steps * batch), :]
    for j in range(n_loc):
        x_s[l ^ j] = dot(below, inputs[j])

    def gates_of(t, q):
        x = [x_s[i, pl.ds(t * batch, batch), :] for i in range(n_loc)]
        both = [x[i] + q[i] for i in range(n_loc)]
        sizes = (hidden, chunk, wide)
        return (
            gate_of(0, both, *sizes), gate_of(1, both, *sizes), gate_of(2, x, *sizes), gate_of(2, q, *sizes)
        )

    run_steps(
        steps, batch, hidden, l, keep_ref, weights, gates_of, moved, state_ref,
        (res_ref, res_s, res_sem), q_s,
    )


def score_kernel(dims, valid_ref, slot_ref, state_ref, tg_ref, *refs):
    steps, batch, n_loc = dims
    rows = steps * batch
    neg_refs, refs = refs[:n_loc], refs[n_loc:]
    gn_refs, into_ref, send_ref = refs[:n_loc], refs[n_loc], refs[n_loc + 1]
    sn_s, tgt_s, tgg_s, neg_buf, neg_sem = refs[n_loc + 2 :]
    negs = Loader(
        {
            j: [pltpu.make_async_copy(neg_refs[j], neg_buf.at[j], neg_sem.at[j])]
            for j in range(n_loc)
        }
    )
    diag = iota((batch, batch), 0) == iota((batch, batch), 1)
    slots = tg_ref.shape[0]
    pick = low(iota((rows, slots), 1) == slot_ref[...])
    tgt_s[...] = dot(pick, tg_ref[...]).astype(BF16)
    every = state_ref[pl.ds(batch, rows), :]
    for j in range(n_loc):
        negs.ready(j)
        sn_s[j] = dot(every, neg_buf[j], 1, 1)
    for t in range(steps):
        at = pl.ds(t * batch, batch)
        second = state_ref[pl.ds((t + 1) * batch, batch), :]
        targets = tgt_s[at, :]
        st = dot(second, targets, 1, 1)
        sn = [sn_s[j, at, :] for j in range(n_loc)]
        pos = jnp.sum(jnp.where(diag, st, 0.0), axis=1, keepdims=True)
        top = jnp.max(jnp.where(diag, -jnp.inf, st), axis=1, keepdims=True)
        for s in sn:
            top = jnp.maximum(top, jnp.max(s, axis=1, keepdims=True))
        parts = [(st, jnp.where(diag, 0.0, jnp.exp(st - top)))]
        parts += [(s, jnp.exp(s - top)) for s in sn]
        mass = sum(jnp.sum(e, axis=1, keepdims=True) for _, e in parts)
        scale = 1.0 / mass
        parts = [(s, e * scale, jax.nn.sigmoid(pos - s)) for s, e in parts]
        inside = sum(jnp.sum(w * g, axis=1, keepdims=True) for _, w, g in parts)
        penalty = sum(jnp.sum(w * s * s, axis=1, keepdims=True) for s, w, _ in parts)
        slope = sum(jnp.sum(w * g * (1.0 - g), axis=1, keepdims=True) for _, w, g in parts)
        inv = 1.0 / inside
        weight = valid_ref[at, :]
        grads = [
            weight * w * (1.0 + BPREG * (s * s + 2.0 * s - penalty) - g * g * inv)
            for s, w, g in parts
        ]
        gt = grads[0] - jnp.where(diag, weight * slope * inv, 0.0)
        gt_low = gt.astype(BF16)
        into_ref[at, :] = dot(gt_low, targets)
        for j in range(n_loc):
            gn_refs[j][at, :] = grads[j + 1].astype(BF16)
        tgg_s[at, :] = dot(gt_low, second, 0, 0).astype(BF16)
    total = into_ref[...]
    for j in range(n_loc):
        total += dot(gn_refs[j][...], neg_buf[j])
    into_ref[...] = total
    send_ref[...] = dot(pick, tgg_s[...], 0, 0).astype(BF16)


def back_steps(steps, batch, hidden, l, keep_ref, weights, into_ref, res, dq_s, chunks_of):
    loader, res_s = res
    n_loc = dq_s.shape[0]
    wide = into_ref.shape[1]
    lane = iota((batch, wide), 1)
    carry = jnp.zeros((batch, wide), F32)
    for t in reversed(range(steps)):
        at = pl.ds(t * batch, batch)
        g = jnp.where(lane < hidden, into_ref[at, :] + carry, 0.0)
        loader.ready(t)
        z, r, n, qn, p = (res_s[k, at, :] for k in range(5))
        dc = g * (1.0 - z) * (1.0 - n * n)
        da_z = g * (p - n) * z * (1.0 - z)
        da_r = dc * qn * r * (1.0 - r)
        for i, value in enumerate(chunks_of(t, da_z, da_r, dc, dc * r)):
            dq_s[i] = value.astype(BF16)
        dp = g * z
        for j in range(n_loc):
            dp += dot(dq_s[l ^ j], weights[j], 1, 1)
        carry = dp * keep_ref[at, :]
    return jnp.where(lane < hidden, carry, 0.0)


def back_second_kernel(dims, n_in, n_w, l_ref, keep_ref, into_ref, *refs):
    steps, batch, hidden, chunk, n_loc = dims
    res_ref, refs = refs[0], refs[1:]
    in_refs, w_refs, refs = refs[:n_in], refs[n_in : n_in + n_w], refs[n_in + n_w :]
    init_ref, first_ref, refs = refs[0], refs[1], refs[2:]
    ch_refs, refs = refs[: 2 * n_loc], refs[2 * n_loc :]
    dq_s, da_all, dq_all, in_buf, in_sem, w_buf, w_sem, res_s, res_sem = refs
    l = l_ref[0]
    loader = Loader(step_copies(res_ref, res_s, res_sem, steps, batch, False))
    weights = Weights(w_refs, w_buf, w_sem)
    inputs = Weights(in_refs, in_buf, in_sem, l_ref[1] & 1)
    sizes = (hidden, chunk, n_loc, dq_s.shape[2])

    def chunks_of(t, da_z, da_r, da_n, dq_n):
        at = pl.ds(t * batch, batch)
        out = []
        for i in range(n_loc):
            dq = chunk_of(i, (da_z, da_r, dq_n), *sizes)
            same = (i + 1) * chunk <= 2 * hidden
            da = dq if same else chunk_of(i, (da_z, da_r, da_n), *sizes)
            da_all[i, at, :] = da.astype(BF16)
            dq_all[i, at, :] = dq.astype(BF16)
            out.append(dq)
        return out

    init_ref[...] = back_steps(
        steps, batch, hidden, l, keep_ref, weights, into_ref, (loader, res_s), dq_s, chunks_of
    )
    rows = steps * batch
    total = None
    for j in range(n_loc):
        da_low = da_all[l ^ j]
        ch_refs[j][...] = da_low
        ch_refs[n_loc + j][...] = dq_all[l ^ j]
        part = dot(da_low, inputs[j], 1, 1)
        total = part if total is None else total + part
    first_ref[...] = total


def back_first_kernel(dims, n_w, l_ref, keep_ref, into_ref, *refs):
    steps, batch, hidden, chunk, n_loc = dims
    res_ref, refs = refs[0], refs[1:]
    w_refs, refs = refs[:n_w], refs[n_w:]
    init_ref, da_all, refs = refs[0], refs[1], refs[2:]
    ch_refs, refs = refs[:n_loc], refs[n_loc:]
    dq_s, dq_all, bias_s, w_buf, w_sem, res_s, res_sem = refs
    l = l_ref[0]
    loader = Loader(step_copies(res_ref, res_s, res_sem, steps, batch, False))
    weights = Weights(w_refs, w_buf, w_sem)
    wide = into_ref.shape[1]
    sizes = (hidden, chunk, n_loc, dq_s.shape[2])
    bias_s[...] = jnp.zeros(bias_s.shape, F32)

    def chunks_of(t, da_z, da_r, da_n, dq_n):
        at = pl.ds(t * batch, batch)
        for g, da in enumerate((da_z, da_r, da_n)):
            da_all[at, g * wide : (g + 1) * wide] = da.astype(BF16)
        out = [chunk_of(i, (da_z, da_r, dq_n), *sizes) for i in range(n_loc)]
        for i, dq in enumerate(out):
            dq_all[i, at, :] = dq.astype(BF16)
        return out

    init_ref[...] = back_steps(
        steps, batch, hidden, l, keep_ref, weights, into_ref, (loader, res_s), dq_s, chunks_of
    )
    rows = steps * batch
    bias = jnp.sum(da_all[...].astype(F32), axis=0, keepdims=True)
    bias = [bias[:, g * wide : (g + 1) * wide] for g in range(3)]
    for i in range(n_loc):
        bias_s[i, 0:1, :] = chunk_of(i, bias, *sizes)
    for j in range(n_loc):
        ch_refs[j][pl.ds(0, rows), :] = dq_all[l ^ j]
        ch_refs[j][pl.ds(rows, 16), :] = bias_s[l ^ j].astype(BF16)


def return_kernel(slot_ref, land_ref, da_ref, init_ref, init2_ref, send_ref, back_ref):
    rows, cols = da_ref.shape
    wide = init_ref.shape[1]
    pick = low(iota((rows, send_ref.shape[0]), 1) == slot_ref[...])
    send_ref[...] = dot(pick, da_ref[...], 0, 0).astype(BF16)
    land = low(iota((land_ref.shape[0], init_ref.shape[0]), 1) == land_ref[...])
    back_ref[:, :wide] = dot(land, init_ref[...].astype(BF16)).astype(BF16)
    back_ref[:, wide:] = dot(land, init2_ref[...].astype(BF16)).astype(BF16)


def scaled(ref, rows, hidden):
    left = ref[pl.ds(0, rows), :].astype(F32)
    return (left * left[:, hidden + 1 : hidden + 2]).astype(BF16)


def dense_kernel(dims, l_ref, *refs):
    steps, batch, hidden, skip, bias_row, n_loc = dims
    rows = steps * batch
    left_refs, ch_refs = refs[:n_loc], refs[n_loc : 2 * n_loc]
    keep_ref, send_ref, all_s = refs[2 * n_loc :]
    half = keep_ref.shape[0]
    side = l_ref[0] & 1
    total, bias = None, None
    for j in range(n_loc):
        left = left_refs[j][pl.ds(batch, rows), :] if skip else scaled(left_refs[j], rows, hidden)
        part = dot(left, ch_refs[j][pl.ds(0, rows), :], 0, 0)
        total = part if total is None else total + part
        if bias_row is not None:
            extra = ch_refs[j][pl.ds(rows, 16), :].astype(F32)
            bias = extra if bias is None else bias + extra
    all_s[...] = total.astype(BF16)
    if bias_row is not None:
        all_s[pl.ds(bias_row, 16), :] = bias.astype(BF16)
    keep_ref[...] = all_s[pl.ds(pl.multiple_of(side * half, half), half), :]
    send_ref[...] = all_s[pl.ds(pl.multiple_of((1 - side) * half, half), half), :]


def neg_kernel(n_loc, owners, *refs):
    gn_refs, b_refs, out_ref = refs[:n_loc], refs[n_loc : 2 * n_loc], refs[2 * n_loc]
    rows = gn_refs[0].shape[0]
    batch = b_refs[0].shape[0] - rows
    total = None
    for j in range(n_loc):
        part = dot(gn_refs[j][...], b_refs[j][pl.ds(batch, rows), :], 0, 0)
        total = part if total is None else total + part
    own = out_ref.shape[0] // owners
    places = [(g >> 1) + (g & 1) * (owners // 2) for g in range(owners)]
    blocks = [total[p * own : (p + 1) * own, :] for p in places]
    out_ref[...] = jnp.concatenate(blocks, axis=0).astype(BF16)


def on_device(
    carried,
    session_plan,
    item_ids,
    target_ids,
    reset_mask,
    valid_counts,
    negative_ids,
    input_table,
    output_table,
    output_bias,
    hidden_one,
    input_two,
    hidden_two,
    gate_biases,
):
    hidden = carried.shape[2]
    wide = -(-(hidden + 2) // LANES) * LANES
    bias_row = wide - 16
    steps, batch = item_ids.shape
    events = steps * batch
    owners = lax.axis_size("grp")
    n_loc = lax.axis_size("loc")
    grp = lax.axis_index("grp")
    loc = lax.axis_index("loc")
    rows = input_table.shape[0]
    base = grp * rows
    gates = input_table.shape[1]
    chunk = gates // n_loc
    cap = events // owners + events // (2 * owners)
    ccap = 4 * batch // owners
    slots, cslots = owners * cap, owners * ccap
    neg_own = negative_ids.shape[0] // owners // n_loc
    neg_part = owners * neg_own
    l_arr = jnp.stack([loc, grp]).astype(I32)

    cpad = -(-chunk // LANES) * LANES
    gpad = 3 * wide
    w_shape = shape((wide, cpad), BF16)

    g_arr = grp.astype(I32).reshape(1)
    bits = owners.bit_length() - 1

    def padded(w, at, first):
        ins = [l_arr, w] if at is None else [l_arr, w, gate_biases]
        outs = [w_shape]
        if first:
            outs.append(shape((first, cpad), BF16))
            if 2 * first < wide:
                outs.append(shape((wide - first, cpad), BF16))
        return kernel_call(functools.partial(pad_kernel, at, len(ins)), outs, ins, 1)

    def near(x):
        return swap(x, "loc", 1)

    def across(x):
        return swap(x, "loc", 2)

    def join(bit, kept, got, index=g_arr):
        return kernel_call(
            functools.partial(join_kernel, bit),
            [shape((2 * kept.shape[0],) + kept.shape[1:], BF16)],
            [index, kept, got], 1,
        )[0]

    p_one, *one_pieces = padded(hidden_one, (0, bias_row), wide // 8)
    y_one = [across(one_pieces[0])]
    y_one.append(across(after(one_pieces[1], y_one[0])))

    slot_in, slot_tg, slot_pl, packed = kernel_call(
        functools.partial(start_kernel, (owners, rows, cap, batch, ccap)),
        [
            shape((events, 1), I32),
            shape((events, 1), I32),
            shape((batch, 1), I32),
            shape((cslots, 2 * wide), BF16),
        ],
        [
            after(item_ids, p_one).reshape(events, 1),
            target_ids.reshape(events, 1),
            session_plan.reshape(batch, 1),
            carried,
        ],
        0, (), 3,
    )

    def to_owners(x):
        got = lax.all_to_all(
            x.reshape((owners, x.shape[0] // owners) + x.shape[1:]),
            "grp", split_axis=0, concat_axis=0, tiled=True,
        )
        return got.reshape(x.shape)

    got_c = to_owners(after(packed, y_one[0]))

    bias_col = output_bias[:, None]
    mine = lax.dynamic_slice(
        negative_ids.reshape(owners, n_loc, neg_own), (grp, loc, 0), (1, 1, neg_own)
    ).reshape(neg_own) - base
    negs_own = kernel_call(
        gather_neg_kernel,
        [shape((neg_own, wide), BF16)],
        [after(mine, p_one).reshape(neg_own, 1), output_table, bias_col],
    )[0]
    negs_half = negs_own
    for bit in range(1, bits):
        negs_half = join(bit, negs_half, swap(negs_half, "grp", 1 << bit))
    negs = join(0, negs_half, swap(negs_half, "grp", 1))

    place = np.arange(slots)
    turns = -(-cap // ccap)
    place_row = jnp.asarray((place // cap * ccap + place % cap % ccap)[:, None], I32)
    place_turn = jnp.asarray((place % cap // ccap)[:, None], I32)
    base_arr = base.astype(I32).reshape(1)
    ids_shape = shape((slots, 1), I32)
    reply_in, in_ids, land = kernel_call(
        functools.partial(gather_in_kernel, (hidden, turns)),
        [shape((slots, gpad), BF16), ids_shape, shape((cslots, 1), I32)],
        [base_arr, got_c, place_row, place_turn, input_table],
        1, (), 4,
    )
    p_in, h_in = padded(input_two, (1, hidden), wide // 2)
    p_two = padded(hidden_two, None, 0)[0]
    y_in = across(after(h_in, y_one[1]))
    got_rows = to_owners(after(reply_in, negs_half, y_one[1]))
    y_two = across(after(p_two, y_in))
    y_in = [y_in, swap(y_in, "grp", 1)]
    y_neg = across(after(negs, y_two))
    reply_tg, tg_ids = kernel_call(
        functools.partial(gather_tg_kernel, (hidden, turns)),
        [shape((slots, wide), BF16), ids_shape],
        [base_arr, got_c, place_row, place_turn, output_table, bias_col],
        1, (), 3,
    )
    tg_rows = to_owners(after(reply_tg, got_rows))

    def four(own, pieces):
        return [own, near(own), *pieces, *(near(p) for p in pieces)]

    w_one = four(p_one, y_one)

    keep = (1 - reset_mask).astype(F32).reshape(events, 1)
    valid = (jnp.arange(steps, dtype=I32)[:, None] < valid_counts[None, :]).astype(F32)
    valid = (valid / steps).reshape(events, 1)

    res_shape = shape((5, events, wide), F32)
    n_w = 2 + n_loc
    w_scratch = [pltpu.VMEM((n_loc, wide, cpad), BF16), pltpu.SemaphoreType.DMA((n_w,))]
    res_scratch = [pltpu.VMEM((5, events, wide), F32), pltpu.SemaphoreType.DMA((steps,))]
    state_shape = shape(((steps + 1) * batch, wide), BF16)
    q_scratch = pltpu.VMEM((n_loc, batch, cpad), F32)
    dq_scratch = pltpu.VMEM((n_loc, batch, cpad), BF16)
    x_scratch = pltpu.VMEM((n_loc, events, cpad), F32)
    all_scratch = pltpu.VMEM((n_loc, events, cpad), BF16)

    state_a, res_one = kernel_call(
        functools.partial(first_kernel, (steps, batch, hidden, bias_row, n_loc), n_w),
        [state_shape, res_shape],
        [l_arr, keep, slot_in, land, got_c, after(got_rows, reply_tg, negs, y_in[1])] + w_one,
        1,
        w_scratch
        + res_scratch
        + [q_scratch, pltpu.VMEM((n_loc, 16, chunk), F32), pltpu.VMEM((events, gpad), F32)],
        12, n_w, 1,
    )
    w_in = four(p_in, [after(y, state_a) for y in y_in])
    w_two = four(p_two, [after(y_two, state_a)])
    state_b, res_two = kernel_call(
        functools.partial(second_kernel, (steps, batch, hidden, chunk, n_loc), n_w, n_loc),
        [state_shape, res_shape],
        [l_arr, keep, land, got_c, state_a] + w_in + w_two,
        1,
        w_scratch + w_scratch + res_scratch + [q_scratch, x_scratch],
        0, n_w + n_loc, 1,
    )
    y_b = across(after(state_b, y_neg))

    y_neg = after(y_neg, state_b)
    negs = [negs, near(negs), y_neg, near(y_neg)]
    *g_neg, into_second, send_tg = kernel_call(
        functools.partial(score_kernel, (steps, batch, n_loc)),
        [shape((events, neg_part), BF16)] * n_loc
        + [shape((events, wide), F32), shape((slots, wide), BF16)],
        [valid, slot_tg, state_b, tg_rows] + negs,
        0,
        [
            pltpu.VMEM((n_loc, events, neg_part), F32),
            pltpu.VMEM((events, wide), BF16),
            pltpu.VMEM((events, wide), BF16),
            pltpu.VMEM((n_loc, neg_part, wide), BF16),
            pltpu.SemaphoreType.DMA((n_loc,)),
        ],
        12, n_loc,
    )
    init_two, into_first, *ch_two = kernel_call(
        functools.partial(back_second_kernel, (steps, batch, hidden, chunk, n_loc), n_w, n_loc),
        [shape((batch, wide), F32), shape((events, wide), F32)]
        + [shape((events, cpad), BF16)] * (2 * n_loc),
        [l_arr, keep, after(into_second, y_b), res_two] + w_in + w_two,
        1,
        [dq_scratch, all_scratch, all_scratch] + w_scratch + w_scratch + res_scratch,
        17, n_w + n_loc + 1,
    )
    def send_after(chunks, *deps):
        return send_xor([after(c, *deps) for c in chunks], "loc")

    ch_in, ch_two = send_xor(ch_two[:n_loc], "loc"), send_xor(ch_two[n_loc:], "loc")
    y_a = across(after(state_a, into_second))
    got_tg_g = to_owners(send_tg)
    init_one, da_one, *ch_one = kernel_call(
        functools.partial(back_first_kernel, (steps, batch, hidden, chunk, n_loc), n_w),
        [shape((batch, wide), F32), shape((events, gpad), BF16)]
        + [shape((events + 16, cpad), BF16)] * n_loc,
        [l_arr, keep, after(into_first, y_a), res_one] + w_one,
        1,
        [dq_scratch, all_scratch, pltpu.VMEM((n_loc, 16, cpad), F32)] + w_scratch + res_scratch,
        13, n_w + 1,
    )
    send_in, back_c = kernel_call(
        return_kernel,
        [shape((slots, gpad), BF16), shape((cslots, 2 * wide), BF16)],
        [slot_in, land, after(da_one, *ch_in[2:]), init_one, init_two],
        0, (), 3,
    )
    got_in_g = to_owners(after(send_in, got_tg_g))
    ch_one = send_xor(ch_one, "loc")
    g_neg = send_after(g_neg, *ch_one[2:])

    y_a, y_b = after(y_a, send_in), after(y_b, send_in)
    states_a = [state_a, near(state_a), y_a, near(y_a)]
    states_b = [state_b, near(state_b), y_b, near(y_b)]

    neg_grad = kernel_call(
        functools.partial(neg_kernel, n_loc, owners),
        [shape((neg_part, wide), BF16)],
        g_neg + states_b,
        0, (), 2,
    )[0]

    def all_sums(makers, waits):
        def one(make):
            kept, sent = make()
            rest = kept.shape[0]
            for bit in range(bits):
                got = yield sent, 1 << bit
                if bit < bits - 2:
                    rest //= 2
                    kept, sent = kernel_call(
                        functools.partial(split_kernel, bit + 1),
                        [shape((rest, cpad), BF16)] * 2,
                        [g_arr, kept, got],
                        1,
                    )
                else:
                    kept = kernel_call(add_kernel, [shape((rest, cpad), BF16)], [kept, got])[0]
                    sent = kept
            for bit in reversed(range(1, bits - 1)):
                kept = join(bit, kept, (yield kept, 1 << bit))
            got = yield kept, 1
            return kept, got

        chains = [one(make) for make in makers]
        results, asks, before, step = [None] * len(chains), {}, (), 0
        while None in results:
            if step < len(chains):
                asks[step] = next(chains[step])
            wait = tuple(before) + tuple(waits.get(step, lambda: ())())
            answers = {
                k: swap(after(ask[0], *wait) if wait else ask[0], "grp", ask[1])
                for k, ask in asks.items()
            }
            asks, before = {}, list(answers.values())
            for k, answer in answers.items():
                try:
                    asks[k] = chains[k].send(answer)
                except StopIteration as done:
                    results[k] = done.value
            step += 1
        return results

    half_shape = shape((wide // 2, cpad), BF16)

    def product(lefts, chunks, skip, bias_at):
        return kernel_call(
            functools.partial(dense_kernel, (steps, batch, hidden, skip, bias_at, n_loc)),
            [half_shape] * 2,
            [g_arr] + lefts + chunks,
            1, [pltpu.VMEM((wide, cpad), BF16)], 5,
        )

    def finish(parts, bias_row):
        return kernel_call(
            functools.partial(final_kernel, hidden, bias_row),
            [shape((hidden, chunk), F32), shape((1, chunk), F32)],
            [g_arr, *parts],
            1, (), 2,
        )

    own = rows // n_loc
    own_pad = -(-own // 16) * 16

    def table_start(ids, grads, *wait):
        across_cols = grads[0].shape[1]
        full = shape((own_pad, across_cols), F32)
        sent = shape((own_pad, across_cols), BF16)
        mine_p, far_p, near_p = kernel_call(
            functools.partial(table_kernel, own, len(ids)),
            [full, full, shape((2, own_pad, across_cols), BF16)],
            [l_arr] + [i.reshape(1, i.size) for i in ids] + grads,
            1, (), 4,
        )
        total, far_s = kernel_call(
            table_add_kernel, [full, sent], [after(mine_p, *wait), far_p, near(near_p)]
        )
        return total, across(far_s)

    def table_end(pair, cols, parts):
        return kernel_call(
            functools.partial(table_out_kernel, parts), [shape((own, cols), F32)], list(pair)
        )[0]

    sums = {}

    def made(name, *args):
        def make():
            sums[name] = product(*args)
            return sums[name]

        return make

    def start_back():
        sums["back"] = to_owners(after(back_c, got_in_g, sums["one"][0]))
        return ()

    def table_first():
        sums["table"] = table_start([in_ids], [got_in_g], sums["back"])
        return ()

    def table_moved():
        return (sums["table"][1],)

    def bring_back():
        return (sums["back"],)

    in_parts, two_parts, one_parts = all_sums(
        [
            made("in", states_a, ch_in, True, None),
            made("two", states_b, ch_two, False, None),
            made("one", states_a, ch_one, False, bias_row),
        ],
        {1: lambda: tuple(ch_one[2:]), 2: start_back, 3: lambda: (got_in_g,), 4: table_first, 5: bring_back, 6: table_moved},
    )
    got_back = sums["back"]
    got_neg_g = to_owners(after(neg_grad, got_back))
    grad_in, bias_in = finish(in_parts, hidden)
    grad_two, _ = finish(two_parts, hidden)
    grad_one, bias_one = finish(one_parts, bias_row)

    table_in = table_end(sums["table"], gates, 3)
    neg_ids = jnp.broadcast_to(mine[None, :], (owners, neg_own)).reshape(neg_part)
    table_out = table_end(table_start([tg_ids, neg_ids], [got_tg_g, got_neg_g]), wide, 1)
    grad_carried = kernel_call(
        carry_kernel, [shape((2, batch, hidden), F32)], [slot_pl, got_back]
    )[0]
    return (
        table_in,
        table_out[:, :hidden],
        table_out[:, hidden],
        grad_one,
        grad_in,
        grad_two,
        jnp.concatenate([bias_one, bias_in], axis=0),
        grad_carried,
    )


def solution(mesh):
    in_specs = (
        P(None, ("grp", "loc"), None),
        P(("grp", "loc")),
        P(None, ("grp", "loc")),
        P(None, ("grp", "loc")),
        P(None, ("grp", "loc")),
        P(("grp", "loc")),
        P(),
        P("grp", None),
        P("grp", None),
        P("grp"),
        P(None, "loc"),
        P(None, "loc"),
        P(None, "loc"),
        P(None, "loc"),
    )
    out_specs = (
        P(("grp", "loc"), None),
        P(("grp", "loc"), None),
        P(("grp", "loc")),
        P(None, "loc"),
        P(None, "loc"),
        P(None, "loc"),
        P(None, "loc"),
        P(None, ("grp", "loc"), None),
    )
    return jax.shard_map(
        on_device, mesh=mesh, in_specs=in_specs, out_specs=out_specs, check_vma=False
    )
```

```python
import functools

import jax
import jax.numpy as jnp
import numpy as np
from jax import lax
from jax.experimental import pallas as pl
from jax.experimental.pallas import tpu as pltpu
from jax.sharding import PartitionSpec as P

BPREG = 1.0
BF16 = jnp.bfloat16
F32 = jnp.float32
I32 = jnp.int32
LANES = 128
VMEM_LIMIT = 48 << 20


def swap(x, axis, bit):
    n = lax.axis_size(axis)
    return lax.ppermute(x, axis, [(i, i ^ bit) for i in range(n)])


def gather_xor(x, axis):
    blocks = {0: x}
    bit = lax.axis_size(axis) // 2
    while bit:
        for k in list(blocks):
            blocks[k | bit] = swap(blocks[k], axis, bit)
        bit //= 2
    return [blocks[k] for k in range(len(blocks))]


def send_xor(chunks, axis):
    return [chunks[0]] + [swap(chunks[j], axis, j) for j in range(1, len(chunks))]


def kernel_call(body, outs, ins, smem=0, scratch=(), us=1, left=0, left_outs=0):
    vmem, place = pl.BlockSpec(memory_space=pltpu.VMEM), pl.BlockSpec(memory_space=pl.ANY)
    nbytes = sum(a.size * a.dtype.itemsize for a in ins)
    nbytes += sum(int(functools.reduce(lambda a, b: a * b, o.shape)) * o.dtype.itemsize for o in outs)
    return pl.pallas_call(
        body,
        out_shape=outs,
        in_specs=[pl.BlockSpec(memory_space=pltpu.SMEM)] * smem
        + [vmem] * (len(ins) - smem - left)
        + [place] * left,
        out_specs=[vmem] * (len(outs) - left_outs) + [place] * left_outs,
        scratch_shapes=list(scratch),
        compiler_params=pltpu.CompilerParams(vmem_limit_bytes=VMEM_LIMIT),
        cost_estimate=pl.CostEstimate(flops=us * 10**9, bytes_accessed=nbytes, transcendentals=0),
    )(*ins)


def after(x, *deps):
    return lax.optimization_barrier((x,) + deps)[0]


def shape(dims, dtype):
    return jax.ShapeDtypeStruct(dims, dtype)


def iota(dims, dim):
    return lax.broadcasted_iota(I32, dims, dim)


def dot(a, b, ca=1, cb=0):
    return lax.dot_general(a, b, (((ca,), (cb,)), ((), ())), preferred_element_type=F32)


class Loader:
    def __init__(self, copies):
        self.copies = copies
        self.waited = set()
        for group in copies.values():
            for copy in group:
                copy.start()

    def ready(self, slot):
        if slot not in self.waited:
            self.waited.add(slot)
            for copy in self.copies[slot]:
                copy.wait()


class Weights(Loader):
    def __init__(self, refs, buf, sem, side=None):
        n = buf.shape[0]
        pieces = (len(refs) - n // 2) // (n // 2)
        copies, k = {}, 0
        for j in range(n):
            row, copies[j] = 0, []
            for _ in range(1 if j < n // 2 else pieces):
                size = refs[k].shape[0]
                at = row
                if side is not None and j >= n // 2:
                    at = pl.multiple_of((side if row == 0 else 1 - side) * size, size)
                part = buf.at[j, pl.ds(at, size), :]
                copies[j].append(pltpu.make_async_copy(refs[k], part, sem.at[k]))
                row, k = row + size, k + 1
        self.buf = buf
        super().__init__(copies)

    def __getitem__(self, j):
        self.ready(j)
        return self.buf[j]


def step_copies(ref, buf, sem, steps, batch, out):
    copies = {}
    for t in reversed(range(steps)):
        at = (slice(None), pl.ds(t * batch, batch), slice(None))
        pair = (buf.at[at], ref.at[at]) if out else (ref.at[at], buf.at[at])
        copies[t] = [pltpu.make_async_copy(*pair, sem.at[t])]
    return copies


def low(cond):
    return jnp.where(cond, 1.0, 0.0).astype(BF16)


def start_kernel(dims, in_ref, tg_ref, plan_ref, carried_ref, s_in, s_tg, s_pl, out_ref):
    owners, rows, cap, batch, ccap = dims
    hidden = carried_ref.shape[2]
    wide = out_ref.shape[1] // 2
    spare = wide - hidden

    def place(ids, span):
        n = ids.shape[0]
        owner_i = iota((n, owners), 1)
        member = (ids >= owner_i * span) & (ids < (owner_i + 1) * span)
        earlier = low(iota((n, n), 1) < iota((n, n), 0))
        before = dot(earlier, low(member))
        rank = jnp.sum(jnp.where(member, before, 0.0), axis=1, keepdims=True).astype(I32)
        owner = jnp.sum(jnp.where(member, owner_i, 0).astype(F32), axis=1, keepdims=True).astype(I32)
        return owner, rank

    def digits(owner, rank, first, value):
        n = owner.shape[0]
        turn = sum((rank >= k * ccap).astype(I32) for k in range(1, -(-cap // ccap)))
        row = owner * ccap + rank - turn * ccap
        hit = low(iota((n, owners * ccap), 1) == row)
        lane = iota((n, LANES), 1)
        high, rest = (value >> 8).astype(F32), (value & 255).astype(F32)
        at = first + 2 * turn
        code = jnp.where(lane == at, high, jnp.where(lane == at + 1, rest, 0.0))
        return dot(hit, code.astype(BF16), 0, 0)

    o_in, r_in = place(in_ref[...], rows)
    o_tg, r_tg = place(tg_ref[...], rows)
    o_pl, r_pl = place(plan_ref[...], batch)
    s_in[...] = o_in * cap + r_in
    s_tg[...] = o_tg * cap + r_tg
    s_pl[...] = o_pl * ccap + r_pl
    turns = -(-cap // ccap)
    code = digits(o_in, r_in, 0, in_ref[...] + 1)
    code += digits(o_tg, r_tg, 2 * turns, tg_ref[...] + 1)
    code += digits(o_pl, r_pl, 4 * turns, plan_ref[...] - o_pl * batch + 1)
    pick = low(iota((batch, owners * ccap), 1) == o_pl * ccap + r_pl)
    parts = [dot(pick, carried_ref[k].astype(BF16), 0, 0) for k in range(2)]
    parts = [parts[0], code[:, :spare], parts[1], jnp.zeros((owners * ccap, spare), F32)]
    out_ref[...] = jnp.concatenate(parts, axis=1).astype(BF16)


def decode(got_ref, row_ref, turn_ref, hidden, first):
    wide = got_ref.shape[1] // 2
    block = got_ref[:, wide - LANES : wide]
    n = row_ref.shape[0]
    found = dot(low(iota((n, block.shape[0]), 1) == row_ref[...]), block)
    at = hidden - wide + LANES + first + 2 * turn_ref[...]
    lane = iota((n, LANES), 1)
    worth = jnp.where(lane == at, 256.0, jnp.where(lane == at + 1, 1.0, 0.0))
    return jnp.sum(found * worth, axis=1, keepdims=True).astype(I32)


def landing(land_ref, got_ref, layer, batch, hidden):
    wide = got_ref.shape[1] // 2
    land = low(iota((land_ref.shape[0], batch), 1) == land_ref[...])
    moved = dot(land, got_ref[:, layer * wide : (layer + 1) * wide], 0, 0)
    return jnp.where(iota(moved.shape, 1) < hidden, moved, 0.0)


def cut(hidden, chunk, n_loc):
    gates = []
    for g in range(3):
        parts = []
        for i in range(n_loc):
            lo, hi = max(g * hidden, i * chunk), min((g + 1) * hidden, (i + 1) * chunk)
            if lo < hi:
                parts.append((i, lo - i * chunk, hi - i * chunk))
        gates.append(parts)
    return gates


def gate_of(g, chunks, hidden, chunk, wide):
    parts = [chunks[i][:, lo:hi] for i, lo, hi in cut(hidden, chunk, len(chunks))[g]]
    pad = jnp.zeros((parts[0].shape[0], wide - hidden), parts[0].dtype)
    return jnp.concatenate(parts + [pad], axis=1)


def chunk_of(i, gates, hidden, chunk, n_loc, cpad):
    parts = []
    for g, places in enumerate(cut(hidden, chunk, n_loc)):
        for k, lo, hi in places:
            if k == i:
                at = i * chunk + lo - g * hidden
                parts.append(gates[g][:, at : at + hi - lo])
    pad = jnp.zeros((parts[0].shape[0], cpad - chunk), parts[0].dtype)
    return jnp.concatenate(parts + [pad], axis=1)


def extend(value, keep, hidden):
    lane = iota(value.shape, 1)
    return jnp.where(lane == hidden, 1.0, jnp.where(lane == hidden + 1, keep, value)).astype(BF16)


def run_steps(steps, batch, hidden, l, keep_ref, weights, gates_of, start, state_ref, res, q_s):
    res_ref, res_s, res_sem = res
    n_loc = q_s.shape[0]
    wide = start.shape[1]
    lane = iota((batch, wide), 1)
    prev = start
    writes = step_copies(res_ref, res_s, res_sem, steps, batch, True)
    for t in range(steps):
        at = pl.ds(t * batch, batch)
        keep = keep_ref[at, :]
        state_ref[at, :] = extend(prev, keep, hidden)
        p = prev * keep
        p_low = p.astype(BF16)
        for j in range(n_loc):
            q_s[l ^ j] = dot(p_low, weights[j])
        in_z, in_r, in_n, qn = gates_of(t, [q_s[i] for i in range(n_loc)])
        z = jax.nn.sigmoid(in_z)
        r = jax.nn.sigmoid(in_r)
        n = jnp.tanh(in_n + r * qn)
        prev = jnp.where(lane < hidden, n + z * (p - n), 0.0)
        for k, val in enumerate((z, r, n, qn, p)):
            res_s[k, at, :] = val
        writes[t][0].start()
    state_ref[pl.ds(steps * batch, batch), :] = extend(prev, 0.0, hidden)
    for t in range(steps):
        writes[t][0].wait()


def pad_kernel(at, n_in, l_ref, w_ref, *refs):
    refs, outs = refs[: n_in - 2], refs[n_in - 2 :]
    out_ref = outs[0]
    rows, cols = w_ref.shape
    out_ref[...] = jnp.zeros(out_ref.shape, BF16)
    out_ref[:rows, :cols] = w_ref[...]
    if at is not None:
        which, row = at
        tile = row // 16 * 16
        here = (iota((16, cols), 0) == row - tile).astype(F32)
        old = out_ref[tile : tile + 16, :cols].astype(F32)
        extra = refs[0][which : which + 1, :].astype(F32)
        out_ref[tile : tile + 16, :cols] = (old + here * extra).astype(BF16)
    if len(outs) == 1:
        pass
    elif len(outs) == 2:
        half = outs[1].shape[0]
        side = l_ref[1] & 1
        outs[1][...] = out_ref[pl.ds(pl.multiple_of(side * half, half), half), :]
    else:
        first = outs[1].shape[0]
        outs[1][...] = out_ref[:first, :]
        outs[2][...] = out_ref[first:, :]


def gather_in_kernel(dims, base_ref, got_ref, row_ref, turn_ref, table_ref, out_ref, ids_ref, land_ref):
    hidden, turns = dims
    rows, cols = table_ref.shape
    wide = got_ref.shape[1] // 2
    ids = decode(got_ref, row_ref, turn_ref, hidden, 0) - 1 - base_ref[0]
    ids_ref[...] = ids
    at = hidden - wide + LANES + 4 * turns + 1
    land = got_ref[:, wide - LANES : wide].astype(F32)[:, at : at + 1]
    land_ref[...] = land.astype(I32) - 1
    pick = low(iota((ids.shape[0], rows), 1) == ids)
    found = dot(pick, table_ref[...])
    for g in range(3):
        part = found[:, g * hidden : (g + 1) * hidden]
        pad = jnp.zeros((part.shape[0], wide - hidden), F32)
        out_ref[:, g * wide : (g + 1) * wide] = jnp.concatenate([part, pad], axis=1).astype(BF16)


def biased_rows(ids, table_ref, bias_ref, wide):
    n = ids.shape[0]
    rows, cols = table_ref.shape
    pick = low(iota((n, rows), 1) == ids)
    parts = [dot(pick, table_ref[...]), dot(pick, bias_ref[...])[:, :1]]
    parts.append(jnp.zeros((n, wide - cols - 1), F32))
    return jnp.concatenate(parts, axis=1).astype(BF16)


def gather_tg_kernel(dims, base_ref, got_ref, row_ref, turn_ref, table_ref, bias_ref, out_ref, ids_ref):
    hidden, turns = dims
    ids = decode(got_ref, row_ref, turn_ref, hidden, 2 * turns) - 1 - base_ref[0]
    ids_ref[...] = ids
    out_ref[...] = biased_rows(ids, table_ref, bias_ref, out_ref.shape[1])


def gather_neg_kernel(ids_ref, table_ref, bias_ref, out_ref):
    out_ref[...] = biased_rows(ids_ref[...], table_ref, bias_ref, out_ref.shape[1])


def table_kernel(own, pairs, l_ref, *refs):
    mine_ref, far_ref, near_ref = refs[2 * pairs :]
    pad = mine_ref.shape[0]
    l = l_ref[0]
    for j, (ref, at) in enumerate(((mine_ref, None), (near_ref, 0), (far_ref, None), (near_ref, 1))):
        part = None
        for ids_ref, got_ref in zip(refs[:pairs], refs[pairs : 2 * pairs]):
            row = iota((pad, ids_ref.shape[1]), 0)
            hit = (row < own) & (row + (l ^ j) * own == ids_ref[...])
            term = dot(low(hit), got_ref[...])
            part = term if part is None else part + term
        if at is None:
            ref[...] = part
        else:
            ref[at, :, :] = part.astype(BF16)


def table_add_kernel(mine_ref, far_ref, got_ref, sum_ref, send_ref):
    sum_ref[...] = mine_ref[...] + got_ref[0].astype(F32)
    send_ref[...] = (far_ref[...] + got_ref[1].astype(F32)).astype(BF16)


def table_out_kernel(parts, sum_ref, got_ref, out_ref):
    rows, cols = out_ref.shape
    total = (sum_ref[...] + got_ref[...].astype(F32))[:rows]
    wide = total.shape[1] // parts
    size = cols // parts
    split = [total[:, g * wide : g * wide + size] for g in range(parts)]
    out_ref[...] = jnp.concatenate(split, axis=1)


def carry_kernel(slot_ref, got_ref, out_ref):
    hidden = out_ref.shape[2]
    wide = got_ref.shape[1] // 2
    pick = low(iota((slot_ref.shape[0], got_ref.shape[0]), 1) == slot_ref[...])
    back = dot(pick, got_ref[...])
    out_ref[0] = back[:, :hidden]
    out_ref[1] = back[:, wide : wide + hidden]


def split_kernel(bit, l_ref, a_ref, b_ref, keep_ref, send_ref):
    half = keep_ref.shape[0]
    side = (l_ref[0] >> bit) & 1
    for ref, at in ((keep_ref, side), (send_ref, 1 - side)):
        rows = pl.ds(pl.multiple_of(at * half, half), half)
        ref[...] = (a_ref[rows, :].astype(F32) + b_ref[rows, :].astype(F32)).astype(BF16)


def add_kernel(a_ref, b_ref, out_ref):
    out_ref[...] = (a_ref[...].astype(F32) + b_ref[...].astype(F32)).astype(BF16)


def join_kernel(bit, l_ref, a_ref, b_ref, out_ref):
    half = a_ref.shape[0]
    side = (l_ref[0] >> bit) & 1
    for ref, at in ((a_ref, side), (b_ref, 1 - side)):
        out_ref[pl.ds(pl.multiple_of(at * half, half), half), :] = ref[...]


def final_kernel(hidden, bias_row, l_ref, a_ref, b_ref, out_ref, bias_ref):
    side = l_ref[0] & 1
    cols = out_ref.shape[1]
    half = a_ref.shape[0]
    at = (bias_row - half) // 16 * 16
    for first, second, when in ((a_ref, b_ref, 0), (b_ref, a_ref, 1)):

        @pl.when(side == when)
        def _():
            out_ref[:half, :] = first[...].astype(F32)[:, :cols]
            out_ref[half:, :] = second[...].astype(F32)[: hidden - half, :cols]
            row = bias_row - half - at
            bias_ref[...] = second[at : at + 16, :].astype(F32)[row : row + 1, :cols]


def first_kernel(dims, n_w, l_ref, keep_ref, slot_ref, land_ref, got_ref, rows_ref, *refs):
    steps, batch, hidden, bias_row, n_loc = dims
    w_refs, refs = refs[:n_w], refs[n_w:]
    state_ref, res_ref, w_buf, w_sem, res_s, res_sem, q_s, b_s, x_s = refs
    wide = res_s.shape[2]
    l = l_ref[0]
    weights = Weights(w_refs, w_buf, w_sem)
    chunk = b_s.shape[2]
    pick = low(iota((steps * batch, rows_ref.shape[0]), 1) == slot_ref[...])
    rows = dot(pick, rows_ref[...])
    moved = landing(land_ref, got_ref, 0, batch, hidden)
    for j in range(n_loc):
        weights.ready(j)
        b_s[l ^ j] = w_buf[j, bias_row : bias_row + 16, :].astype(F32)[:, :chunk]
    bias = [b_s[i][0:1, :] for i in range(n_loc)]
    bias = [gate_of(g, bias, hidden, chunk, wide) for g in range(3)]
    x_s[...] = rows + jnp.concatenate(bias, axis=1)

    def gates_of(t, q):
        x = x_s[pl.ds(t * batch, batch), :]
        gates = [gate_of(g, q, hidden, chunk, wide) for g in range(3)]
        return x[:, :wide] + gates[0], x[:, wide : 2 * wide] + gates[1], x[:, 2 * wide :], gates[2]

    run_steps(
        steps, batch, hidden, l, keep_ref, weights, gates_of, moved, state_ref,
        (res_ref, res_s, res_sem), q_s,
    )


def second_kernel(dims, n_in, n_w, l_ref, keep_ref, land_ref, got_ref, below_ref, *refs):
    steps, batch, hidden, chunk, n_loc = dims
    in_refs, w_refs, refs = refs[:n_in], refs[n_in : n_in + n_w], refs[n_in + n_w :]
    state_ref, res_ref, in_buf, in_sem, w_buf, w_sem, res_s, res_sem, q_s, x_s = refs
    wide = res_s.shape[2]
    l = l_ref[0]
    inputs = Weights(in_refs, in_buf, in_sem, l_ref[1] & 1)
    weights = Weights(w_refs, w_buf, w_sem)
    moved = landing(land_ref, got_ref, 1, batch, hidden)
    below = below_ref[pl.ds(batch, steps * batch), :]
    for j in range(n_loc):
        x_s[l ^ j] = dot(below, inputs[j])

    def gates_of(t, q):
        x = [x_s[i, pl.ds(t * batch, batch), :] for i in range(n_loc)]
        both = [x[i] + q[i] for i in range(n_loc)]
        sizes = (hidden, chunk, wide)
        return (
            gate_of(0, both, *sizes), gate_of(1, both, *sizes), gate_of(2, x, *sizes), gate_of(2, q, *sizes)
        )

    run_steps(
        steps, batch, hidden, l, keep_ref, weights, gates_of, moved, state_ref,
        (res_ref, res_s, res_sem), q_s,
    )


def score_kernel(dims, valid_ref, slot_ref, state_ref, tg_ref, *refs):
    steps, batch, n_loc = dims
    rows = steps * batch
    neg_refs, refs = refs[:n_loc], refs[n_loc:]
    gn_refs, into_ref, send_ref = refs[:n_loc], refs[n_loc], refs[n_loc + 1]
    sn_s, tgt_s, tgg_s, neg_buf, neg_sem = refs[n_loc + 2 :]
    negs = Loader(
        {
            j: [pltpu.make_async_copy(neg_refs[j], neg_buf.at[j], neg_sem.at[j])]
            for j in range(n_loc)
        }
    )
    diag = iota((batch, batch), 0) == iota((batch, batch), 1)
    slots = tg_ref.shape[0]
    pick = low(iota((rows, slots), 1) == slot_ref[...])
    tgt_s[...] = dot(pick, tg_ref[...]).astype(BF16)
    every = state_ref[pl.ds(batch, rows), :]
    for j in range(n_loc):
        negs.ready(j)
        sn_s[j] = dot(every, neg_buf[j], 1, 1)
    for t in range(steps):
        at = pl.ds(t * batch, batch)
        second = state_ref[pl.ds((t + 1) * batch, batch), :]
        targets = tgt_s[at, :]
        st = dot(second, targets, 1, 1)
        sn = [sn_s[j, at, :] for j in range(n_loc)]
        pos = jnp.sum(jnp.where(diag, st, 0.0), axis=1, keepdims=True)
        top = jnp.max(jnp.where(diag, -jnp.inf, st), axis=1, keepdims=True)
        for s in sn:
            top = jnp.maximum(top, jnp.max(s, axis=1, keepdims=True))
        parts = [(st, jnp.where(diag, 0.0, jnp.exp(st - top)))]
        parts += [(s, jnp.exp(s - top)) for s in sn]
        mass = sum(jnp.sum(e, axis=1, keepdims=True) for _, e in parts)
        scale = 1.0 / mass
        parts = [(s, e * scale, jax.nn.sigmoid(pos - s)) for s, e in parts]
        inside = sum(jnp.sum(w * g, axis=1, keepdims=True) for _, w, g in parts)
        penalty = sum(jnp.sum(w * s * s, axis=1, keepdims=True) for s, w, _ in parts)
        slope = sum(jnp.sum(w * g * (1.0 - g), axis=1, keepdims=True) for _, w, g in parts)
        inv = 1.0 / inside
        weight = valid_ref[at, :]
        grads = [
            weight * w * (1.0 + BPREG * (s * s + 2.0 * s - penalty) - g * g * inv)
            for s, w, g in parts
        ]
        gt = grads[0] - jnp.where(diag, weight * slope * inv, 0.0)
        gt_low = gt.astype(BF16)
        into_ref[at, :] = dot(gt_low, targets)
        for j in range(n_loc):
            gn_refs[j][at, :] = grads[j + 1].astype(BF16)
        tgg_s[at, :] = dot(gt_low, second, 0, 0).astype(BF16)
    total = into_ref[...]
    for j in range(n_loc):
        total += dot(gn_refs[j][...], neg_buf[j])
    into_ref[...] = total
    send_ref[...] = dot(pick, tgg_s[...], 0, 0).astype(BF16)


def back_steps(steps, batch, hidden, l, keep_ref, weights, into_ref, res, dq_s, chunks_of):
    loader, res_s = res
    n_loc = dq_s.shape[0]
    wide = into_ref.shape[1]
    lane = iota((batch, wide), 1)
    carry = jnp.zeros((batch, wide), F32)
    for t in reversed(range(steps)):
        at = pl.ds(t * batch, batch)
        g = jnp.where(lane < hidden, into_ref[at, :] + carry, 0.0)
        loader.ready(t)
        z, r, n, qn, p = (res_s[k, at, :] for k in range(5))
        dc = g * (1.0 - z) * (1.0 - n * n)
        da_z = g * (p - n) * z * (1.0 - z)
        da_r = dc * qn * r * (1.0 - r)
        for i, value in enumerate(chunks_of(t, da_z, da_r, dc, dc * r)):
            dq_s[i] = value.astype(BF16)
        dp = g * z
        for j in range(n_loc):
            dp += dot(dq_s[l ^ j], weights[j], 1, 1)
        carry = dp * keep_ref[at, :]
    return jnp.where(lane < hidden, carry, 0.0)


def back_second_kernel(dims, n_in, n_w, l_ref, keep_ref, into_ref, *refs):
    steps, batch, hidden, chunk, n_loc = dims
    res_ref, refs = refs[0], refs[1:]
    in_refs, w_refs, refs = refs[:n_in], refs[n_in : n_in + n_w], refs[n_in + n_w :]
    init_ref, first_ref, refs = refs[0], refs[1], refs[2:]
    ch_refs, refs = refs[: 2 * n_loc], refs[2 * n_loc :]
    dq_s, da_all, dq_all, in_buf, in_sem, w_buf, w_sem, res_s, res_sem = refs
    l = l_ref[0]
    loader = Loader(step_copies(res_ref, res_s, res_sem, steps, batch, False))
    weights = Weights(w_refs, w_buf, w_sem)
    inputs = Weights(in_refs, in_buf, in_sem, l_ref[1] & 1)
    sizes = (hidden, chunk, n_loc, dq_s.shape[2])

    def chunks_of(t, da_z, da_r, da_n, dq_n):
        at = pl.ds(t * batch, batch)
        out = []
        for i in range(n_loc):
            dq = chunk_of(i, (da_z, da_r, dq_n), *sizes)
            same = (i + 1) * chunk <= 2 * hidden
            da = dq if same else chunk_of(i, (da_z, da_r, da_n), *sizes)
            da_all[i, at, :] = da.astype(BF16)
            dq_all[i, at, :] = dq.astype(BF16)
            out.append(dq)
        return out

    init_ref[...] = back_steps(
        steps, batch, hidden, l, keep_ref, weights, into_ref, (loader, res_s), dq_s, chunks_of
    )
    rows = steps * batch
    total = None
    for j in range(n_loc):
        da_low = da_all[l ^ j]
        ch_refs[j][...] = da_low
        ch_refs[n_loc + j][...] = dq_all[l ^ j]
        part = dot(da_low, inputs[j], 1, 1)
        total = part if total is None else total + part
    first_ref[...] = total


def back_first_kernel(dims, n_w, l_ref, keep_ref, into_ref, *refs):
    steps, batch, hidden, chunk, n_loc = dims
    res_ref, refs = refs[0], refs[1:]
    w_refs, refs = refs[:n_w], refs[n_w:]
    init_ref, da_all, refs = refs[0], refs[1], refs[2:]
    ch_refs, refs = refs[:n_loc], refs[n_loc:]
    dq_s, dq_all, bias_s, w_buf, w_sem, res_s, res_sem = refs
    l = l_ref[0]
    loader = Loader(step_copies(res_ref, res_s, res_sem, steps, batch, False))
    weights = Weights(w_refs, w_buf, w_sem)
    wide = into_ref.shape[1]
    sizes = (hidden, chunk, n_loc, dq_s.shape[2])
    bias_s[...] = jnp.zeros(bias_s.shape, F32)

    def chunks_of(t, da_z, da_r, da_n, dq_n):
        at = pl.ds(t * batch, batch)
        for g, da in enumerate((da_z, da_r, da_n)):
            da_all[at, g * wide : (g + 1) * wide] = da.astype(BF16)
        out = [chunk_of(i, (da_z, da_r, dq_n), *sizes) for i in range(n_loc)]
        for i, dq in enumerate(out):
            dq_all[i, at, :] = dq.astype(BF16)
        return out

    init_ref[...] = back_steps(
        steps, batch, hidden, l, keep_ref, weights, into_ref, (loader, res_s), dq_s, chunks_of
    )
    rows = steps * batch
    bias = jnp.sum(da_all[...].astype(F32), axis=0, keepdims=True)
    bias = [bias[:, g * wide : (g + 1) * wide] for g in range(3)]
    for i in range(n_loc):
        bias_s[i, 0:1, :] = chunk_of(i, bias, *sizes)
    for j in range(n_loc):
        ch_refs[j][pl.ds(0, rows), :] = dq_all[l ^ j]
        ch_refs[j][pl.ds(rows, 16), :] = bias_s[l ^ j].astype(BF16)


def return_kernel(slot_ref, land_ref, da_ref, init_ref, init2_ref, send_ref, back_ref):
    rows, cols = da_ref.shape
    wide = init_ref.shape[1]
    pick = low(iota((rows, send_ref.shape[0]), 1) == slot_ref[...])
    send_ref[...] = dot(pick, da_ref[...], 0, 0).astype(BF16)
    land = low(iota((land_ref.shape[0], init_ref.shape[0]), 1) == land_ref[...])
    back_ref[:, :wide] = dot(land, init_ref[...].astype(BF16)).astype(BF16)
    back_ref[:, wide:] = dot(land, init2_ref[...].astype(BF16)).astype(BF16)


def scaled(ref, rows, hidden):
    left = ref[pl.ds(0, rows), :].astype(F32)
    return (left * left[:, hidden + 1 : hidden + 2]).astype(BF16)


def dense_kernel(dims, l_ref, *refs):
    steps, batch, hidden, skip, bias_row, n_loc = dims
    rows = steps * batch
    left_refs, ch_refs = refs[:n_loc], refs[n_loc : 2 * n_loc]
    keep_ref, send_ref, all_s = refs[2 * n_loc :]
    half = keep_ref.shape[0]
    side = l_ref[0] & 1
    total, bias = None, None
    for j in range(n_loc):
        left = left_refs[j][pl.ds(batch, rows), :] if skip else scaled(left_refs[j], rows, hidden)
        part = dot(left, ch_refs[j][pl.ds(0, rows), :], 0, 0)
        total = part if total is None else total + part
        if bias_row is not None:
            extra = ch_refs[j][pl.ds(rows, 16), :].astype(F32)
            bias = extra if bias is None else bias + extra
    all_s[...] = total.astype(BF16)
    if bias_row is not None:
        all_s[pl.ds(bias_row, 16), :] = bias.astype(BF16)
    keep_ref[...] = all_s[pl.ds(pl.multiple_of(side * half, half), half), :]
    send_ref[...] = all_s[pl.ds(pl.multiple_of((1 - side) * half, half), half), :]


def neg_kernel(n_loc, owners, *refs):
    gn_refs, b_refs, out_ref = refs[:n_loc], refs[n_loc : 2 * n_loc], refs[2 * n_loc]
    rows = gn_refs[0].shape[0]
    batch = b_refs[0].shape[0] - rows
    total = None
    for j in range(n_loc):
        part = dot(gn_refs[j][...], b_refs[j][pl.ds(batch, rows), :], 0, 0)
        total = part if total is None else total + part
    own = out_ref.shape[0] // owners
    places = [(g >> 1) + (g & 1) * (owners // 2) for g in range(owners)]
    blocks = [total[p * own : (p + 1) * own, :] for p in places]
    out_ref[...] = jnp.concatenate(blocks, axis=0).astype(BF16)


def on_device(
    carried,
    session_plan,
    item_ids,
    target_ids,
    reset_mask,
    valid_counts,
    negative_ids,
    input_table,
    output_table,
    output_bias,
    hidden_one,
    input_two,
    hidden_two,
    gate_biases,
):
    hidden = carried.shape[2]
    wide = -(-(hidden + 2) // LANES) * LANES
    bias_row = wide - 16
    steps, batch = item_ids.shape
    events = steps * batch
    owners = lax.axis_size("grp")
    n_loc = lax.axis_size("loc")
    grp = lax.axis_index("grp")
    loc = lax.axis_index("loc")
    rows = input_table.shape[0]
    base = grp * rows
    gates = input_table.shape[1]
    chunk = gates // n_loc
    cap = events // owners + events // (2 * owners)
    ccap = 4 * batch // owners
    slots, cslots = owners * cap, owners * ccap
    neg_own = negative_ids.shape[0] // owners // n_loc
    neg_part = owners * neg_own
    l_arr = jnp.stack([loc, grp]).astype(I32)

    cpad = -(-chunk // LANES) * LANES
    gpad = 3 * wide
    w_shape = shape((wide, cpad), BF16)

    g_arr = grp.astype(I32).reshape(1)
    bits = owners.bit_length() - 1

    def padded(w, at, first):
        ins = [l_arr, w] if at is None else [l_arr, w, gate_biases]
        outs = [w_shape]
        if first:
            outs.append(shape((first, cpad), BF16))
            if 2 * first < wide:
                outs.append(shape((wide - first, cpad), BF16))
        return kernel_call(functools.partial(pad_kernel, at, len(ins)), outs, ins, 1)

    def near(x):
        return swap(x, "loc", 1)

    def across(x):
        return swap(x, "loc", 2)

    def join(bit, kept, got, index=g_arr):
        return kernel_call(
            functools.partial(join_kernel, bit),
            [shape((2 * kept.shape[0],) + kept.shape[1:], BF16)],
            [index, kept, got], 1,
        )[0]

    p_one, *one_pieces = padded(hidden_one, (0, bias_row), wide // 8)
    y_one = [across(one_pieces[0])]
    y_one.append(across(after(one_pieces[1], y_one[0])))

    slot_in, slot_tg, slot_pl, packed = kernel_call(
        functools.partial(start_kernel, (owners, rows, cap, batch, ccap)),
        [
            shape((events, 1), I32),
            shape((events, 1), I32),
            shape((batch, 1), I32),
            shape((cslots, 2 * wide), BF16),
        ],
        [
            after(item_ids, p_one).reshape(events, 1),
            target_ids.reshape(events, 1),
            session_plan.reshape(batch, 1),
            carried,
        ],
        0, (), 3,
    )

    def to_owners(x):
        got = lax.all_to_all(
            x.reshape((owners, x.shape[0] // owners) + x.shape[1:]),
            "grp", split_axis=0, concat_axis=0, tiled=True,
        )
        return got.reshape(x.shape)

    got_c = to_owners(after(packed, y_one[0]))

    bias_col = output_bias[:, None]
    mine = lax.dynamic_slice(
        negative_ids.reshape(owners, n_loc, neg_own), (grp, loc, 0), (1, 1, neg_own)
    ).reshape(neg_own) - base
    negs_own = kernel_call(
        gather_neg_kernel,
        [shape((neg_own, wide), BF16)],
        [after(mine, p_one).reshape(neg_own, 1), output_table, bias_col],
    )[0]
    negs_half = negs_own
    for bit in range(1, bits):
        negs_half = join(bit, negs_half, swap(negs_half, "grp", 1 << bit))
    negs = join(0, negs_half, swap(negs_half, "grp", 1))

    place = np.arange(slots)
    turns = -(-cap // ccap)
    place_row = jnp.asarray((place // cap * ccap + place % cap % ccap)[:, None], I32)
    place_turn = jnp.asarray((place % cap // ccap)[:, None], I32)
    base_arr = base.astype(I32).reshape(1)
    ids_shape = shape((slots, 1), I32)
    reply_in, in_ids, land = kernel_call(
        functools.partial(gather_in_kernel, (hidden, turns)),
        [shape((slots, gpad), BF16), ids_shape, shape((cslots, 1), I32)],
        [base_arr, got_c, place_row, place_turn, input_table],
        1, (), 4,
    )
    p_in, h_in = padded(input_two, (1, hidden), wide // 2)
    p_two = padded(hidden_two, None, 0)[0]
    y_in = across(after(h_in, y_one[1]))
    got_rows = to_owners(after(reply_in, negs_half, y_one[1]))
    y_two = across(after(p_two, y_in))
    y_in = [y_in, swap(y_in, "grp", 1)]
    y_neg = across(after(negs, y_two))
    reply_tg, tg_ids = kernel_call(
        functools.partial(gather_tg_kernel, (hidden, turns)),
        [shape((slots, wide), BF16), ids_shape],
        [base_arr, got_c, place_row, place_turn, output_table, bias_col],
        1, (), 3,
    )
    tg_rows = to_owners(after(reply_tg, got_rows))

    def four(own, pieces):
        return [own, near(own), *pieces, *(near(p) for p in pieces)]

    w_one = four(p_one, y_one)

    keep = (1 - reset_mask).astype(F32).reshape(events, 1)
    valid = (jnp.arange(steps, dtype=I32)[:, None] < valid_counts[None, :]).astype(F32)
    valid = (valid / steps).reshape(events, 1)

    res_shape = shape((5, events, wide), F32)
    n_w = 2 + n_loc
    w_scratch = [pltpu.VMEM((n_loc, wide, cpad), BF16), pltpu.SemaphoreType.DMA((n_w,))]
    res_scratch = [pltpu.VMEM((5, events, wide), F32), pltpu.SemaphoreType.DMA((steps,))]
    state_shape = shape(((steps + 1) * batch, wide), BF16)
    q_scratch = pltpu.VMEM((n_loc, batch, cpad), F32)
    dq_scratch = pltpu.VMEM((n_loc, batch, cpad), BF16)
    x_scratch = pltpu.VMEM((n_loc, events, cpad), F32)
    all_scratch = pltpu.VMEM((n_loc, events, cpad), BF16)

    state_a, res_one = kernel_call(
        functools.partial(first_kernel, (steps, batch, hidden, bias_row, n_loc), n_w),
        [state_shape, res_shape],
        [l_arr, keep, slot_in, land, got_c, after(got_rows, reply_tg, negs, y_in[1])] + w_one,
        1,
        w_scratch
        + res_scratch
        + [q_scratch, pltpu.VMEM((n_loc, 16, chunk), F32), pltpu.VMEM((events, gpad), F32)],
        12, n_w, 1,
    )
    w_in = four(p_in, [after(y, state_a) for y in y_in])
    w_two = four(p_two, [after(y_two, state_a)])
    state_b, res_two = kernel_call(
        functools.partial(second_kernel, (steps, batch, hidden, chunk, n_loc), n_w, n_loc),
        [state_shape, res_shape],
        [l_arr, keep, land, got_c, state_a] + w_in + w_two,
        1,
        w_scratch + w_scratch + res_scratch + [q_scratch, x_scratch],
        0, n_w + n_loc, 1,
    )
    y_b = across(after(state_b, y_neg))

    y_neg = after(y_neg, state_b)
    negs = [negs, near(negs), y_neg, near(y_neg)]
    *g_neg, into_second, send_tg = kernel_call(
        functools.partial(score_kernel, (steps, batch, n_loc)),
        [shape((events, neg_part), BF16)] * n_loc
        + [shape((events, wide), F32), shape((slots, wide), BF16)],
        [valid, slot_tg, state_b, tg_rows] + negs,
        0,
        [
            pltpu.VMEM((n_loc, events, neg_part), F32),
            pltpu.VMEM((events, wide), BF16),
            pltpu.VMEM((events, wide), BF16),
            pltpu.VMEM((n_loc, neg_part, wide), BF16),
            pltpu.SemaphoreType.DMA((n_loc,)),
        ],
        3, n_loc,
    )
    init_two, into_first, *ch_two = kernel_call(
        functools.partial(back_second_kernel, (steps, batch, hidden, chunk, n_loc), n_w, n_loc),
        [shape((batch, wide), F32), shape((events, wide), F32)]
        + [shape((events, cpad), BF16)] * (2 * n_loc),
        [l_arr, keep, after(into_second, y_b), res_two] + w_in + w_two,
        1,
        [dq_scratch, all_scratch, all_scratch] + w_scratch + w_scratch + res_scratch,
        17, n_w + n_loc + 1,
    )
    def send_after(chunks, *deps):
        return send_xor([after(c, *deps) for c in chunks], "loc")

    ch_in, ch_two = send_xor(ch_two[:n_loc], "loc"), send_xor(ch_two[n_loc:], "loc")
    y_a = across(after(state_a, into_second))
    got_tg_g = to_owners(send_tg)
    init_one, da_one, *ch_one = kernel_call(
        functools.partial(back_first_kernel, (steps, batch, hidden, chunk, n_loc), n_w),
        [shape((batch, wide), F32), shape((events, gpad), BF16)]
        + [shape((events + 16, cpad), BF16)] * n_loc,
        [l_arr, keep, after(into_first, y_a), res_one] + w_one,
        1,
        [dq_scratch, all_scratch, pltpu.VMEM((n_loc, 16, cpad), F32)] + w_scratch + res_scratch,
        13, n_w + 1,
    )
    send_in, back_c = kernel_call(
        return_kernel,
        [shape((slots, gpad), BF16), shape((cslots, 2 * wide), BF16)],
        [slot_in, land, after(da_one, *ch_in[2:]), init_one, init_two],
        0, (), 3,
    )
    got_in_g = to_owners(after(send_in, got_tg_g))
    ch_one = send_xor(ch_one, "loc")
    g_neg = send_after(g_neg, *ch_one[2:])

    y_a, y_b = after(y_a, send_in), after(y_b, send_in)
    states_a = [state_a, near(state_a), y_a, near(y_a)]
    states_b = [state_b, near(state_b), y_b, near(y_b)]

    neg_grad = kernel_call(
        functools.partial(neg_kernel, n_loc, owners),
        [shape((neg_part, wide), BF16)],
        g_neg + states_b,
        0, (), 2,
    )[0]

    def all_sums(makers, waits):
        def one(make):
            kept, sent = make()
            rest = kept.shape[0]
            for bit in range(bits):
                got = yield sent, 1 << bit
                if bit < bits - 2:
                    rest //= 2
                    kept, sent = kernel_call(
                        functools.partial(split_kernel, bit + 1),
                        [shape((rest, cpad), BF16)] * 2,
                        [g_arr, kept, got],
                        1,
                    )
                else:
                    kept = kernel_call(add_kernel, [shape((rest, cpad), BF16)], [kept, got])[0]
                    sent = kept
            for bit in reversed(range(1, bits - 1)):
                kept = join(bit, kept, (yield kept, 1 << bit))
            got = yield kept, 1
            return kept, got

        chains = [one(make) for make in makers]
        results, asks, before, step = [None] * len(chains), {}, (), 0
        while None in results:
            if step < len(chains):
                asks[step] = next(chains[step])
            wait = tuple(before) + tuple(waits.get(step, lambda: ())())
            answers = {
                k: swap(after(ask[0], *wait) if wait else ask[0], "grp", ask[1])
                for k, ask in asks.items()
            }
            asks, before = {}, list(answers.values())
            for k, answer in answers.items():
                try:
                    asks[k] = chains[k].send(answer)
                except StopIteration as done:
                    results[k] = done.value
            step += 1
        return results

    half_shape = shape((wide // 2, cpad), BF16)

    def product(lefts, chunks, skip, bias_at):
        return kernel_call(
            functools.partial(dense_kernel, (steps, batch, hidden, skip, bias_at, n_loc)),
            [half_shape] * 2,
            [g_arr] + lefts + chunks,
            1, [pltpu.VMEM((wide, cpad), BF16)], 5,
        )

    def finish(parts, bias_row):
        return kernel_call(
            functools.partial(final_kernel, hidden, bias_row),
            [shape((hidden, chunk), F32), shape((1, chunk), F32)],
            [g_arr, *parts],
            1, (), 2,
        )

    own = rows // n_loc
    own_pad = -(-own // 16) * 16

    def table_start(ids, grads, *wait):
        across_cols = grads[0].shape[1]
        full = shape((own_pad, across_cols), F32)
        sent = shape((own_pad, across_cols), BF16)
        mine_p, far_p, near_p = kernel_call(
            functools.partial(table_kernel, own, len(ids)),
            [full, full, shape((2, own_pad, across_cols), BF16)],
            [l_arr] + [i.reshape(1, i.size) for i in ids] + grads,
            1, (), 4,
        )
        total, far_s = kernel_call(
            table_add_kernel, [full, sent], [after(mine_p, *wait), far_p, near(near_p)]
        )
        return total, across(far_s)

    def table_end(pair, cols, parts):
        return kernel_call(
            functools.partial(table_out_kernel, parts), [shape((own, cols), F32)], list(pair)
        )[0]

    sums = {}

    def made(name, *args):
        def make():
            sums[name] = product(*args)
            return sums[name]

        return make

    def start_back():
        sums["back"] = to_owners(after(back_c, got_in_g, sums["one"][0]))
        return ()

    def table_first():
        sums["table"] = table_start([in_ids], [got_in_g], sums["back"])
        return ()

    def table_moved():
        return (sums["table"][1],)

    def bring_back():
        return (sums["back"],)

    in_parts, two_parts, one_parts = all_sums(
        [
            made("in", states_a, ch_in, True, None),
            made("two", states_b, ch_two, False, None),
            made("one", states_a, ch_one, False, bias_row),
        ],
        {1: lambda: tuple(ch_one[2:]), 2: start_back, 3: lambda: (got_in_g,), 4: table_first, 5: bring_back, 6: table_moved},
    )
    got_back = sums["back"]
    got_neg_g = to_owners(after(neg_grad, got_back))
    grad_in, bias_in = finish(in_parts, hidden)
    grad_two, _ = finish(two_parts, hidden)
    grad_one, bias_one = finish(one_parts, bias_row)

    table_in = table_end(sums["table"], gates, 3)
    neg_ids = jnp.broadcast_to(mine[None, :], (owners, neg_own)).reshape(neg_part)
    table_out = table_end(table_start([tg_ids, neg_ids], [got_tg_g, got_neg_g]), wide, 1)
    grad_carried = kernel_call(
        carry_kernel, [shape((2, batch, hidden), F32)], [slot_pl, got_back]
    )[0]
    return (
        table_in,
        table_out[:, :hidden],
        table_out[:, hidden],
        grad_one,
        grad_in,
        grad_two,
        jnp.concatenate([bias_one, bias_in], axis=0),
        grad_carried,
    )


def solution(mesh):
    in_specs = (
        P(None, ("grp", "loc"), None),
        P(("grp", "loc")),
        P(None, ("grp", "loc")),
        P(None, ("grp", "loc")),
        P(None, ("grp", "loc")),
        P(("grp", "loc")),
        P(),
        P("grp", None),
        P("grp", None),
        P("grp"),
        P(None, "loc"),
        P(None, "loc"),
        P(None, "loc"),
        P(None, "loc"),
    )
    out_specs = (
        P(("grp", "loc"), None),
        P(("grp", "loc"), None),
        P(("grp", "loc")),
        P(None, "loc"),
        P(None, "loc"),
        P(None, "loc"),
        P(None, "loc"),
        P(None, ("grp", "loc"), None),
    )
    return jax.shard_map(
        on_device, mesh=mesh, in_specs=in_specs, out_specs=out_specs, check_vma=False
    )
```

```python
import functools

import jax
import jax.numpy as jnp
import numpy as np
from jax import lax
from jax.experimental import pallas as pl
from jax.experimental.pallas import tpu as pltpu
from jax.sharding import PartitionSpec as P

BPREG = 1.0
BF16 = jnp.bfloat16
F32 = jnp.float32
I32 = jnp.int32
LANES = 128
VMEM_LIMIT = 48 << 20


def swap(x, axis, bit):
    n = lax.axis_size(axis)
    return lax.ppermute(x, axis, [(i, i ^ bit) for i in range(n)])


def gather_xor(x, axis):
    blocks = {0: x}
    bit = lax.axis_size(axis) // 2
    while bit:
        for k in list(blocks):
            blocks[k | bit] = swap(blocks[k], axis, bit)
        bit //= 2
    return [blocks[k] for k in range(len(blocks))]


def send_xor(chunks, axis):
    return [chunks[0]] + [swap(chunks[j], axis, j) for j in range(1, len(chunks))]


def kernel_call(body, outs, ins, smem=0, scratch=(), us=1, left=0, left_outs=0):
    vmem, place = pl.BlockSpec(memory_space=pltpu.VMEM), pl.BlockSpec(memory_space=pl.ANY)
    nbytes = sum(a.size * a.dtype.itemsize for a in ins)
    nbytes += sum(int(functools.reduce(lambda a, b: a * b, o.shape)) * o.dtype.itemsize for o in outs)
    return pl.pallas_call(
        body,
        out_shape=outs,
        in_specs=[pl.BlockSpec(memory_space=pltpu.SMEM)] * smem
        + [vmem] * (len(ins) - smem - left)
        + [place] * left,
        out_specs=[vmem] * (len(outs) - left_outs) + [place] * left_outs,
        scratch_shapes=list(scratch),
        compiler_params=pltpu.CompilerParams(vmem_limit_bytes=VMEM_LIMIT),
        cost_estimate=pl.CostEstimate(flops=us * 10**9, bytes_accessed=nbytes, transcendentals=0),
    )(*ins)


def after(x, *deps):
    return lax.optimization_barrier((x,) + deps)[0]


def shape(dims, dtype):
    return jax.ShapeDtypeStruct(dims, dtype)


def iota(dims, dim):
    return lax.broadcasted_iota(I32, dims, dim)


def dot(a, b, ca=1, cb=0):
    return lax.dot_general(a, b, (((ca,), (cb,)), ((), ())), preferred_element_type=F32)


class Loader:
    def __init__(self, copies):
        self.copies = copies
        self.waited = set()
        for group in copies.values():
            for copy in group:
                copy.start()

    def ready(self, slot):
        if slot not in self.waited:
            self.waited.add(slot)
            for copy in self.copies[slot]:
                copy.wait()


class Weights(Loader):
    def __init__(self, refs, buf, sem, side=None):
        n = buf.shape[0]
        pieces = (len(refs) - n // 2) // (n // 2)
        copies, k = {}, 0
        for j in range(n):
            row, copies[j] = 0, []
            for _ in range(1 if j < n // 2 else pieces):
                size = refs[k].shape[0]
                at = row
                if side is not None and j >= n // 2:
                    at = pl.multiple_of((side if row == 0 else 1 - side) * size, size)
                part = buf.at[j, pl.ds(at, size), :]
                copies[j].append(pltpu.make_async_copy(refs[k], part, sem.at[k]))
                row, k = row + size, k + 1
        self.buf = buf
        super().__init__(copies)

    def __getitem__(self, j):
        self.ready(j)
        return self.buf[j]


def step_copies(ref, buf, sem, steps, batch, out):
    copies = {}
    for t in reversed(range(steps)):
        at = (slice(None), pl.ds(t * batch, batch), slice(None))
        pair = (buf.at[at], ref.at[at]) if out else (ref.at[at], buf.at[at])
        copies[t] = [pltpu.make_async_copy(*pair, sem.at[t])]
    return copies


def low(cond):
    return jnp.where(cond, 1.0, 0.0).astype(BF16)


def start_kernel(dims, in_ref, tg_ref, plan_ref, carried_ref, s_in, s_tg, s_pl, out_ref):
    owners, rows, cap, batch, ccap = dims
    hidden = carried_ref.shape[2]
    wide = out_ref.shape[1] // 2
    spare = wide - hidden

    def place(ids, span):
        n = ids.shape[0]
        owner_i = iota((n, owners), 1)
        member = (ids >= owner_i * span) & (ids < (owner_i + 1) * span)
        earlier = low(iota((n, n), 1) < iota((n, n), 0))
        before = dot(earlier, low(member))
        rank = jnp.sum(jnp.where(member, before, 0.0), axis=1, keepdims=True).astype(I32)
        owner = jnp.sum(jnp.where(member, owner_i, 0).astype(F32), axis=1, keepdims=True).astype(I32)
        return owner, rank

    def digits(owner, rank, first, value):
        n = owner.shape[0]
        turn = sum((rank >= k * ccap).astype(I32) for k in range(1, -(-cap // ccap)))
        row = owner * ccap + rank - turn * ccap
        hit = low(iota((n, owners * ccap), 1) == row)
        lane = iota((n, LANES), 1)
        high, rest = (value >> 8).astype(F32), (value & 255).astype(F32)
        at = first + 2 * turn
        code = jnp.where(lane == at, high, jnp.where(lane == at + 1, rest, 0.0))
        return dot(hit, code.astype(BF16), 0, 0)

    o_in, r_in = place(in_ref[...], rows)
    o_tg, r_tg = place(tg_ref[...], rows)
    o_pl, r_pl = place(plan_ref[...], batch)
    s_in[...] = o_in * cap + r_in
    s_tg[...] = o_tg * cap + r_tg
    s_pl[...] = o_pl * ccap + r_pl
    turns = -(-cap // ccap)
    code = digits(o_in, r_in, 0, in_ref[...] + 1)
    code += digits(o_tg, r_tg, 2 * turns, tg_ref[...] + 1)
    code += digits(o_pl, r_pl, 4 * turns, plan_ref[...] - o_pl * batch + 1)
    pick = low(iota((batch, owners * ccap), 1) == o_pl * ccap + r_pl)
    parts = [dot(pick, carried_ref[k].astype(BF16), 0, 0) for k in range(2)]
    parts = [parts[0], code[:, :spare], parts[1], jnp.zeros((owners * ccap, spare), F32)]
    out_ref[...] = jnp.concatenate(parts, axis=1).astype(BF16)


def decode(got_ref, row_ref, turn_ref, hidden, first):
    wide = got_ref.shape[1] // 2
    block = got_ref[:, wide - LANES : wide]
    n = row_ref.shape[0]
    found = dot(low(iota((n, block.shape[0]), 1) == row_ref[...]), block)
    at = hidden - wide + LANES + first + 2 * turn_ref[...]
    lane = iota((n, LANES), 1)
    worth = jnp.where(lane == at, 256.0, jnp.where(lane == at + 1, 1.0, 0.0))
    return jnp.sum(found * worth, axis=1, keepdims=True).astype(I32)


def landing(land_ref, got_ref, layer, batch, hidden):
    wide = got_ref.shape[1] // 2
    land = low(iota((land_ref.shape[0], batch), 1) == land_ref[...])
    moved = dot(land, got_ref[:, layer * wide : (layer + 1) * wide], 0, 0)
    return jnp.where(iota(moved.shape, 1) < hidden, moved, 0.0)


def cut(hidden, chunk, n_loc):
    gates = []
    for g in range(3):
        parts = []
        for i in range(n_loc):
            lo, hi = max(g * hidden, i * chunk), min((g + 1) * hidden, (i + 1) * chunk)
            if lo < hi:
                parts.append((i, lo - i * chunk, hi - i * chunk))
        gates.append(parts)
    return gates


def gate_of(g, chunks, hidden, chunk, wide):
    parts = [chunks[i][:, lo:hi] for i, lo, hi in cut(hidden, chunk, len(chunks))[g]]
    pad = jnp.zeros((parts[0].shape[0], wide - hidden), parts[0].dtype)
    return jnp.concatenate(parts + [pad], axis=1)


def chunk_of(i, gates, hidden, chunk, n_loc, cpad):
    parts = []
    for g, places in enumerate(cut(hidden, chunk, n_loc)):
        for k, lo, hi in places:
            if k == i:
                at = i * chunk + lo - g * hidden
                parts.append(gates[g][:, at : at + hi - lo])
    pad = jnp.zeros((parts[0].shape[0], cpad - chunk), parts[0].dtype)
    return jnp.concatenate(parts + [pad], axis=1)


def extend(value, keep, hidden):
    lane = iota(value.shape, 1)
    return jnp.where(lane == hidden, 1.0, jnp.where(lane == hidden + 1, keep, value)).astype(BF16)


def run_steps(steps, batch, hidden, l, keep_ref, weights, gates_of, start, state_ref, res, q_s):
    res_ref, res_s, res_sem = res
    n_loc = q_s.shape[0]
    wide = start.shape[1]
    lane = iota((batch, wide), 1)
    prev = start
    writes = step_copies(res_ref, res_s, res_sem, steps, batch, True)
    for t in range(steps):
        at = pl.ds(t * batch, batch)
        keep = keep_ref[at, :]
        state_ref[at, :] = extend(prev, keep, hidden)
        p = prev * keep
        p_low = p.astype(BF16)
        for j in range(n_loc):
            q_s[l ^ j] = dot(p_low, weights[j])
        in_z, in_r, in_n, qn = gates_of(t, [q_s[i] for i in range(n_loc)])
        z = jax.nn.sigmoid(in_z)
        r = jax.nn.sigmoid(in_r)
        n = jnp.tanh(in_n + r * qn)
        prev = jnp.where(lane < hidden, n + z * (p - n), 0.0)
        for k, val in enumerate((z, r, n, qn, p)):
            res_s[k, at, :] = val
        writes[t][0].start()
    state_ref[pl.ds(steps * batch, batch), :] = extend(prev, 0.0, hidden)
    for t in range(steps):
        writes[t][0].wait()


def pad_kernel(at, n_in, l_ref, w_ref, *refs):
    refs, outs = refs[: n_in - 2], refs[n_in - 2 :]
    out_ref = outs[0]
    rows, cols = w_ref.shape
    out_ref[...] = jnp.zeros(out_ref.shape, BF16)
    out_ref[:rows, :cols] = w_ref[...]
    if at is not None:
        which, row = at
        tile = row // 16 * 16
        here = (iota((16, cols), 0) == row - tile).astype(F32)
        old = out_ref[tile : tile + 16, :cols].astype(F32)
        extra = refs[0][which : which + 1, :].astype(F32)
        out_ref[tile : tile + 16, :cols] = (old + here * extra).astype(BF16)
    if len(outs) == 1:
        pass
    elif len(outs) == 2:
        half = outs[1].shape[0]
        side = l_ref[1] & 1
        outs[1][...] = out_ref[pl.ds(pl.multiple_of(side * half, half), half), :]
    else:
        first = outs[1].shape[0]
        outs[1][...] = out_ref[:first, :]
        outs[2][...] = out_ref[first:, :]


def gather_in_kernel(dims, base_ref, got_ref, row_ref, turn_ref, table_ref, out_ref, ids_ref, land_ref):
    hidden, turns = dims
    rows, cols = table_ref.shape
    wide = got_ref.shape[1] // 2
    ids = decode(got_ref, row_ref, turn_ref, hidden, 0) - 1 - base_ref[0]
    ids_ref[...] = ids
    at = hidden - wide + LANES + 4 * turns + 1
    land = got_ref[:, wide - LANES : wide].astype(F32)[:, at : at + 1]
    land_ref[...] = land.astype(I32) - 1
    pick = low(iota((ids.shape[0], rows), 1) == ids)
    found = dot(pick, table_ref[...])
    for g in range(3):
        part = found[:, g * hidden : (g + 1) * hidden]
        pad = jnp.zeros((part.shape[0], wide - hidden), F32)
        out_ref[:, g * wide : (g + 1) * wide] = jnp.concatenate([part, pad], axis=1).astype(BF16)


def biased_rows(ids, table_ref, bias_ref, wide):
    n = ids.shape[0]
    rows, cols = table_ref.shape
    pick = low(iota((n, rows), 1) == ids)
    parts = [dot(pick, table_ref[...]), dot(pick, bias_ref[...])[:, :1]]
    parts.append(jnp.zeros((n, wide - cols - 1), F32))
    return jnp.concatenate(parts, axis=1).astype(BF16)


def gather_tg_kernel(dims, base_ref, got_ref, row_ref, turn_ref, table_ref, bias_ref, out_ref, ids_ref):
    hidden, turns = dims
    ids = decode(got_ref, row_ref, turn_ref, hidden, 2 * turns) - 1 - base_ref[0]
    ids_ref[...] = ids
    out_ref[...] = biased_rows(ids, table_ref, bias_ref, out_ref.shape[1])


def gather_neg_kernel(ids_ref, table_ref, bias_ref, out_ref):
    out_ref[...] = biased_rows(ids_ref[...], table_ref, bias_ref, out_ref.shape[1])


def table_kernel(own, pairs, l_ref, *refs):
    mine_ref, far_ref, near_ref = refs[2 * pairs :]
    pad = mine_ref.shape[0]
    l = l_ref[0]
    for j, (ref, at) in enumerate(((mine_ref, None), (near_ref, 0), (far_ref, None), (near_ref, 1))):
        part = None
        for ids_ref, got_ref in zip(refs[:pairs], refs[pairs : 2 * pairs]):
            row = iota((pad, ids_ref.shape[1]), 0)
            hit = (row < own) & (row + (l ^ j) * own == ids_ref[...])
            term = dot(low(hit), got_ref[...])
            part = term if part is None else part + term
        if at is None:
            ref[...] = part
        else:
            ref[at, :, :] = part.astype(BF16)


def table_add_kernel(mine_ref, far_ref, got_ref, sum_ref, send_ref):
    sum_ref[...] = mine_ref[...] + got_ref[0].astype(F32)
    send_ref[...] = (far_ref[...] + got_ref[1].astype(F32)).astype(BF16)


def table_out_kernel(parts, sum_ref, got_ref, out_ref, *bias_ref):
    rows, cols = out_ref.shape
    total = (sum_ref[...] + got_ref[...].astype(F32))[:rows]
    wide = total.shape[1] // parts
    size = cols // parts
    split = [total[:, g * wide : g * wide + size] for g in range(parts)]
    out_ref[...] = jnp.concatenate(split, axis=1) if parts > 1 else split[0]
    for ref in bias_ref:
        ref[...] = total[:, cols : cols + 1]


def carry_kernel(slot_ref, got_ref, out_ref):
    hidden = out_ref.shape[2]
    wide = got_ref.shape[1] // 2
    pick = low(iota((slot_ref.shape[0], got_ref.shape[0]), 1) == slot_ref[...])
    back = dot(pick, got_ref[...])
    out_ref[0] = back[:, :hidden]
    out_ref[1] = back[:, wide : wide + hidden]


def split_kernel(bit, l_ref, a_ref, b_ref, keep_ref, send_ref):
    half = keep_ref.shape[0]
    side = (l_ref[0] >> bit) & 1
    for ref, at in ((keep_ref, side), (send_ref, 1 - side)):
        rows = pl.ds(pl.multiple_of(at * half, half), half)
        ref[...] = (a_ref[rows, :].astype(F32) + b_ref[rows, :].astype(F32)).astype(BF16)


def add_kernel(a_ref, b_ref, out_ref):
    out_ref[...] = (a_ref[...].astype(F32) + b_ref[...].astype(F32)).astype(BF16)


def join_kernel(bit, l_ref, a_ref, b_ref, out_ref):
    half = a_ref.shape[0]
    side = (l_ref[0] >> bit) & 1
    for ref, at in ((a_ref, side), (b_ref, 1 - side)):
        out_ref[pl.ds(pl.multiple_of(at * half, half), half), :] = ref[...]


def final_kernel(hidden, bias_row, l_ref, a_ref, b_ref, out_ref, bias_ref):
    side = l_ref[0] & 1
    cols = out_ref.shape[1]
    half = a_ref.shape[0]
    at = (bias_row - half) // 16 * 16
    for first, second, when in ((a_ref, b_ref, 0), (b_ref, a_ref, 1)):

        @pl.when(side == when)
        def _():
            out_ref[:half, :] = first[...].astype(F32)[:, :cols]
            out_ref[half:, :] = second[...].astype(F32)[: hidden - half, :cols]
            row = bias_row - half - at
            bias_ref[...] = second[at : at + 16, :].astype(F32)[row : row + 1, :cols]


def first_kernel(dims, n_w, l_ref, keep_ref, slot_ref, land_ref, got_ref, rows_ref, *refs):
    steps, batch, hidden, bias_row, n_loc = dims
    w_refs, refs = refs[:n_w], refs[n_w:]
    state_ref, res_ref, w_buf, w_sem, res_s, res_sem, q_s, b_s, x_s = refs
    wide = res_s.shape[2]
    l = l_ref[0]
    weights = Weights(w_refs, w_buf, w_sem)
    chunk = b_s.shape[2]
    pick = low(iota((steps * batch, rows_ref.shape[0]), 1) == slot_ref[...])
    rows = dot(pick, rows_ref[...])
    moved = landing(land_ref, got_ref, 0, batch, hidden)
    for j in range(n_loc):
        weights.ready(j)
        b_s[l ^ j] = w_buf[j, bias_row : bias_row + 16, :].astype(F32)[:, :chunk]
    bias = [b_s[i][0:1, :] for i in range(n_loc)]
    bias = [gate_of(g, bias, hidden, chunk, wide) for g in range(3)]
    x_s[...] = rows + jnp.concatenate(bias, axis=1)

    def gates_of(t, q):
        x = x_s[pl.ds(t * batch, batch), :]
        gates = [gate_of(g, q, hidden, chunk, wide) for g in range(3)]
        return x[:, :wide] + gates[0], x[:, wide : 2 * wide] + gates[1], x[:, 2 * wide :], gates[2]

    run_steps(
        steps, batch, hidden, l, keep_ref, weights, gates_of, moved, state_ref,
        (res_ref, res_s, res_sem), q_s,
    )


def second_kernel(dims, n_in, n_w, l_ref, keep_ref, land_ref, got_ref, below_ref, *refs):
    steps, batch, hidden, chunk, n_loc = dims
    in_refs, w_refs, refs = refs[:n_in], refs[n_in : n_in + n_w], refs[n_in + n_w :]
    state_ref, res_ref, in_buf, in_sem, w_buf, w_sem, res_s, res_sem, q_s, x_s = refs
    wide = res_s.shape[2]
    l = l_ref[0]
    inputs = Weights(in_refs, in_buf, in_sem, l_ref[1] & 1)
    weights = Weights(w_refs, w_buf, w_sem)
    moved = landing(land_ref, got_ref, 1, batch, hidden)
    below = below_ref[pl.ds(batch, steps * batch), :]
    for j in range(n_loc):
        x_s[l ^ j] = dot(below, inputs[j])

    def gates_of(t, q):
        x = [x_s[i, pl.ds(t * batch, batch), :] for i in range(n_loc)]
        both = [x[i] + q[i] for i in range(n_loc)]
        sizes = (hidden, chunk, wide)
        return (
            gate_of(0, both, *sizes), gate_of(1, both, *sizes), gate_of(2, x, *sizes), gate_of(2, q, *sizes)
        )

    run_steps(
        steps, batch, hidden, l, keep_ref, weights, gates_of, moved, state_ref,
        (res_ref, res_s, res_sem), q_s,
    )


def score_kernel(dims, valid_ref, slot_ref, state_ref, tg_ref, *refs):
    steps, batch, n_loc = dims
    rows = steps * batch
    neg_refs, refs = refs[:n_loc], refs[n_loc:]
    gn_refs, into_ref, send_ref = refs[:n_loc], refs[n_loc], refs[n_loc + 1]
    sn_s, tgt_s, tgg_s, neg_buf, neg_sem = refs[n_loc + 2 :]
    negs = Loader(
        {
            j: [pltpu.make_async_copy(neg_refs[j], neg_buf.at[j], neg_sem.at[j])]
            for j in range(n_loc)
        }
    )
    diag = iota((batch, batch), 0) == iota((batch, batch), 1)
    slots = tg_ref.shape[0]
    pick = low(iota((rows, slots), 1) == slot_ref[...])
    tgt_s[...] = dot(pick, tg_ref[...]).astype(BF16)
    every = state_ref[pl.ds(batch, rows), :]
    for j in range(n_loc):
        negs.ready(j)
        sn_s[j] = dot(every, neg_buf[j], 1, 1)
    for t in range(steps):
        at = pl.ds(t * batch, batch)
        second = state_ref[pl.ds((t + 1) * batch, batch), :]
        targets = tgt_s[at, :]
        st = dot(second, targets, 1, 1)
        sn = [sn_s[j, at, :] for j in range(n_loc)]
        pos = jnp.sum(jnp.where(diag, st, 0.0), axis=1, keepdims=True)
        top = jnp.max(jnp.where(diag, -jnp.inf, st), axis=1, keepdims=True)
        for s in sn:
            top = jnp.maximum(top, jnp.max(s, axis=1, keepdims=True))
        parts = [(st, jnp.where(diag, 0.0, jnp.exp(st - top)))]
        parts += [(s, jnp.exp(s - top)) for s in sn]
        mass = sum(jnp.sum(e, axis=1, keepdims=True) for _, e in parts)
        scale = 1.0 / mass
        parts = [(s, e * scale, jax.nn.sigmoid(pos - s)) for s, e in parts]
        inside = sum(jnp.sum(w * g, axis=1, keepdims=True) for _, w, g in parts)
        penalty = sum(jnp.sum(w * s * s, axis=1, keepdims=True) for s, w, _ in parts)
        slope = sum(jnp.sum(w * g * (1.0 - g), axis=1, keepdims=True) for _, w, g in parts)
        inv = 1.0 / inside
        weight = valid_ref[at, :]
        grads = [
            weight * w * (1.0 + BPREG * (s * s + 2.0 * s - penalty) - g * g * inv)
            for s, w, g in parts
        ]
        gt = grads[0] - jnp.where(diag, weight * slope * inv, 0.0)
        gt_low = gt.astype(BF16)
        into_ref[at, :] = dot(gt_low, targets)
        for j in range(n_loc):
            gn_refs[j][at, :] = grads[j + 1].astype(BF16)
        tgg_s[at, :] = dot(gt_low, second, 0, 0).astype(BF16)
    total = into_ref[...]
    for j in range(n_loc):
        total += dot(gn_refs[j][...], neg_buf[j])
    into_ref[...] = total
    send_ref[...] = dot(pick, tgg_s[...], 0, 0).astype(BF16)


def back_steps(steps, batch, hidden, l, keep_ref, weights, into_ref, res, dq_s, chunks_of):
    loader, res_s = res
    n_loc = dq_s.shape[0]
    wide = into_ref.shape[1]
    lane = iota((batch, wide), 1)
    carry = jnp.zeros((batch, wide), F32)
    for t in reversed(range(steps)):
        at = pl.ds(t * batch, batch)
        g = jnp.where(lane < hidden, into_ref[at, :] + carry, 0.0)
        loader.ready(t)
        z, r, n, qn, p = (res_s[k, at, :] for k in range(5))
        dc = g * (1.0 - z) * (1.0 - n * n)
        da_z = g * (p - n) * z * (1.0 - z)
        da_r = dc * qn * r * (1.0 - r)
        for i, value in enumerate(chunks_of(t, da_z, da_r, dc, dc * r)):
            dq_s[i] = value.astype(BF16)
        dp = g * z
        for j in range(n_loc):
            dp += dot(dq_s[l ^ j], weights[j], 1, 1)
        carry = dp * keep_ref[at, :]
    return jnp.where(lane < hidden, carry, 0.0)


def back_second_kernel(dims, n_in, n_w, l_ref, keep_ref, into_ref, *refs):
    steps, batch, hidden, chunk, n_loc = dims
    res_ref, refs = refs[0], refs[1:]
    in_refs, w_refs, refs = refs[:n_in], refs[n_in : n_in + n_w], refs[n_in + n_w :]
    init_ref, first_ref, refs = refs[0], refs[1], refs[2:]
    ch_refs, refs = refs[: 2 * n_loc], refs[2 * n_loc :]
    dq_s, da_all, dq_all, in_buf, in_sem, w_buf, w_sem, res_s, res_sem = refs
    l = l_ref[0]
    loader = Loader(step_copies(res_ref, res_s, res_sem, steps, batch, False))
    weights = Weights(w_refs, w_buf, w_sem)
    inputs = Weights(in_refs, in_buf, in_sem, l_ref[1] & 1)
    sizes = (hidden, chunk, n_loc, dq_s.shape[2])

    def chunks_of(t, da_z, da_r, da_n, dq_n):
        at = pl.ds(t * batch, batch)
        out = []
        for i in range(n_loc):
            dq = chunk_of(i, (da_z, da_r, dq_n), *sizes)
            same = (i + 1) * chunk <= 2 * hidden
            da = dq if same else chunk_of(i, (da_z, da_r, da_n), *sizes)
            da_all[i, at, :] = da.astype(BF16)
            dq_all[i, at, :] = dq.astype(BF16)
            out.append(dq)
        return out

    init_ref[...] = back_steps(
        steps, batch, hidden, l, keep_ref, weights, into_ref, (loader, res_s), dq_s, chunks_of
    )
    rows = steps * batch
    total = None
    for j in range(n_loc):
        da_low = da_all[l ^ j]
        ch_refs[j][...] = da_low
        ch_refs[n_loc + j][...] = dq_all[l ^ j]
        part = dot(da_low, inputs[j], 1, 1)
        total = part if total is None else total + part
    first_ref[...] = total


def back_first_kernel(dims, n_w, l_ref, keep_ref, into_ref, *refs):
    steps, batch, hidden, chunk, n_loc = dims
    res_ref, refs = refs[0], refs[1:]
    w_refs, refs = refs[:n_w], refs[n_w:]
    init_ref, da_all, refs = refs[0], refs[1], refs[2:]
    ch_refs, refs = refs[:n_loc], refs[n_loc:]
    dq_s, dq_all, bias_s, w_buf, w_sem, res_s, res_sem = refs
    l = l_ref[0]
    loader = Loader(step_copies(res_ref, res_s, res_sem, steps, batch, False))
    weights = Weights(w_refs, w_buf, w_sem)
    wide = into_ref.shape[1]
    sizes = (hidden, chunk, n_loc, dq_s.shape[2])
    bias_s[...] = jnp.zeros(bias_s.shape, F32)

    def chunks_of(t, da_z, da_r, da_n, dq_n):
        at = pl.ds(t * batch, batch)
        for g, da in enumerate((da_z, da_r, da_n)):
            da_all[at, g * wide : (g + 1) * wide] = da.astype(BF16)
        out = [chunk_of(i, (da_z, da_r, dq_n), *sizes) for i in range(n_loc)]
        for i, dq in enumerate(out):
            dq_all[i, at, :] = dq.astype(BF16)
        return out

    init_ref[...] = back_steps(
        steps, batch, hidden, l, keep_ref, weights, into_ref, (loader, res_s), dq_s, chunks_of
    )
    rows = steps * batch
    bias = jnp.sum(da_all[...].astype(F32), axis=0, keepdims=True)
    bias = [bias[:, g * wide : (g + 1) * wide] for g in range(3)]
    for i in range(n_loc):
        bias_s[i, 0:1, :] = chunk_of(i, bias, *sizes)
    for j in range(n_loc):
        ch_refs[j][pl.ds(0, rows), :] = dq_all[l ^ j]
        ch_refs[j][pl.ds(rows, 16), :] = bias_s[l ^ j].astype(BF16)


def return_kernel(slot_ref, land_ref, da_ref, init_ref, init2_ref, send_ref, back_ref):
    rows, cols = da_ref.shape
    wide = init_ref.shape[1]
    pick = low(iota((rows, send_ref.shape[0]), 1) == slot_ref[...])
    send_ref[...] = dot(pick, da_ref[...], 0, 0).astype(BF16)
    land = low(iota((land_ref.shape[0], init_ref.shape[0]), 1) == land_ref[...])
    back_ref[:, :wide] = dot(land, init_ref[...].astype(BF16)).astype(BF16)
    back_ref[:, wide:] = dot(land, init2_ref[...].astype(BF16)).astype(BF16)


def scaled(ref, rows, hidden):
    left = ref[pl.ds(0, rows), :].astype(F32)
    return (left * left[:, hidden + 1 : hidden + 2]).astype(BF16)


def dense_kernel(dims, l_ref, *refs):
    steps, batch, hidden, skip, bias_row, n_loc = dims
    rows = steps * batch
    left_refs, ch_refs = refs[:n_loc], refs[n_loc : 2 * n_loc]
    keep_ref, send_ref, all_s = refs[2 * n_loc :]
    half = keep_ref.shape[0]
    side = l_ref[0] & 1
    total, bias = None, None
    for j in range(n_loc):
        left = left_refs[j][pl.ds(batch, rows), :] if skip else scaled(left_refs[j], rows, hidden)
        part = dot(left, ch_refs[j][pl.ds(0, rows), :], 0, 0)
        total = part if total is None else total + part
        if bias_row is not None:
            extra = ch_refs[j][pl.ds(rows, 16), :].astype(F32)
            bias = extra if bias is None else bias + extra
    all_s[...] = total.astype(BF16)
    if bias_row is not None:
        all_s[pl.ds(bias_row, 16), :] = bias.astype(BF16)
    keep_ref[...] = all_s[pl.ds(pl.multiple_of(side * half, half), half), :]
    send_ref[...] = all_s[pl.ds(pl.multiple_of((1 - side) * half, half), half), :]


def neg_kernel(n_loc, owners, *refs):
    gn_refs, b_refs, out_ref = refs[:n_loc], refs[n_loc : 2 * n_loc], refs[2 * n_loc]
    rows = gn_refs[0].shape[0]
    batch = b_refs[0].shape[0] - rows
    total = None
    for j in range(n_loc):
        part = dot(gn_refs[j][...], b_refs[j][pl.ds(batch, rows), :], 0, 0)
        total = part if total is None else total + part
    own = out_ref.shape[0] // owners
    places = [(g >> 1) + (g & 1) * (owners // 2) for g in range(owners)]
    blocks = [total[p * own : (p + 1) * own, :] for p in places]
    out_ref[...] = jnp.concatenate(blocks, axis=0).astype(BF16)


def on_device(
    carried,
    session_plan,
    item_ids,
    target_ids,
    reset_mask,
    valid_counts,
    negative_ids,
    input_table,
    output_table,
    output_bias,
    hidden_one,
    input_two,
    hidden_two,
    gate_biases,
):
    hidden = carried.shape[2]
    wide = -(-(hidden + 2) // LANES) * LANES
    bias_row = wide - 16
    steps, batch = item_ids.shape
    events = steps * batch
    owners = lax.axis_size("grp")
    n_loc = lax.axis_size("loc")
    grp = lax.axis_index("grp")
    loc = lax.axis_index("loc")
    rows = input_table.shape[0]
    base = grp * rows
    gates = input_table.shape[1]
    chunk = gates // n_loc
    cap = events // owners + events // (2 * owners)
    ccap = 4 * batch // owners
    slots, cslots = owners * cap, owners * ccap
    neg_own = negative_ids.shape[0] // owners // n_loc
    neg_part = owners * neg_own
    l_arr = jnp.stack([loc, grp]).astype(I32)

    cpad = -(-chunk // LANES) * LANES
    gpad = 3 * wide
    w_shape = shape((wide, cpad), BF16)

    g_arr = grp.astype(I32).reshape(1)
    bits = owners.bit_length() - 1

    def padded(w, at, first):
        ins = [l_arr, w] if at is None else [l_arr, w, gate_biases]
        outs = [w_shape]
        if first:
            outs.append(shape((first, cpad), BF16))
            if 2 * first < wide:
                outs.append(shape((wide - first, cpad), BF16))
        return kernel_call(functools.partial(pad_kernel, at, len(ins)), outs, ins, 1)

    def near(x):
        return swap(x, "loc", 1)

    def across(x):
        return swap(x, "loc", 2)

    def join(bit, kept, got, index=g_arr):
        return kernel_call(
            functools.partial(join_kernel, bit),
            [shape((2 * kept.shape[0],) + kept.shape[1:], BF16)],
            [index, kept, got], 1,
        )[0]

    p_one, *one_pieces = padded(hidden_one, (0, bias_row), wide // 8)
    y_one = [across(one_pieces[0])]
    y_one.append(across(after(one_pieces[1], y_one[0])))

    slot_in, slot_tg, slot_pl, packed = kernel_call(
        functools.partial(start_kernel, (owners, rows, cap, batch, ccap)),
        [
            shape((events, 1), I32),
            shape((events, 1), I32),
            shape((batch, 1), I32),
            shape((cslots, 2 * wide), BF16),
        ],
        [
            after(item_ids, p_one).reshape(events, 1),
            target_ids.reshape(events, 1),
            session_plan.reshape(batch, 1),
            carried,
        ],
        0, (), 3,
    )

    def to_owners(x):
        got = lax.all_to_all(
            x.reshape((owners, x.shape[0] // owners) + x.shape[1:]),
            "grp", split_axis=0, concat_axis=0, tiled=True,
        )
        return got.reshape(x.shape)

    got_c = to_owners(after(packed, y_one[0]))

    bias_col = output_bias[:, None]
    mine = lax.dynamic_slice(
        negative_ids.reshape(owners, n_loc, neg_own), (grp, loc, 0), (1, 1, neg_own)
    ).reshape(neg_own) - base
    negs_own = kernel_call(
        gather_neg_kernel,
        [shape((neg_own, wide), BF16)],
        [after(mine, p_one).reshape(neg_own, 1), output_table, bias_col],
    )[0]
    negs_half = negs_own
    for bit in range(1, bits):
        negs_half = join(bit, negs_half, swap(negs_half, "grp", 1 << bit))
    negs = join(0, negs_half, swap(negs_half, "grp", 1))

    place = np.arange(slots)
    turns = -(-cap // ccap)
    place_row = jnp.asarray((place // cap * ccap + place % cap % ccap)[:, None], I32)
    place_turn = jnp.asarray((place % cap // ccap)[:, None], I32)
    base_arr = base.astype(I32).reshape(1)
    ids_shape = shape((slots, 1), I32)
    reply_in, in_ids, land = kernel_call(
        functools.partial(gather_in_kernel, (hidden, turns)),
        [shape((slots, gpad), BF16), ids_shape, shape((cslots, 1), I32)],
        [base_arr, got_c, place_row, place_turn, input_table],
        1, (), 4,
    )
    p_in, h_in = padded(input_two, (1, hidden), wide // 2)
    p_two = padded(hidden_two, None, 0)[0]
    y_in = across(after(h_in, y_one[1]))
    got_rows = to_owners(after(reply_in, negs_half, y_one[1]))
    y_two = across(after(p_two, y_in))
    y_in = [y_in, swap(y_in, "grp", 1)]
    y_neg = across(after(negs, y_two))
    reply_tg, tg_ids = kernel_call(
        functools.partial(gather_tg_kernel, (hidden, turns)),
        [shape((slots, wide), BF16), ids_shape],
        [base_arr, got_c, place_row, place_turn, output_table, bias_col],
        1, (), 3,
    )
    tg_rows = to_owners(after(reply_tg, got_rows))

    def four(own, pieces):
        return [own, near(own), *pieces, *(near(p) for p in pieces)]

    w_one = four(p_one, y_one)

    keep = (1 - reset_mask).astype(F32).reshape(events, 1)
    valid = (jnp.arange(steps, dtype=I32)[:, None] < valid_counts[None, :]).astype(F32)
    valid = (valid / steps).reshape(events, 1)

    res_shape = shape((5, events, wide), F32)
    n_w = 2 + n_loc
    w_scratch = [pltpu.VMEM((n_loc, wide, cpad), BF16), pltpu.SemaphoreType.DMA((n_w,))]
    res_scratch = [pltpu.VMEM((5, events, wide), F32), pltpu.SemaphoreType.DMA((steps,))]
    state_shape = shape(((steps + 1) * batch, wide), BF16)
    q_scratch = pltpu.VMEM((n_loc, batch, cpad), F32)
    dq_scratch = pltpu.VMEM((n_loc, batch, cpad), BF16)
    x_scratch = pltpu.VMEM((n_loc, events, cpad), F32)
    all_scratch = pltpu.VMEM((n_loc, events, cpad), BF16)

    state_a, res_one = kernel_call(
        functools.partial(first_kernel, (steps, batch, hidden, bias_row, n_loc), n_w),
        [state_shape, res_shape],
        [l_arr, keep, slot_in, land, got_c, after(got_rows, reply_tg, negs, y_in[1])] + w_one,
        1,
        w_scratch
        + res_scratch
        + [q_scratch, pltpu.VMEM((n_loc, 16, chunk), F32), pltpu.VMEM((events, gpad), F32)],
        12, n_w, 1,
    )
    w_in = four(p_in, [after(y, state_a) for y in y_in])
    w_two = four(p_two, [after(y_two, state_a)])
    state_b, res_two = kernel_call(
        functools.partial(second_kernel, (steps, batch, hidden, chunk, n_loc), n_w, n_loc),
        [state_shape, res_shape],
        [l_arr, keep, land, got_c, state_a] + w_in + w_two,
        1,
        w_scratch + w_scratch + res_scratch + [q_scratch, x_scratch],
        0, n_w + n_loc, 1,
    )
    y_b = across(after(state_b, y_neg))

    y_neg = after(y_neg, state_b)
    negs = [negs, near(negs), y_neg, near(y_neg)]
    *g_neg, into_second, send_tg = kernel_call(
        functools.partial(score_kernel, (steps, batch, n_loc)),
        [shape((events, neg_part), BF16)] * n_loc
        + [shape((events, wide), F32), shape((slots, wide), BF16)],
        [valid, slot_tg, state_b, tg_rows] + negs,
        0,
        [
            pltpu.VMEM((n_loc, events, neg_part), F32),
            pltpu.VMEM((events, wide), BF16),
            pltpu.VMEM((events, wide), BF16),
            pltpu.VMEM((n_loc, neg_part, wide), BF16),
            pltpu.SemaphoreType.DMA((n_loc,)),
        ],
        3, n_loc,
    )
    init_two, into_first, *ch_two = kernel_call(
        functools.partial(back_second_kernel, (steps, batch, hidden, chunk, n_loc), n_w, n_loc),
        [shape((batch, wide), F32), shape((events, wide), F32)]
        + [shape((events, cpad), BF16)] * (2 * n_loc),
        [l_arr, keep, after(into_second, y_b), res_two] + w_in + w_two,
        1,
        [dq_scratch, all_scratch, all_scratch] + w_scratch + w_scratch + res_scratch,
        17, n_w + n_loc + 1,
    )
    def send_after(chunks, *deps):
        return send_xor([after(c, *deps) for c in chunks], "loc")

    ch_in, ch_two = send_xor(ch_two[:n_loc], "loc"), send_xor(ch_two[n_loc:], "loc")
    y_a = across(after(state_a, into_second))
    got_tg_g = to_owners(send_tg)
    init_one, da_one, *ch_one = kernel_call(
        functools.partial(back_first_kernel, (steps, batch, hidden, chunk, n_loc), n_w),
        [shape((batch, wide), F32), shape((events, gpad), BF16)]
        + [shape((events + 16, cpad), BF16)] * n_loc,
        [l_arr, keep, after(into_first, y_a), res_one] + w_one,
        1,
        [dq_scratch, all_scratch, pltpu.VMEM((n_loc, 16, cpad), F32)] + w_scratch + res_scratch,
        13, n_w + 1,
    )
    send_in, back_c = kernel_call(
        return_kernel,
        [shape((slots, gpad), BF16), shape((cslots, 2 * wide), BF16)],
        [slot_in, land, after(da_one, *ch_in[2:]), init_one, init_two],
        0, (), 3,
    )
    got_in_g = to_owners(after(send_in, got_tg_g))
    ch_one = send_xor(ch_one, "loc")
    g_neg = send_after(g_neg, *ch_one[2:])

    y_a, y_b = after(y_a, send_in), after(y_b, send_in)
    states_a = [state_a, near(state_a), y_a, near(y_a)]
    states_b = [state_b, near(state_b), y_b, near(y_b)]

    neg_grad = kernel_call(
        functools.partial(neg_kernel, n_loc, owners),
        [shape((neg_part, wide), BF16)],
        g_neg + states_b,
        0, (), 2,
    )[0]

    def all_sums(makers, waits):
        def one(make):
            kept, sent = make()
            rest = kept.shape[0]
            for bit in range(bits):
                got = yield sent, 1 << bit
                if bit < bits - 2:
                    rest //= 2
                    kept, sent = kernel_call(
                        functools.partial(split_kernel, bit + 1),
                        [shape((rest, cpad), BF16)] * 2,
                        [g_arr, kept, got],
                        1,
                    )
                else:
                    kept = kernel_call(add_kernel, [shape((rest, cpad), BF16)], [kept, got])[0]
                    sent = kept
            for bit in reversed(range(1, bits - 1)):
                kept = join(bit, kept, (yield kept, 1 << bit))
            got = yield kept, 1
            return kept, got

        chains = [one(make) for make in makers]
        results, asks, before, step = [None] * len(chains), {}, (), 0
        while None in results:
            if step < len(chains):
                asks[step] = next(chains[step])
            wait = tuple(before) + tuple(waits.get(step, lambda: ())())
            answers = {
                k: swap(after(ask[0], *wait) if wait else ask[0], "grp", ask[1])
                for k, ask in asks.items()
            }
            asks, before = {}, list(answers.values())
            for k, answer in answers.items():
                try:
                    asks[k] = chains[k].send(answer)
                except StopIteration as done:
                    results[k] = done.value
            step += 1
        return results

    half_shape = shape((wide // 2, cpad), BF16)

    def product(lefts, chunks, skip, bias_at):
        return kernel_call(
            functools.partial(dense_kernel, (steps, batch, hidden, skip, bias_at, n_loc)),
            [half_shape] * 2,
            [g_arr] + lefts + chunks,
            1, [pltpu.VMEM((wide, cpad), BF16)], 5,
        )

    def finish(parts, bias_row):
        return kernel_call(
            functools.partial(final_kernel, hidden, bias_row),
            [shape((hidden, chunk), F32), shape((1, chunk), F32)],
            [g_arr, *parts],
            1, (), 2,
        )

    own = rows // n_loc
    own_pad = -(-own // 16) * 16

    def table_start(ids, grads, *wait):
        across_cols = grads[0].shape[1]
        full = shape((own_pad, across_cols), F32)
        sent = shape((own_pad, across_cols), BF16)
        mine_p, far_p, near_p = kernel_call(
            functools.partial(table_kernel, own, len(ids)),
            [full, full, shape((2, own_pad, across_cols), BF16)],
            [l_arr] + [i.reshape(1, i.size) for i in ids] + grads,
            1, (), 4,
        )
        total, far_s = kernel_call(
            table_add_kernel, [full, sent], [after(mine_p, *wait), far_p, near(near_p)]
        )
        return total, across(far_s)

    def table_end(pair, cols, parts):
        outs = [shape((own, cols), F32)] + [shape((own, 1), F32)] * (parts == 1)
        return kernel_call(functools.partial(table_out_kernel, parts), outs, list(pair))

    sums = {}

    def made(name, *args):
        def make():
            sums[name] = product(*args)
            return sums[name]

        return make

    def start_back():
        sums["back"] = to_owners(after(back_c, got_in_g, sums["one"][0]))
        return ()

    def table_first():
        sums["table"] = table_start([in_ids], [got_in_g], sums["back"])
        return ()

    def table_moved():
        return (sums["table"][1],)

    def bring_back():
        return (sums["back"],)

    in_parts, two_parts, one_parts = all_sums(
        [
            made("in", states_a, ch_in, True, None),
            made("two", states_b, ch_two, False, None),
            made("one", states_a, ch_one, False, bias_row),
        ],
        {1: lambda: tuple(ch_one[2:]), 2: start_back, 3: lambda: (got_in_g,), 4: table_first, 5: bring_back, 6: table_moved},
    )
    got_back = sums["back"]
    got_neg_g = to_owners(after(neg_grad, got_back))
    grad_in, bias_in = finish(in_parts, hidden)
    grad_two, _ = finish(two_parts, hidden)
    grad_one, bias_one = finish(one_parts, bias_row)

    (table_in,) = table_end(sums["table"], gates, 3)
    neg_ids = jnp.broadcast_to(mine[None, :], (owners, neg_own)).reshape(neg_part)
    table_out, table_bias = table_end(table_start([tg_ids, neg_ids], [got_tg_g, got_neg_g]), hidden, 1)
    grad_carried = kernel_call(
        carry_kernel, [shape((2, batch, hidden), F32)], [slot_pl, got_back]
    )[0]
    return (
        table_in,
        table_out,
        table_bias[:, 0],
        grad_one,
        grad_in,
        grad_two,
        jnp.concatenate([bias_one, bias_in], axis=0),
        grad_carried,
    )


def solution(mesh):
    in_specs = (
        P(None, ("grp", "loc"), None),
        P(("grp", "loc")),
        P(None, ("grp", "loc")),
        P(None, ("grp", "loc")),
        P(None, ("grp", "loc")),
        P(("grp", "loc")),
        P(),
        P("grp", None),
        P("grp", None),
        P("grp"),
        P(None, "loc"),
        P(None, "loc"),
        P(None, "loc"),
        P(None, "loc"),
    )
    out_specs = (
        P(("grp", "loc"), None),
        P(("grp", "loc"), None),
        P(("grp", "loc")),
        P(None, "loc"),
        P(None, "loc"),
        P(None, "loc"),
        P(None, "loc"),
        P(None, ("grp", "loc"), None),
    )
    return jax.shard_map(
        on_device, mesh=mesh, in_specs=in_specs, out_specs=out_specs, check_vma=False
    )
```
